32 devices in a mesh: dp: 2 (over y), fsdp: 16 (over z, x, core).
Axes of the slice: x: 2, y: 2, z: 4, core: 2. Of those that a mesh axis runs over, the one named last changes fastest.
Arguments:
- tokens: bfloat16 [16384, 1024], P(('dp', 'fsdp')), may hold values from -6 to 6
- memory: bfloat16 [16384, 1024], P(('dp', 'fsdp')), may hold values from -6 to 6
- cotangent: bfloat16 [16384, 1024], P(('dp', 'fsdp')), may hold values from -6 to 6
- sent_len: int32 [32, 4], P(('dp', 'fsdp')), may hold values from 1 to 256, 512 in all within a row
- mem_len: int32 [32, 4], P(('dp', 'fsdp')), may hold values from 1 to 256, 512 in all within a row
- proj_in: bfloat16 [6, 1024, 1024], P(None, ('dp', 'fsdp')), may hold values from -0.1875 to 0.1875
- proj_out: bfloat16 [2, 1024, 1024], P(None, ('dp', 'fsdp')), may hold values from -2 to 2
- ffn_in: bfloat16 [1024, 4096], P(('dp', 'fsdp')), may hold values from -0.1875 to 0.1875
- ffn_out: bfloat16 [4096, 1024], P(('dp', 'fsdp')), may hold values from -0.375 to 0.375
- ln_gain: bfloat16 [3, 1024], P(None, ('dp', 'fsdp')), may hold values from 0.25 to 1.75
- ln_bias: bfloat16 [3, 1024], P(None, ('dp', 'fsdp')), may hold values from -2 to 2
Outputs:
- output: bfloat16 [16384, 1024], P(('dp', 'fsdp'))
- grad_tokens: bfloat16 [16384, 1024], P(('dp', 'fsdp'))
- grad_memory: bfloat16 [16384, 1024], P(('dp', 'fsdp'))
- grad_proj_in: float32 [6, 1024, 1024], P(None, ('dp', 'fsdp'))
- grad_proj_out: float32 [2, 1024, 1024], P(None, ('dp', 'fsdp'))
- grad_ffn_in: float32 [1024, 4096], P(('dp', 'fsdp'))
- grad_ffn_out: float32 [4096, 1024], P(('dp', 'fsdp'))
- grad_gain: float32 [3, 1024], P(None, ('dp', 'fsdp'))
- grad_bias: float32 [3, 1024], P(None, ('dp', 'fsdp'))
The draws below stay inside these ranges and needn't reach their ends.
Inputs may be any that keep to these rules, and one draw needn't show every extreme that they name: `sent_len`: each device's 4 sentence lengths sum to 512; on every device the longest is exactly 256. `mem_len`: each device's 4 memory lengths sum to 512; on every device the longest is exactly 256.
All inputs are finite; a program needn't handle non-finite values.
Results may differ from the reference program's by a relative error of at most 0.02.
The reference program's roundings to bfloat16 on the way count: a program that leaves them out, or rounds other values in their place, can miss the bound.
Values may be sent and summed in bfloat16 or wider, within the bound.
A program may use at most 256 MiB of HBM per device.

```python
import math
from functools import partial
import jax
import jax.numpy as jnp
import numpy as np
from jax import lax

D = 1024
FF = 4096
HEADS = 16
HEAD_DIM = 64
TOK_DEV = 512
SENT_DEV = 4
MOST_LEN = 256
TOKENS = 16384
DEVICES = 32


def strengthened(values, rng, source, target, blocks, factor):
    owner, partner = [(jnp.arange(values.shape[axis_at]) // (values.shape[axis_at] // blocks)).reshape([-1 if axis == axis_at else 1 for axis in range(values.ndim)]) for axis_at in (source, target)]
    chosen = jax.random.permutation(rng, blocks)[partner]
    strong = (owner == chosen) | (owner == (partner + blocks // 2) % blocks)
    return jnp.where(strong, factor * values, values)


def steps_of(rng, extent, cuts, smallest, high):
    def one(position, parts):
        heights = jax.random.uniform(jax.random.fold_in(jax.random.fold_in(rng, 6), position), (parts,), jnp.float32, smallest / len(cuts), high / len(cuts))
        return jnp.repeat(jnp.exp(heights), extent[position] // parts).reshape((-1,) + (1,) * (len(extent) - position - 1))

    loudness = one(*cuts[0])
    for cut in cuts[1:]:
        loudness = loudness * one(*cut)
    return loudness


def split_up(count, total, limit, lean):
    loads = [(1 << 20) // math.isqrt(standing ** lean) + 1 for standing in range(2, count + 1)]
    rest, holding = total - limit - (count - 1), [1] * (count - 1)
    while rest > 0:
        candidates = [i for i in range(count - 1) if holding[i] < limit]
        pool, left = sum([loads[i] for i in candidates]), rest
        for i in candidates:
            addition = min(limit - holding[i], max(1, left * loads[i] // pool), rest)
            holding[i] = holding[i] + addition
            rest = rest - addition
    return np.array([limit] + holding)


def ragged(own_key, amount, total, reach, lean):
    if amount == 2:
        one = jax.random.randint(own_key, (), max(1, total - reach), min(reach, total - 1) + 1)
        return jnp.stack([one, total - one])
    sizes = jnp.asarray(split_up(amount, total, reach, lean), jnp.int32)
    pairs = (amount - 1) // 2
    source_of, taker = sizes[1:1 + 2 * pairs:2], sizes[2:2 + 2 * pairs:2]
    room = jnp.minimum(source_of - 1, reach - taker)
    moved = jax.random.randint(jax.random.fold_in(own_key, 1), (pairs,), 0, 1 << 20) % (room + 1)
    sizes = sizes.at[1:1 + 2 * pairs:2].set(source_of - moved).at[2:2 + 2 * pairs:2].set(taker + moved)
    return sizes[jax.random.permutation(jax.random.fold_in(own_key, 2), amount)]


def noise(rng, dims, deviation, reach, shards=(), held_as=jnp.bfloat16):
    factor_of = steps_of(rng, dims, shards, -0.22, 0.18) if shards else 1.0
    values = jax.random.normal(rng, dims, jnp.float32) * deviation * factor_of
    return jnp.minimum(jnp.maximum(values, -reach), reach).astype(held_as)


def heavy_noise(own_key, extent, deviation, limit, pieces, heavy, kind=jnp.bfloat16):
    values = deviation * jax.random.normal(own_key, extent, jnp.float32)
    if pieces:
        values = values * steps_of(own_key, extent, pieces, -0.22, 0.18)
    return jnp.clip(strengthened(values, jax.random.fold_in(own_key, 3), *heavy), -limit, limit).astype(kind)


def setup_inputs(seed: int = 0) -> dict:
    seeds = jax.random.split(jax.random.key(seed), 12)
    tokens = heavy_noise(seeds[0], (TOKENS, D), 1.0, 6.0, ((0, 32),), (0, 1, 32, 2.75))
    memory = heavy_noise(seeds[1], (TOKENS, D), 1.0, 6.0, ((0, 32),), (0, 1, 32, 2.75))
    cotangent = noise(seeds[2], (TOKENS, D), 1.0, 6.0, ((0, 32),))
    sent_len = jax.vmap(lambda own: ragged(own, SENT_DEV, TOK_DEV, MOST_LEN, 2))(jax.random.split(seeds[3], DEVICES)).reshape((DEVICES, SENT_DEV)).astype(jnp.int32)
    mem_len = jax.vmap(lambda own: ragged(own, SENT_DEV, TOK_DEV, MOST_LEN, 2))(jax.random.split(seeds[4], DEVICES)).reshape((DEVICES, SENT_DEV)).astype(jnp.int32)
    proj_in = noise(seeds[5], (6, D, D), D ** -0.5, 0.1875, ((1, 32),))
    proj_out = noise(seeds[6], (2, D, D), (D // 128) ** -0.5, 2.0, ((1, 32),))
    ffn_in = noise(seeds[7], (D, FF), D ** -0.5, 0.1875, ((0, 32),))
    ffn_out = noise(seeds[8], (FF, D), (FF // 16) ** -0.5, 0.375, ((0, 32),))
    ln_gain = jnp.clip(1.0 + 0.15 * jax.random.normal(seeds[9], (3, D), jnp.float32), 0.25, 1.75).astype(jnp.bfloat16)
    ln_bias = noise(seeds[10], (3, D), 0.3, 2.0, ((1, 32),))
    return dict(tokens=tokens, memory=memory, cotangent=cotangent, sent_len=sent_len, mem_len=mem_len, proj_in=proj_in, proj_out=proj_out, ffn_in=ffn_in, ffn_out=ffn_out, ln_gain=ln_gain, ln_bias=ln_bias)


@jax.custom_vjp
def low(v):
    return lax.optimization_barrier(v.astype(jnp.bfloat16)).astype(jnp.float32)

@jax.custom_vjp
def low_back(v):
    return v

def low_keep(v):
    return (low(v), None)

def low_pass(kept, grad):
    return (grad,)

def back_keep(v):
    return (v, None)

def back_low(kept, grad):
    return (low(grad),)
low.defvjp(low_keep, low_pass)
low_back.defvjp(back_keep, back_low)
residual_scale = 300.0 ** 0.25
masked_score = -1000000000.0
highest = lax.Precision.HIGHEST

def both_ways(value):
    return low_back(low(value))

def matmul(left, right):
    return jnp.dot(left, right, precision=highest)

def layer_norm(summed, scale_row, shift_row):
    middle = lax.optimization_barrier(jnp.mean(summed, axis=-1, keepdims=True))
    centered = summed - middle
    spread = lax.optimization_barrier(jnp.mean(centered * centered, axis=-1, keepdims=True))
    return centered * lax.rsqrt(spread + 1e-05) * scale_row + shift_row

def segment_ids(lengths, seg_count):
    sent_ends = jnp.cumsum(lengths)
    positions = jnp.arange(seg_count, dtype=jnp.int32)
    return lax.optimization_barrier(jnp.sum((positions[:, None] >= sent_ends[None, :]).astype(jnp.int32), axis=1))

def attend(queries, key_rows, values, allowed):
    row_count = queries.shape[0]
    query_heads = queries.reshape(row_count, HEADS, HEAD_DIM)
    key_heads = key_rows.reshape(key_rows.shape[0], HEADS, HEAD_DIM)
    value_heads = values.reshape(values.shape[0], HEADS, HEAD_DIM)
    scores = jnp.einsum('qhd,khd->hqk', query_heads, key_heads, precision=highest) * HEAD_DIM ** (-0.5)
    scores = low_back(scores)
    scores = jnp.where(allowed[None], scores, masked_score)
    peaks = lax.optimization_barrier(jnp.max(scores, axis=-1, keepdims=True))
    powers = jnp.exp(scores - peaks)
    weights = low(powers / lax.optimization_barrier(jnp.sum(powers, axis=-1, keepdims=True)))
    mixture = jnp.einsum('hqk,khd->qhd', weights, value_heads, precision=highest)
    return mixture.reshape(row_count, HEADS * HEAD_DIM)

def device_layer(tokens, memory, sent_seg, mem_seg, weights):
    proj_in, proj_out, ffn_in, ffn_out, ln_gain, ln_bias = weights
    positions = jnp.arange(tokens.shape[0], dtype=jnp.int32)
    self_allowed = (sent_seg[:, None] == sent_seg[None, :]) & (positions[None, :] <= positions[:, None])
    cross_allowed = sent_seg[:, None] == mem_seg[None, :]
    queries = both_ways(matmul(tokens, proj_in[0]))
    key_rows = both_ways(matmul(tokens, proj_in[1]))
    values = both_ways(matmul(tokens, proj_in[2]))
    self_mix = both_ways(attend(queries, key_rows, values, self_allowed))
    first_sum = residual_scale * tokens + low_back(matmul(self_mix, proj_out[0]))
    first_out = layer_norm(first_sum, ln_gain[0], ln_bias[0])
    first_low = low(first_out)
    cross_query = both_ways(matmul(first_low, proj_in[3]))
    cross_keys = both_ways(matmul(memory, proj_in[4]))
    cross_values = both_ways(matmul(memory, proj_in[5]))
    cross_mix = both_ways(attend(cross_query, cross_keys, cross_values, cross_allowed))
    second_sum = residual_scale * first_out + low_back(matmul(cross_mix, proj_out[1]))
    second_out = layer_norm(second_sum, ln_gain[1], ln_bias[1])
    second_low = low(second_out)
    hidden_pre = low_back(matmul(second_low, ffn_in))
    hidden_act = low(jax.nn.gelu(hidden_pre))
    third_sum = residual_scale * second_out + low_back(matmul(hidden_act, ffn_out))
    return layer_norm(third_sum, ln_gain[2], ln_bias[2])

def reference(tokens, memory, cotangent, sent_len, mem_len, proj_in, proj_out, ffn_in, ffn_out, ln_gain, ln_bias):
    width = tokens.shape[1]
    dev_count = tokens.shape[0] // TOK_DEV
    token_blocks = tokens.astype(jnp.float32).reshape(dev_count, TOK_DEV, width)
    memory_blocks = memory.astype(jnp.float32).reshape(dev_count, TOK_DEV, width)
    grad_blocks = cotangent.astype(jnp.float32).reshape(dev_count, TOK_DEV, width)
    sent_seg = jax.vmap(partial(segment_ids, seg_count=TOK_DEV))(sent_len)
    mem_seg = jax.vmap(partial(segment_ids, seg_count=TOK_DEV))(mem_len)
    weights = tuple((weight.astype(jnp.float32) for weight in (proj_in, proj_out, ffn_in, ffn_out, ln_gain, ln_bias)))

    def forward(token_blocks, memory_blocks, weights):

        def layer_step(unused_carry, block_data):
            result = jax.checkpoint(device_layer)(block_data[0], block_data[1], block_data[2], block_data[3], weights)
            return (unused_carry, result)
        _, outputs = lax.scan(layer_step, None, (token_blocks, memory_blocks, sent_seg, mem_seg))
        return outputs
    outputs, pullback = jax.vjp(forward, token_blocks, memory_blocks, weights)
    grad_tok, grad_mem, grad_weights = pullback(grad_blocks)
    return (outputs.reshape(-1, width).astype(jnp.bfloat16), grad_tok.reshape(-1, width).astype(jnp.bfloat16), grad_mem.reshape(-1, width).astype(jnp.bfloat16), grad_weights[0], grad_weights[1], grad_weights[2], grad_weights[3], grad_weights[4], grad_weights[5])
```

```python
import functools

import jax
import jax.numpy as jnp
from jax import lax
from jax.experimental import pallas as pl
from jax.experimental.pallas import tpu as pltpu
from jax.sharding import PartitionSpec as P

HEADS = 16
HEAD_DIM = 64


residual_scale = 300.0**0.25
masked_score = -1000000000.0


def layer_norm(summed, scale_row, shift_row):
    middle = jnp.mean(summed, axis=-1, keepdims=True)
    centered = summed - middle
    spread = jnp.mean(centered * centered, axis=-1, keepdims=True)
    return centered * lax.rsqrt(spread + 1e-05) * scale_row + shift_row


def segment_ids(lengths, seg_count):
    sent_ends = jnp.cumsum(lengths)
    positions = jnp.arange(seg_count, dtype=jnp.int32)
    return jnp.sum((positions[:, None] >= sent_ends[None, :]).astype(jnp.int32), axis=1)


def split_blocks(array, block_rows):
    return array.reshape((array.shape[0] // block_rows, block_rows) + array.shape[1:])


def block_scores(query_blk, key_heads, seg_blk, row_blk, key_seg, causal):
    scores = jnp.einsum(
        "qhd,khd->hqk", query_blk, key_heads, preferred_element_type=jnp.float32
    ) * HEAD_DIM ** (-0.5)
    allowed = seg_blk[:, None] == key_seg[None, :]
    if causal:
        allowed = allowed & (
            jnp.arange(key_seg.shape[0], dtype=jnp.int32)[None, :] <= row_blk[:, None]
        )
    return jnp.where(allowed[None], scores, masked_score)


def attend_forward(queries, key_rows, values, query_seg, key_seg, causal):
    row_count = queries.shape[0]
    block_rows = min(row_count, 512)
    key_heads = key_rows.reshape(key_rows.shape[0], HEADS, HEAD_DIM)
    value_heads = values.reshape(values.shape[0], HEADS, HEAD_DIM)
    positions = jnp.arange(row_count, dtype=jnp.int32)
    pieces = (
        split_blocks(queries.reshape(row_count, HEADS, HEAD_DIM), block_rows),
        split_blocks(query_seg, block_rows),
        split_blocks(positions, block_rows),
    )

    def one_block(piece):
        query_blk, seg_blk, row_blk = piece
        scores = block_scores(query_blk, key_heads, seg_blk, row_blk, key_seg, causal)
        peaks = jnp.max(scores, axis=-1, keepdims=True)
        powers = jnp.exp(scores - peaks)
        totals = jnp.sum(powers, axis=-1, keepdims=True)
        weights = (powers / totals).astype(jnp.bfloat16)
        mixture = jnp.einsum(
            "hqk,khd->qhd", weights, value_heads, preferred_element_type=jnp.float32
        )
        return (mixture, (peaks + jnp.log(totals))[..., 0])

    mixture, log_totals = lax.map(one_block, pieces)
    return (mixture.reshape(row_count, HEADS * HEAD_DIM).astype(jnp.bfloat16), log_totals)


def attend_backward(queries, key_rows, values, query_seg, key_seg, causal, log_totals, grad_mix):
    row_count = queries.shape[0]
    block_rows = min(row_count, 512)
    score_scale = HEAD_DIM ** (-0.5)
    key_heads = key_rows.reshape(key_rows.shape[0], HEADS, HEAD_DIM)
    value_heads = values.reshape(values.shape[0], HEADS, HEAD_DIM)
    positions = jnp.arange(row_count, dtype=jnp.int32)
    pieces = (
        split_blocks(queries.reshape(row_count, HEADS, HEAD_DIM), block_rows),
        split_blocks(query_seg, block_rows),
        split_blocks(positions, block_rows),
        log_totals,
        split_blocks(grad_mix.reshape(row_count, HEADS, HEAD_DIM), block_rows),
    )

    def one_block(carried, piece):
        grad_keys, grad_values = carried
        query_blk, seg_blk, row_blk, lse_blk, grad_blk = piece
        scores = block_scores(query_blk, key_heads, seg_blk, row_blk, key_seg, causal)
        probs = jnp.exp(scores - lse_blk[:, :, None])
        grad_values = grad_values + jnp.einsum(
            "hqk,qhd->khd", probs.astype(jnp.bfloat16), grad_blk, preferred_element_type=jnp.float32
        )
        grad_probs = jnp.einsum(
            "qhd,khd->hqk", grad_blk, value_heads, preferred_element_type=jnp.float32
        )
        inner = jnp.sum(grad_probs * probs, axis=-1, keepdims=True)
        grad_scores = (probs * (grad_probs - inner)).astype(jnp.bfloat16)
        grad_query = (
            jnp.einsum("hqk,khd->qhd", grad_scores, key_heads, preferred_element_type=jnp.float32)
            * score_scale
        )
        grad_keys = (
            grad_keys
            + jnp.einsum("hqk,qhd->khd", grad_scores, query_blk, preferred_element_type=jnp.float32)
            * score_scale
        )
        return ((grad_keys, grad_values), grad_query)

    zeros = jnp.zeros(key_heads.shape, jnp.float32)
    (grad_keys, grad_values), grad_query = lax.scan(one_block, (zeros, zeros), pieces)
    width = HEADS * HEAD_DIM
    return (
        grad_query.reshape(row_count, width).astype(jnp.bfloat16),
        grad_keys.reshape(-1, width).astype(jnp.bfloat16),
        grad_values.reshape(-1, width).astype(jnp.bfloat16),
    )


def run_forward(tokens, memory, sent_seg, mem_seg, weights):
    proj_in, proj_out, ffn_in, ffn_out, ln_gain, ln_bias = weights
    gains = ln_gain.astype(jnp.float32)
    shifts = ln_bias.astype(jnp.float32)
    self_qkv = jnp.einsum(
        "td,wde->wte", tokens, proj_in[0:3], preferred_element_type=jnp.float32
    ).astype(jnp.bfloat16)
    self_mix, self_lse = attend_forward(
        self_qkv[0], self_qkv[1], self_qkv[2], sent_seg, sent_seg, True
    )
    first_sum = residual_scale * tokens.astype(jnp.float32) + jnp.dot(
        self_mix, proj_out[0], preferred_element_type=jnp.float32
    )
    first_out = layer_norm(first_sum, gains[0], shifts[0])
    first_low = first_out.astype(jnp.bfloat16)
    cross_query = jnp.dot(first_low, proj_in[3], preferred_element_type=jnp.float32).astype(
        jnp.bfloat16
    )
    cross_kv = jnp.einsum(
        "td,wde->wte", memory, proj_in[4:6], preferred_element_type=jnp.float32
    ).astype(jnp.bfloat16)
    cross_mix, cross_lse = attend_forward(
        cross_query, cross_kv[0], cross_kv[1], sent_seg, mem_seg, False
    )
    second_sum = residual_scale * first_out + jnp.dot(
        cross_mix, proj_out[1], preferred_element_type=jnp.float32
    )
    second_out = layer_norm(second_sum, gains[1], shifts[1])
    second_low = second_out.astype(jnp.bfloat16)
    hidden_pre = jnp.dot(second_low, ffn_in, preferred_element_type=jnp.float32)
    hidden_act = jax.nn.gelu(hidden_pre).astype(jnp.bfloat16)
    third_sum = residual_scale * second_out + jnp.dot(
        hidden_act, ffn_out, preferred_element_type=jnp.float32
    )
    final = layer_norm(third_sum, gains[2], shifts[2])
    return {
        "self_qkv": self_qkv,
        "self_mix": self_mix,
        "self_lse": self_lse,
        "first_sum": first_sum,
        "first_low": first_low,
        "cross_query": cross_query,
        "cross_kv": cross_kv,
        "cross_mix": cross_mix,
        "cross_lse": cross_lse,
        "second_sum": second_sum,
        "second_low": second_low,
        "hidden_pre": hidden_pre,
        "hidden_act": hidden_act,
        "third_sum": third_sum,
        "final": final,
    }


def run_backward(saved, tokens, memory, sent_seg, mem_seg, weights, cotangent):
    proj_in, proj_out, ffn_in, ffn_out, ln_gain, ln_bias = weights
    gains = ln_gain.astype(jnp.float32)
    shifts = ln_bias.astype(jnp.float32)
    _, pull_third = jax.vjp(layer_norm, saved["third_sum"], gains[2], shifts[2])
    grad_third, gain_third, shift_third = pull_third(cotangent.astype(jnp.float32))
    third_low = grad_third.astype(jnp.bfloat16)
    grad_ffn_out = jnp.einsum(
        "tf,td->fd", saved["hidden_act"], third_low, preferred_element_type=jnp.float32
    )
    grad_act = jnp.einsum("td,fd->tf", third_low, ffn_out, preferred_element_type=jnp.float32)
    _, pull_gelu = jax.vjp(jax.nn.gelu, saved["hidden_pre"])
    grad_pre = pull_gelu(grad_act)[0].astype(jnp.bfloat16)
    grad_ffn_in = jnp.einsum(
        "td,tf->df", saved["second_low"], grad_pre, preferred_element_type=jnp.float32
    )
    grad_second = residual_scale * grad_third + jnp.einsum(
        "tf,df->td", grad_pre, ffn_in, preferred_element_type=jnp.float32
    )
    ffn_grads = (grad_ffn_in, grad_ffn_out, gain_third, shift_third)
    _, pull_second = jax.vjp(layer_norm, saved["second_sum"], gains[1], shifts[1])
    grad_two, gain_second, shift_second = pull_second(grad_second)
    two_low = grad_two.astype(jnp.bfloat16)
    grad_cross_out = jnp.einsum(
        "te,td->ed", saved["cross_mix"], two_low, preferred_element_type=jnp.float32
    )
    grad_cross_mix = jnp.einsum(
        "td,ed->te", two_low, proj_out[1], preferred_element_type=jnp.float32
    ).astype(jnp.bfloat16)
    grad_cq, grad_ck, grad_cv = attend_backward(
        saved["cross_query"],
        saved["cross_kv"][0],
        saved["cross_kv"][1],
        sent_seg,
        mem_seg,
        False,
        saved["cross_lse"],
        grad_cross_mix,
    )
    grad_ckv = jnp.stack([grad_ck, grad_cv])
    grad_cross_in = jnp.concatenate(
        [
            jnp.einsum(
                "td,te->de", saved["first_low"], grad_cq, preferred_element_type=jnp.float32
            )[None],
            jnp.einsum("td,wte->wde", memory, grad_ckv, preferred_element_type=jnp.float32),
        ],
        axis=0,
    )
    grad_memory = jnp.einsum(
        "wte,wde->td", grad_ckv, proj_in[4:6], preferred_element_type=jnp.float32
    ).astype(jnp.bfloat16)
    grad_first = residual_scale * grad_two + jnp.einsum(
        "te,de->td", grad_cq, proj_in[3], preferred_element_type=jnp.float32
    )
    cross_grads = (grad_cross_in, grad_cross_out, gain_second, shift_second)
    _, pull_first = jax.vjp(layer_norm, saved["first_sum"], gains[0], shifts[0])
    grad_one, gain_first, shift_first = pull_first(grad_first)
    one_low = grad_one.astype(jnp.bfloat16)
    grad_self_out = jnp.einsum(
        "te,td->ed", saved["self_mix"], one_low, preferred_element_type=jnp.float32
    )
    grad_self_mix = jnp.einsum(
        "td,ed->te", one_low, proj_out[0], preferred_element_type=jnp.float32
    ).astype(jnp.bfloat16)
    self_qkv = saved["self_qkv"]
    grad_sq, grad_sk, grad_sv = attend_backward(
        self_qkv[0],
        self_qkv[1],
        self_qkv[2],
        sent_seg,
        sent_seg,
        True,
        saved["self_lse"],
        grad_self_mix,
    )
    grad_sqkv = jnp.stack([grad_sq, grad_sk, grad_sv])
    grad_self_in = jnp.einsum("td,wte->wde", tokens, grad_sqkv, preferred_element_type=jnp.float32)
    grad_tokens = (
        residual_scale * grad_one
        + jnp.einsum("wte,wde->td", grad_sqkv, proj_in[0:3], preferred_element_type=jnp.float32)
    ).astype(jnp.bfloat16)
    self_grads = (grad_self_in, grad_self_out, gain_first, shift_first)
    all_in = jnp.concatenate([self_grads[0], cross_grads[0]], axis=0)
    all_out = jnp.stack([self_grads[1], cross_grads[1]])
    all_gain = jnp.stack([self_grads[2], cross_grads[2], ffn_grads[2]])
    all_bias = jnp.stack([self_grads[3], cross_grads[3], ffn_grads[3]])
    return (
        grad_tokens,
        grad_memory,
        all_in,
        all_out,
        ffn_grads[0],
        ffn_grads[1],
        all_gain,
        all_bias,
    )


MESH = pl.DeviceIdType.MESH
BOTH = ("dp", "fsdp")
f32 = jnp.float32
bf16 = jnp.bfloat16
UNITS = 17
def shard_of(unit):
    if unit < 12:
        return (32, 1024)
    return (128, 256) if unit < 16 else (16, 128)


class Place:
    def __init__(self):
        inner = lax.axis_index("fsdp")
        self.y = lax.axis_index("dp")
        self.z = inner // 4
        self.x = (inner // 2) % 2
        self.c = inner % 2

    def at(self, y=None, z=None, x=None, c=None):
        y = self.y if y is None else y
        z = self.z if z is None else z
        x = self.x if x is None else x
        c = self.c if c is None else c
        return (y, (z * 2 + x) * 2 + c)

    def over_x(self):
        return self.at(x=1 - self.x)

    def over_y(self):
        return self.at(y=1 - self.y)

    def sibling(self):
        return self.at(c=1 - self.c)

    def greet(self):
        barrier = pltpu.get_barrier_semaphore()
        friends = [self.at(z=lax.rem(self.z + k, 4)) for k in (1, 2, 3)]
        friends += [self.over_x(), self.over_y(), self.sibling()]
        for friend in friends:
            pl.semaphore_signal(barrier, inc=1, device_id=friend, device_id_type=MESH)
        pl.semaphore_wait(barrier, len(friends))


class Sender:
    def __init__(self, place, send_sem, recv_sem):
        self.p, self.send_sem, self.recv_sem = place, send_sem, recv_sem
        self.pending = {}

    def copy(self, unit, slot, src, dst, device, landing=None):
        return pltpu.make_async_remote_copy(
            src_ref=src,
            dst_ref=dst,
            send_sem=self.send_sem.at[unit, slot],
            recv_sem=self.recv_sem.at[unit, slot if landing is None else landing],
            device_id=device,
            device_id_type=MESH,
        )

    def send(self, unit, slot, src, dst, device, cond=None, landing=None):
        make = lambda: self.copy(unit, slot, src, dst, device, landing)
        if cond is None:
            make().start()
            self.pending.setdefault(unit, []).append(lambda: make().wait_send())
        else:
            pl.when(cond)(lambda: make().start())
            self.pending.setdefault(unit, []).append(
                lambda: pl.when(cond)(lambda: make().wait_send())
            )

    def wait(self, unit, slot, ref):
        self.copy(unit, slot, ref, ref, self.p.sibling()).wait_recv()

    def finish(self, unit):
        for done in self.pending.pop(unit, []):
            done()


class Gather(Sender):
    stages = (0, 0.5, 1, 1.5, 2, 3, 4)

    def __init__(self, place, send_sem, recv_sem, whole, kinds):
        super().__init__(place, send_sem, recv_sem)
        self.whole, self.kinds = whole, kinds

    def view(self, unit, y=None, z=None, x=None, c=None):
        every = slice(None)
        pick = lambda v: every if v is None else v
        return self.whole(unit).at[pick(y), pick(z), pick(x), pick(c)]

    def along_z(self, unit):
        p, kind = self.p, self.kinds[unit]
        if kind[0] == "p":
            return lambda z: self.view(unit, y=p.y, z=z, x=p.x, c=p.c)
        if kind == "rL":
            return lambda z: self.view(unit, y=p.y, z=z, c=p.c)
        return lambda z: self.view(unit, z=z, x=p.x, c=p.c)

    def z_send(self, unit):
        p, part = self.p, self.along_z(unit)
        for k in (1, 2, 3):
            there = lax.rem(p.z + k, 4)
            near = jnp.logical_not(
                ((p.z == 0) & (there == 3)) | ((p.z == 3) & (there == 0))
            )
            self.send(unit, there, part(p.z), part(p.z), p.at(z=there), near, landing=p.z)

    def z_relay(self, unit):
        p, part = self.p, self.along_z(unit)
        for here, source, there in ((2, 0, 3), (1, 3, 0)):
            pl.when(p.z == here)(lambda source=source: self.wait(unit, source, part(source)))
            self.send(
                unit, 8, part(source), part(source), p.at(z=there), p.z == here, landing=source
            )

    def z_wait(self, unit):
        p, part = self.p, self.along_z(unit)
        for k in (1, 2, 3):
            source = lax.rem(p.z + 4 - k, 4)
            relayed = ((p.z == 2) & (source == 0)) | ((p.z == 1) & (source == 3))
            pl.when(jnp.logical_not(relayed))(
                lambda source=source: self.wait(unit, source, part(source))
            )

    def stage(self, unit, step):
        p, kind = self.p, self.kinds[unit]
        y, z, x, c = p.y, p.z, p.x, p.c
        view = lambda **at: self.view(unit, **at)
        send = lambda slot, ref, device: self.send(unit, slot, ref, ref, device)
        if kind[0] == "p":
            if step == 0:
                self.z_send(unit)
            if step == 0.5:
                self.z_relay(unit)
            if step == 1:
                self.z_wait(unit)
                line = view(y=y, x=x, c=c)
                send(4, line, p.over_x())
                send(5, line, p.over_y())
            if step == 2:
                if kind == "pL":
                    line = view(y=y, x=1 - x, c=c)
                    self.wait(unit, 4, line)
                    send(6, line, p.over_y())
                else:
                    line = view(y=1 - y, x=x, c=c)
                    self.wait(unit, 5, line)
                    send(6, line, p.over_x())
            if step == 3:
                if kind == "pL":
                    self.wait(unit, 5, view(y=1 - y, x=x, c=c))
                else:
                    self.wait(unit, 4, view(y=y, x=1 - x, c=c))
                self.wait(unit, 6, view(y=1 - y, x=1 - x, c=c))
                send(7, view(c=c), p.sibling())
        else:
            left = kind == "rL"
            first, last = (p.over_x(), p.over_y()) if left else (p.over_y(), p.over_x())
            if step == 0:
                send(4, view(y=y, z=z, x=x, c=c), first)
            if step == 1:
                self.wait(
                    unit,
                    4,
                    view(y=y, z=z, x=1 - x, c=c) if left else view(y=1 - y, z=z, x=x, c=c),
                )
                self.z_send(unit)
            if step == 1.5:
                self.z_relay(unit)
            if step == 2:
                self.z_wait(unit)
                send(5, view(y=y, c=c) if left else view(x=x, c=c), last)
            if step == 3:
                self.wait(unit, 5, view(y=1 - y, c=c) if left else view(x=1 - x, c=c))
                send(7, view(c=c), p.sibling())
        if step == 4:
            self.wait(unit, 7, view(c=1 - c))


class Scatter(Sender):
    stages = (0, 1, 2, 2.5, 3, 3.5, 4, 5)

    def __init__(self, place, send_sem, recv_sem, other, mine, twin, eight, four, zs, out, kinds):
        super().__init__(place, send_sem, recv_sem)
        self.other, self.mine, self.twin = other, mine, twin
        self.eight, self.four, self.zs, self.out, self.kinds = eight, four, zs, out, kinds

    def add(self, into, *terms):
        total = into[...].astype(f32)
        for term in terms:
            total = total + term[...].astype(f32)
        into[...] = total.astype(into.dtype)

    def along_z(self, unit):
        p, kind, mine = self.p, self.kinds[unit], self.mine(unit)
        if kind[0] == "p":
            return (lambda z: mine.at[p.y, z, p.x]), (lambda ref: ref.at[0])
        if kind == "rL":
            return (lambda z: mine.at[p.y, z]), (lambda ref: ref)
        return (lambda z: mine.at[:, z, p.x]), (lambda ref: ref)

    def z_send(self, unit):
        p, zs = self.p, self.zs(unit)
        part, slot = self.along_z(unit)
        for k in (1, 2, 3):
            there = lax.rem(p.z + k, 4)
            far = ((p.z == 0) & (there == 3)) | ((p.z == 3) & (there == 0))
            relayed = ((p.z == 2) & (there == 0)) | ((p.z == 1) & (there == 3))
            self.send(
                unit,
                4 + there,
                part(there),
                slot(zs.at[p.z]),
                p.at(z=there),
                jnp.logical_not(far | relayed),
                landing=4 + p.z,
            )
        self.send(unit, 8, part(3), slot(zs.at[1]), p.at(z=1), p.z == 0)
        self.send(unit, 8, part(0), slot(zs.at[2]), p.at(z=2), p.z == 3)

    def z_relay(self, unit):
        p, zs = self.p, self.zs(unit)
        part, slot = self.along_z(unit)
        for here, there in ((1, 3), (2, 0)):

            @pl.when(p.z == here)
            def _(here=here, there=there):
                self.wait(unit, 8, slot(zs.at[here]))
                self.add(part(there), slot(zs.at[here]))

            self.send(
                unit,
                4 + there,
                part(there),
                slot(zs.at[here]),
                p.at(z=there),
                p.z == here,
                landing=4 + here,
            )

    def z_sum(self, unit, store):
        p, zs = self.p, self.zs(unit)
        part, slot = self.along_z(unit)
        edge = (p.z == 0) | (p.z == 3)

        @pl.when(edge)
        def _():
            self.wait(unit, 5, slot(zs.at[1]))
            self.wait(unit, 6, slot(zs.at[2]))
            store(
                part(p.z)[...].astype(f32)
                + slot(zs.at[1])[...].astype(f32)
                + slot(zs.at[2])[...].astype(f32)
            )

        @pl.when(jnp.logical_not(edge))
        def _():
            inner = 3 - p.z
            self.wait(unit, 4, slot(zs.at[0]))
            self.wait(unit, 7, slot(zs.at[3]))
            self.wait(unit, 4 + inner, slot(zs.at[inner]))
            store(
                part(p.z)[...].astype(f32)
                + slot(zs.at[inner])[...].astype(f32)
                + slot(zs.at[0])[...].astype(f32)
                + slot(zs.at[3])[...].astype(f32)
            )

    def stage(self, unit, step):
        p, kind = self.p, self.kinds[unit]
        y, z, x = p.y, p.z, p.x
        mine, eight, four, out = self.mine(unit), self.eight(unit), self.four(unit), self.out(unit)
        send = lambda slot, src, dst, device: self.send(unit, slot, src, dst, device)
        if step == 0:
            send(0, self.other(unit), self.twin(unit), p.sibling())
        if step == 1:
            self.wait(unit, 0, self.twin(unit))
            for half in (0, 1):
                self.add(mine.at[half], self.twin(unit).at[half])
            self.finish(unit)
            if kind == "pL":
                send(1, mine.at[1 - y, :, 1 - x], eight.at[0], p.over_y())
                send(3, mine.at[1 - y, :, x], four, p.over_y())
            if kind == "pR":
                send(1, mine.at[1 - y, :, 1 - x], eight.at[0], p.over_x())
                send(3, mine.at[y, :, 1 - x], four, p.over_x())
            for half in (0, 1):
                if kind == "rL":
                    send(1 + half, mine.at[1 - y, :, half], eight.at[half], p.over_y())
                if kind == "rR":
                    send(1 + half, mine.at[half, :, 1 - x], eight.at[half], p.over_x())
        if step == 2:
            if kind[0] == "p":
                self.wait(unit, 1, eight.at[0])
                line = mine.at[y, :, 1 - x] if kind == "pL" else mine.at[1 - y, :, x]
                self.add(line, eight.at[0])
                send(2, line, eight.at[1], p.over_x() if kind == "pL" else p.over_y())
            else:
                for half in (0, 1):
                    self.wait(unit, 1 + half, eight.at[half])
                    self.add(
                        mine.at[y, :, half] if kind == "rL" else mine.at[half, :, x],
                        eight.at[half],
                    )
                self.z_send(unit)
        if step == 2.5 and kind[0] == "r":
            self.z_relay(unit)
        if step == 3:
            if kind[0] == "p":
                self.wait(unit, 3, four)
                self.wait(unit, 2, eight.at[1])
                self.add(mine.at[y, :, x], four, eight.at[1])
                self.z_send(unit)
            else:
                line = mine.at[y, z] if kind == "rL" else mine.at[:, z, x]

                def keep(value):
                    line[...] = value.astype(bf16)

                self.z_sum(unit, keep)
                if kind == "rL":
                    send(3, mine.at[y, z, 1 - x], four.at[0], p.over_x())
                else:
                    send(3, mine.at[1 - y, z, x], four.at[0], p.over_y())
        if step == 3.5 and kind[0] == "p":
            self.z_relay(unit)
        if step == 4:

            def result(value):
                out[...] = value

            if kind[0] == "p":
                self.z_sum(unit, result)
            else:
                self.wait(unit, 3, four.at[0])
                result(mine[y, z, x].astype(f32) + four[0].astype(f32))
        if step == 5:
            self.finish(unit)


def kinds_of(pattern, order):
    kinds = {}
    for place, unit in enumerate(order):
        kinds[unit] = pattern[(place // 2) % len(pattern)] + "LR"[place % 2]
    return kinds

GATHER_ORDER = list(range(17))
GATHER_KINDS = kinds_of("rprrprpr", GATHER_ORDER)
GATHER_LAG = 2.0
SCATTER_ORDER = list(range(17))
SCATTER_KINDS = kinds_of("p", SCATTER_ORDER)
SCATTER_LAG = 1.5


def gather_kernel(
    proj_in, proj_out, ffn_in, ffn_out, small, wide, deep, tiny, send_sem, recv_sem, local_sem
):
    place = Place()

    def whole(unit):
        return wide.at[unit] if unit < 12 else deep.at[unit - 12] if unit < 16 else tiny

    def own(unit):
        if unit < 6:
            return proj_in.at[unit]
        if unit < 8:
            return proj_out.at[unit - 6]
        if unit < 12:
            return ffn_in.at[:, pl.ds((unit - 8) * 1024, 1024)]
        if unit < 16:
            return ffn_out.at[:, pl.ds((unit - 12) * 256, 256)]
        return small

    gather = Gather(place, send_sem, recv_sem, whole, GATHER_KINDS)
    copies = {}
    for unit in GATHER_ORDER:
        copies[unit] = pltpu.make_async_copy(
            own(unit), whole(unit).at[place.y, place.z, place.x, place.c], local_sem.at[unit]
        )
        copies[unit].start()
    place.greet()
    events = sorted(
        (turn + step * GATHER_LAG, step, unit)
        for turn, unit in enumerate(GATHER_ORDER)
        for step in Gather.stages
    )
    for _, step, unit in events:
        if step == 0:
            copies[unit].wait()
        gather.stage(unit, step)
    for unit in GATHER_ORDER:
        gather.finish(unit)


def gather_weights(proj_in, proj_out, ffn_in, ffn_out, small):
    return pl.pallas_call(
        gather_kernel,
        out_shape=(
            jax.ShapeDtypeStruct((12, 2, 4, 2, 2, 32, 1024), bf16),
            jax.ShapeDtypeStruct((4, 2, 4, 2, 2, 128, 256), bf16),
            jax.ShapeDtypeStruct((2, 4, 2, 2, 16, 128), bf16),
        ),
        in_specs=[pl.BlockSpec(memory_space=pl.ANY)] * 5,
        out_specs=[pl.BlockSpec(memory_space=pl.ANY)] * 3,
        scratch_shapes=[
            pltpu.SemaphoreType.DMA((UNITS, 9)),
            pltpu.SemaphoreType.DMA((UNITS, 9)),
            pltpu.SemaphoreType.DMA((UNITS,)),
        ],
        compiler_params=pltpu.CompilerParams(
            collective_id=0, has_side_effects=True, vmem_limit_bytes=56 << 20
        ),
    )(proj_in, proj_out, ffn_in, ffn_out, small)


def scatter_kernel(depth, *refs):
    wide, deep, tiny, out_wide, out_deep, out_tiny = refs[:6]
    buffers, (send_sem, recv_sem, local_sem, out_sem) = refs[6:-4], refs[-4:]
    place = Place()
    sort = lambda unit: 0 if unit < 12 else 1 if unit < 16 else 2
    sums = buffers[18:21]
    rank = {u: sum(1 for v in SCATTER_ORDER[:i] if sort(v) == sort(u)) for i, u in enumerate(SCATTER_ORDER)}

    def ring(kind):
        def pick(unit):
            ref = buffers[3 * kind + sort(unit)]
            return ref.at[rank[unit] % ref.shape[0]]

        return pick

    def out(unit):
        if unit < 12:
            return sums[0].at[unit]
        if unit < 16:
            return sums[1].at[:, pl.ds((unit - 12) * 256, 256)]
        return sums[2]

    scatter = Scatter(
        place, send_sem, recv_sem, *[ring(kind) for kind in range(6)], out, SCATTER_KINDS
    )
    place.greet()

    def fetch(unit):
        source = wide.at[unit] if unit < 12 else deep.at[unit - 12] if unit < 16 else tiny
        made = []
        for k, into in enumerate((scatter.mine(unit), scatter.other(unit))):
            core = place.c if k == 0 else 1 - place.c
            copy = pltpu.make_async_copy(source.at[:, :, :, core], into, local_sem.at[unit, k])
            copy.start()
            made.append(copy)
        return made

    events = [
        (turn + step * SCATTER_LAG, step, unit)
        for turn, unit in enumerate(SCATTER_ORDER)
        for step in Scatter.stages
    ]
    events += [(turn - 0.9, -1, unit) for turn, unit in enumerate(SCATTER_ORDER)]
    fetched = {}
    for _, step, unit in sorted(events):
        if step == -1:
            fetched[unit] = fetch(unit)
            continue
        if step == 0:
            for copy in fetched[unit]:
                copy.wait()
        scatter.stage(unit, step)
    for k, (src, dst) in enumerate(zip(sums, (out_wide, out_deep, out_tiny))):
        copy = pltpu.make_async_copy(src, dst, out_sem.at[k])
        copy.start()
        copy.wait()


def scatter_grads(wide, deep, tiny):
    shapes = [shard_of(0), shard_of(12), shard_of(16)]
    whole = [12, 4, 1]
    rings = [
        ((2, 4, 2), (4, 4, 1)),
        ((2, 4, 2), (10, 4, 1)),
        ((2, 4, 2), whole),
        ((2, 4), whole),
        ((4,), whole),
        ((4, 2), whole),
    ]
    scratch = []
    for lead, counts in rings:
        for shape, count in zip(shapes, counts):
            scratch.append(pltpu.VMEM((count, *lead, *shape), bf16))
    results = [(12, 32, 1024), (128, 1024), (16, 128)]
    return pl.pallas_call(
        functools.partial(scatter_kernel, None),
        out_shape=[jax.ShapeDtypeStruct(shape, f32) for shape in results],
        in_specs=[pl.BlockSpec(memory_space=pl.ANY)] * 3,
        out_specs=[pl.BlockSpec(memory_space=pl.ANY)] * 3,
        scratch_shapes=scratch
        + [pltpu.VMEM(shape, f32) for shape in results]
        + [
            pltpu.SemaphoreType.DMA((UNITS, 9)),
            pltpu.SemaphoreType.DMA((UNITS, 9)),
            pltpu.SemaphoreType.DMA((UNITS, 2)),
            pltpu.SemaphoreType.DMA((3,)),
        ],
        compiler_params=pltpu.CompilerParams(
            collective_id=1, has_side_effects=True, vmem_limit_bytes=62 << 20
        ),
    )(wide, deep, tiny)


def lane_of_device():
    return (lax.axis_index("fsdp") % 4) * 32


def on_device(
    tokens, memory, cotangent, sent_len, mem_len, proj_in, proj_out, ffn_in, ffn_out, ln_gain, ln_bias
):
    small = jnp.concatenate([ln_gain, ln_bias, jnp.zeros((10, 32), bf16)], axis=0)
    small = jnp.concatenate(
        [
            jnp.where(lax.axis_index("fsdp") % 4 == k, small, jnp.zeros_like(small))
            for k in range(4)
        ],
        axis=1,
    )
    wide, deep, tiny = gather_weights(proj_in, proj_out, ffn_in, ffn_out, small)
    square = wide.reshape(12, 1024, 1024)
    rows = tiny.reshape(8, 4, 16, 128).sum(1).transpose(1, 0, 2).reshape(16, 1024)
    weights = (
        square[0:6],
        square[6:8],
        jnp.concatenate([square[k] for k in range(8, 12)], axis=1),
        jnp.concatenate([deep[k].reshape(4096, 256) for k in range(4)], axis=1),
        rows[0:3],
        rows[3:6],
    )
    sent_seg = segment_ids(sent_len[0], tokens.shape[0])
    mem_seg = segment_ids(mem_len[0], memory.shape[0])
    saved = run_forward(tokens, memory, sent_seg, mem_seg, weights)
    output = saved["final"].astype(bf16)
    grad_tokens, grad_memory, all_in, all_out, g_in, g_out, gains, biases = run_backward(
        saved, tokens, memory, sent_seg, mem_seg, weights, cotangent
    )
    terms = jnp.concatenate(
        [all_in.astype(bf16), all_out.astype(bf16), g_in.astype(bf16).reshape(1024, 4, 1024).transpose(1, 0, 2)]
    )
    affine = jnp.concatenate([gains, biases, jnp.zeros((10, 1024), f32)]).astype(bf16)
    affine = affine.reshape(16, 8, 128).transpose(1, 0, 2)
    affine = jnp.broadcast_to(affine[:, None], (8, 4, 16, 128)).reshape(1, 2, 4, 2, 2, 16, 128)
    got_wide, got_deep, got_tiny = scatter_grads(
        terms.reshape(12, 2, 4, 2, 2, 32, 1024),
        g_out.astype(bf16).reshape(4096, 4, 256).transpose(1, 0, 2).reshape(4, 2, 4, 2, 2, 128, 256),
        affine[0],
    )
    own = lax.dynamic_slice(got_tiny, (0, lane_of_device()), (16, 32))
    return (
        output,
        grad_tokens,
        grad_memory,
        got_wide[0:6],
        got_wide[6:8],
        got_wide[8:12].transpose(1, 0, 2).reshape(32, 4096),
        got_deep,
        own[0:3],
        own[3:6],
    )


def on_any_mesh(
    tokens, memory, cotangent, sent_len, mem_len, proj_in, proj_out, ffn_in, ffn_out, ln_gain, ln_bias
):
    dims = (1, 1, 0, 0, 1, 1)
    shards = (proj_in, proj_out, ffn_in, ffn_out, ln_gain, ln_bias)
    weights = tuple(
        lax.all_gather(shard, BOTH, axis=dim, tiled=True) for shard, dim in zip(shards, dims)
    )
    sent_seg = segment_ids(sent_len[0], tokens.shape[0])
    mem_seg = segment_ids(mem_len[0], memory.shape[0])
    saved = run_forward(tokens, memory, sent_seg, mem_seg, weights)
    output = saved["final"].astype(bf16)
    grads = run_backward(saved, tokens, memory, sent_seg, mem_seg, weights, cotangent)
    summed = tuple(
        lax.psum_scatter(grad, BOTH, scatter_dimension=dim, tiled=True)
        for grad, dim in zip(grads[2:], dims)
    )
    return (output, *grads[:2], *summed)


def solution(mesh):
    placed = (
        P(BOTH, None),
        P(BOTH, None),
        P(BOTH, None),
        P(BOTH, None),
        P(BOTH, None),
        P(None, BOTH, None),
        P(None, BOTH, None),
        P(BOTH, None),
        P(BOTH, None),
        P(None, BOTH),
        P(None, BOTH),
    )
    routed = mesh.shape["dp"] == 2 and mesh.shape["fsdp"] == 16
    return jax.shard_map(
        on_device if routed else on_any_mesh,
        mesh=mesh,
        in_specs=placed,
        out_specs=(
            P(BOTH, None),
            P(BOTH, None),
            P(BOTH, None),
            P(None, BOTH, None),
            P(None, BOTH, None),
            P(BOTH, None),
            P(BOTH, None),
            P(None, BOTH),
            P(None, BOTH),
        ),
        check_vma=False,
    )
```

```python
import functools

import jax
import jax.numpy as jnp
from jax import lax
from jax.experimental import pallas as pl
from jax.experimental.pallas import tpu as pltpu
from jax.sharding import PartitionSpec as P

HEADS = 16
HEAD_DIM = 64


residual_scale = 300.0**0.25
masked_score = -1000000000.0


def layer_norm(summed, scale_row, shift_row):
    middle = jnp.mean(summed, axis=-1, keepdims=True)
    centered = summed - middle
    spread = jnp.mean(centered * centered, axis=-1, keepdims=True)
    return centered * lax.rsqrt(spread + 1e-05) * scale_row + shift_row


def segment_ids(lengths, seg_count):
    sent_ends = jnp.cumsum(lengths)
    positions = jnp.arange(seg_count, dtype=jnp.int32)
    return jnp.sum((positions[:, None] >= sent_ends[None, :]).astype(jnp.int32), axis=1)


def split_blocks(array, block_rows):
    return array.reshape((array.shape[0] // block_rows, block_rows) + array.shape[1:])


def block_scores(query_blk, key_heads, seg_blk, row_blk, key_seg, causal):
    scores = jnp.einsum(
        "qhd,khd->hqk", query_blk, key_heads, preferred_element_type=jnp.float32
    ) * HEAD_DIM ** (-0.5)
    allowed = seg_blk[:, None] == key_seg[None, :]
    if causal:
        allowed = allowed & (
            jnp.arange(key_seg.shape[0], dtype=jnp.int32)[None, :] <= row_blk[:, None]
        )
    return jnp.where(allowed[None], scores, masked_score)


def attend_forward(queries, key_rows, values, query_seg, key_seg, causal):
    row_count = queries.shape[0]
    block_rows = min(row_count, 512)
    key_heads = key_rows.reshape(key_rows.shape[0], HEADS, HEAD_DIM)
    value_heads = values.reshape(values.shape[0], HEADS, HEAD_DIM)
    positions = jnp.arange(row_count, dtype=jnp.int32)
    pieces = (
        split_blocks(queries.reshape(row_count, HEADS, HEAD_DIM), block_rows),
        split_blocks(query_seg, block_rows),
        split_blocks(positions, block_rows),
    )

    def one_block(piece):
        query_blk, seg_blk, row_blk = piece
        scores = block_scores(query_blk, key_heads, seg_blk, row_blk, key_seg, causal)
        peaks = jnp.max(scores, axis=-1, keepdims=True)
        powers = jnp.exp(scores - peaks)
        totals = jnp.sum(powers, axis=-1, keepdims=True)
        weights = (powers / totals).astype(jnp.bfloat16)
        mixture = jnp.einsum(
            "hqk,khd->qhd", weights, value_heads, preferred_element_type=jnp.float32
        )
        return (mixture, (peaks + jnp.log(totals))[..., 0])

    mixture, log_totals = lax.map(one_block, pieces)
    return (mixture.reshape(row_count, HEADS * HEAD_DIM).astype(jnp.bfloat16), log_totals)


def attend_backward(queries, key_rows, values, query_seg, key_seg, causal, log_totals, grad_mix):
    row_count = queries.shape[0]
    block_rows = min(row_count, 512)
    score_scale = HEAD_DIM ** (-0.5)
    key_heads = key_rows.reshape(key_rows.shape[0], HEADS, HEAD_DIM)
    value_heads = values.reshape(values.shape[0], HEADS, HEAD_DIM)
    positions = jnp.arange(row_count, dtype=jnp.int32)
    pieces = (
        split_blocks(queries.reshape(row_count, HEADS, HEAD_DIM), block_rows),
        split_blocks(query_seg, block_rows),
        split_blocks(positions, block_rows),
        log_totals,
        split_blocks(grad_mix.reshape(row_count, HEADS, HEAD_DIM), block_rows),
    )

    def one_block(carried, piece):
        grad_keys, grad_values = carried
        query_blk, seg_blk, row_blk, lse_blk, grad_blk = piece
        scores = block_scores(query_blk, key_heads, seg_blk, row_blk, key_seg, causal)
        probs = jnp.exp(scores - lse_blk[:, :, None])
        grad_values = grad_values + jnp.einsum(
            "hqk,qhd->khd", probs.astype(jnp.bfloat16), grad_blk, preferred_element_type=jnp.float32
        )
        grad_probs = jnp.einsum(
            "qhd,khd->hqk", grad_blk, value_heads, preferred_element_type=jnp.float32
        )
        inner = jnp.sum(grad_probs * probs, axis=-1, keepdims=True)
        grad_scores = (probs * (grad_probs - inner)).astype(jnp.bfloat16)
        grad_query = (
            jnp.einsum("hqk,khd->qhd", grad_scores, key_heads, preferred_element_type=jnp.float32)
            * score_scale
        )
        grad_keys = (
            grad_keys
            + jnp.einsum("hqk,qhd->khd", grad_scores, query_blk, preferred_element_type=jnp.float32)
            * score_scale
        )
        return ((grad_keys, grad_values), grad_query)

    zeros = jnp.zeros(key_heads.shape, jnp.float32)
    (grad_keys, grad_values), grad_query = lax.scan(one_block, (zeros, zeros), pieces)
    width = HEADS * HEAD_DIM
    return (
        grad_query.reshape(row_count, width).astype(jnp.bfloat16),
        grad_keys.reshape(-1, width).astype(jnp.bfloat16),
        grad_values.reshape(-1, width).astype(jnp.bfloat16),
    )


def run_forward(tokens, memory, sent_seg, mem_seg, weights):
    proj_in, proj_out, ffn_in, ffn_out, ln_gain, ln_bias = weights
    gains = ln_gain.astype(jnp.float32)
    shifts = ln_bias.astype(jnp.float32)
    self_qkv = jnp.einsum(
        "td,wde->wte", tokens, proj_in[0:3], preferred_element_type=jnp.float32
    ).astype(jnp.bfloat16)
    self_mix, self_lse = attend_forward(
        self_qkv[0], self_qkv[1], self_qkv[2], sent_seg, sent_seg, True
    )
    first_sum = residual_scale * tokens.astype(jnp.float32) + jnp.dot(
        self_mix, proj_out[0], preferred_element_type=jnp.float32
    )
    first_out = layer_norm(first_sum, gains[0], shifts[0])
    first_low = first_out.astype(jnp.bfloat16)
    cross_query = jnp.dot(first_low, proj_in[3], preferred_element_type=jnp.float32).astype(
        jnp.bfloat16
    )
    cross_kv = jnp.einsum(
        "td,wde->wte", memory, proj_in[4:6], preferred_element_type=jnp.float32
    ).astype(jnp.bfloat16)
    cross_mix, cross_lse = attend_forward(
        cross_query, cross_kv[0], cross_kv[1], sent_seg, mem_seg, False
    )
    second_sum = residual_scale * first_out + jnp.dot(
        cross_mix, proj_out[1], preferred_element_type=jnp.float32
    )
    second_out = layer_norm(second_sum, gains[1], shifts[1])
    second_low = second_out.astype(jnp.bfloat16)
    hidden_pre = jnp.dot(second_low, ffn_in, preferred_element_type=jnp.float32)
    hidden_act = jax.nn.gelu(hidden_pre).astype(jnp.bfloat16)
    third_sum = residual_scale * second_out + jnp.dot(
        hidden_act, ffn_out, preferred_element_type=jnp.float32
    )
    final = layer_norm(third_sum, gains[2], shifts[2])
    return {
        "a": self_qkv,
        "b": self_mix,
        "c": self_lse,
        "d": first_sum,
        "e": first_low,
        "f": cross_query,
        "g": cross_kv,
        "h": cross_mix,
        "i": cross_lse,
        "j": second_sum,
        "k": second_low,
        "l": hidden_pre,
        "m": hidden_act,
        "n": third_sum,
        "o": final,
    }


def run_backward(saved, tokens, memory, sent_seg, mem_seg, weights, cotangent):
    proj_in, proj_out, ffn_in, ffn_out, ln_gain, ln_bias = weights
    gains = ln_gain.astype(jnp.float32)
    shifts = ln_bias.astype(jnp.float32)
    _, pull_third = jax.vjp(layer_norm, saved["n"], gains[2], shifts[2])
    grad_third, gain_third, shift_third = pull_third(cotangent.astype(jnp.float32))
    third_low = grad_third.astype(jnp.bfloat16)
    grad_ffn_out = jnp.einsum(
        "tf,td->fd", saved["m"], third_low, preferred_element_type=jnp.float32
    )
    grad_act = jnp.einsum("td,fd->tf", third_low, ffn_out, preferred_element_type=jnp.float32)
    _, pull_gelu = jax.vjp(jax.nn.gelu, saved["l"])
    grad_pre = pull_gelu(grad_act)[0].astype(jnp.bfloat16)
    grad_ffn_in = jnp.einsum(
        "td,tf->df", saved["k"], grad_pre, preferred_element_type=jnp.float32
    )
    grad_second = residual_scale * grad_third + jnp.einsum(
        "tf,df->td", grad_pre, ffn_in, preferred_element_type=jnp.float32
    )
    ffn_grads = (grad_ffn_in, grad_ffn_out, gain_third, shift_third)
    _, pull_second = jax.vjp(layer_norm, saved["j"], gains[1], shifts[1])
    grad_two, gain_second, shift_second = pull_second(grad_second)
    two_low = grad_two.astype(jnp.bfloat16)
    grad_cross_out = jnp.einsum(
        "te,td->ed", saved["h"], two_low, preferred_element_type=jnp.float32
    )
    grad_cross_mix = jnp.einsum(
        "td,ed->te", two_low, proj_out[1], preferred_element_type=jnp.float32
    ).astype(jnp.bfloat16)
    grad_cq, grad_ck, grad_cv = attend_backward(
        saved["f"],
        saved["g"][0],
        saved["g"][1],
        sent_seg,
        mem_seg,
        False,
        saved["i"],
        grad_cross_mix,
    )
    grad_ckv = jnp.stack([grad_ck, grad_cv])
    grad_cross_in = jnp.concatenate(
        [
            jnp.einsum(
                "td,te->de", saved["e"], grad_cq, preferred_element_type=jnp.float32
            )[None],
            jnp.einsum("td,wte->wde", memory, grad_ckv, preferred_element_type=jnp.float32),
        ],
        axis=0,
    )
    grad_memory = jnp.einsum(
        "wte,wde->td", grad_ckv, proj_in[4:6], preferred_element_type=jnp.float32
    ).astype(jnp.bfloat16)
    grad_first = residual_scale * grad_two + jnp.einsum(
        "te,de->td", grad_cq, proj_in[3], preferred_element_type=jnp.float32
    )
    cross_grads = (grad_cross_in, grad_cross_out, gain_second, shift_second)
    _, pull_first = jax.vjp(layer_norm, saved["d"], gains[0], shifts[0])
    grad_one, gain_first, shift_first = pull_first(grad_first)
    one_low = grad_one.astype(jnp.bfloat16)
    grad_self_out = jnp.einsum(
        "te,td->ed", saved["b"], one_low, preferred_element_type=jnp.float32
    )
    grad_self_mix = jnp.einsum(
        "td,ed->te", one_low, proj_out[0], preferred_element_type=jnp.float32
    ).astype(jnp.bfloat16)
    self_qkv = saved["a"]
    grad_sq, grad_sk, grad_sv = attend_backward(
        self_qkv[0],
        self_qkv[1],
        self_qkv[2],
        sent_seg,
        sent_seg,
        True,
        saved["c"],
        grad_self_mix,
    )
    grad_sqkv = jnp.stack([grad_sq, grad_sk, grad_sv])
    grad_self_in = jnp.einsum("td,wte->wde", tokens, grad_sqkv, preferred_element_type=jnp.float32)
    grad_tokens = (
        residual_scale * grad_one
        + jnp.einsum("wte,wde->td", grad_sqkv, proj_in[0:3], preferred_element_type=jnp.float32)
    ).astype(jnp.bfloat16)
    self_grads = (grad_self_in, grad_self_out, gain_first, shift_first)
    all_in = jnp.concatenate([self_grads[0], cross_grads[0]], axis=0)
    all_out = jnp.stack([self_grads[1], cross_grads[1]])
    all_gain = jnp.stack([self_grads[2], cross_grads[2], ffn_grads[2]])
    all_bias = jnp.stack([self_grads[3], cross_grads[3], ffn_grads[3]])
    return (
        grad_tokens,
        grad_memory,
        all_in,
        all_out,
        ffn_grads[0],
        ffn_grads[1],
        all_gain,
        all_bias,
    )


MESH = pl.DeviceIdType.MESH
BOTH = ("dp", "fsdp")
f32 = jnp.float32
bf16 = jnp.bfloat16
UNITS = 17
def shard_of(unit):
    if unit < 12:
        return (32, 1024)
    return (128, 256) if unit < 16 else (16, 128)


class Place:
    def __init__(self):
        inner = lax.axis_index("fsdp")
        self.y = lax.axis_index("dp")
        self.z = inner // 4
        self.x = (inner // 2) % 2
        self.c = inner % 2

    def at(self, y=None, z=None, x=None, c=None):
        y = self.y if y is None else y
        z = self.z if z is None else z
        x = self.x if x is None else x
        c = self.c if c is None else c
        return (y, (z * 2 + x) * 2 + c)

    def over_x(self):
        return self.at(x=1 - self.x)

    def over_y(self):
        return self.at(y=1 - self.y)

    def sibling(self):
        return self.at(c=1 - self.c)

    def greet(self):
        barrier = pltpu.get_barrier_semaphore()
        friends = [self.at(z=lax.rem(self.z + k, 4)) for k in (1, 2, 3)]
        friends += [self.over_x(), self.over_y(), self.sibling()]
        for friend in friends:
            pl.semaphore_signal(barrier, inc=1, device_id=friend, device_id_type=MESH)
        pl.semaphore_wait(barrier, len(friends))


class Sender:
    def __init__(self, place, send_sem, recv_sem):
        self.p, self.send_sem, self.recv_sem = place, send_sem, recv_sem
        self.pending = {}

    def copy(self, unit, slot, src, dst, device, landing=None):
        return pltpu.make_async_remote_copy(
            src_ref=src,
            dst_ref=dst,
            send_sem=self.send_sem.at[unit, slot],
            recv_sem=self.recv_sem.at[unit, slot if landing is None else landing],
            device_id=device,
            device_id_type=MESH,
        )

    def send(self, unit, slot, src, dst, device, cond=None, landing=None):
        make = lambda: self.copy(unit, slot, src, dst, device, landing)
        if cond is None:
            make().start()
            self.pending.setdefault(unit, []).append(lambda: make().wait_send())
        else:
            pl.when(cond)(lambda: make().start())
            self.pending.setdefault(unit, []).append(
                lambda: pl.when(cond)(lambda: make().wait_send())
            )

    def wait(self, unit, slot, ref):
        self.copy(unit, slot, ref, ref, self.p.sibling()).wait_recv()

    def finish(self, unit):
        for done in self.pending.pop(unit, []):
            done()


class Gather(Sender):
    stages = (0, 0.5, 1, 1.5, 2, 3, 4)

    def __init__(self, place, send_sem, recv_sem, whole, own, kinds):
        super().__init__(place, send_sem, recv_sem)
        self.whole, self.own, self.kinds = whole, own, kinds

    def view(self, unit, y=None, z=None, x=None, c=None):
        every = slice(None)
        pick = lambda v: every if v is None else v
        return self.whole(unit).at[pick(y), pick(z), pick(x), pick(c)]

    def along_z(self, unit):
        p, kind = self.p, self.kinds[unit]
        if kind[0] == "p":
            return lambda z: self.view(unit, y=p.y, z=z, x=p.x, c=p.c)
        if kind == "rL":
            return lambda z: self.view(unit, y=p.y, z=z, c=p.c)
        return lambda z: self.view(unit, z=z, x=p.x, c=p.c)

    def z_send(self, unit):
        p, part = self.p, self.along_z(unit)
        for k in (1, 2, 3):
            there = lax.rem(p.z + k, 4)
            near = jnp.logical_not(
                ((p.z == 0) & (there == 3)) | ((p.z == 3) & (there == 0))
            )
            source = self.own(unit) if self.kinds[unit][0] == "p" else part(p.z)
            self.send(unit, there, source, part(p.z), p.at(z=there), near, landing=p.z)

    def z_relay(self, unit):
        p, part = self.p, self.along_z(unit)
        for here, source, there in ((2, 0, 3), (1, 3, 0)):
            pl.when(p.z == here)(lambda source=source: self.wait(unit, source, part(source)))
            self.send(
                unit, 8, part(source), part(source), p.at(z=there), p.z == here, landing=source
            )

    def z_wait(self, unit):
        p, part = self.p, self.along_z(unit)
        for k in (1, 2, 3):
            source = lax.rem(p.z + 4 - k, 4)
            relayed = ((p.z == 2) & (source == 0)) | ((p.z == 1) & (source == 3))
            pl.when(jnp.logical_not(relayed))(
                lambda source=source: self.wait(unit, source, part(source))
            )

    def stage(self, unit, step):
        p, kind = self.p, self.kinds[unit]
        y, z, x, c = p.y, p.z, p.x, p.c
        view = lambda **at: self.view(unit, **at)
        send = lambda slot, ref, device: self.send(unit, slot, ref, ref, device)
        if kind[0] == "p":
            if step == 0:
                self.z_send(unit)
            if step == 0.5:
                self.z_relay(unit)
            if step == 1:
                self.z_wait(unit)
                line = view(y=y, x=x, c=c)
                send(4, line, p.over_x())
                send(5, line, p.over_y())
            if step == 2:
                if kind == "pL":
                    line = view(y=y, x=1 - x, c=c)
                    self.wait(unit, 4, line)
                    send(6, line, p.over_y())
                else:
                    line = view(y=1 - y, x=x, c=c)
                    self.wait(unit, 5, line)
                    send(6, line, p.over_x())
            if step == 3:
                if kind == "pL":
                    self.wait(unit, 5, view(y=1 - y, x=x, c=c))
                else:
                    self.wait(unit, 4, view(y=y, x=1 - x, c=c))
                self.wait(unit, 6, view(y=1 - y, x=1 - x, c=c))
                send(7, view(c=c), p.sibling())
        else:
            left = kind == "rL"
            first, last = (p.over_x(), p.over_y()) if left else (p.over_y(), p.over_x())
            if step == 0:
                self.send(unit, 4, self.own(unit), view(y=y, z=z, x=x, c=c), first)
            if step == 1:
                self.wait(
                    unit,
                    4,
                    view(y=y, z=z, x=1 - x, c=c) if left else view(y=1 - y, z=z, x=x, c=c),
                )
                self.z_send(unit)
            if step == 1.5:
                self.z_relay(unit)
            if step == 2:
                self.z_wait(unit)
                send(5, view(y=y, c=c) if left else view(x=x, c=c), last)
            if step == 3:
                self.wait(unit, 5, view(y=1 - y, c=c) if left else view(x=1 - x, c=c))
                send(7, view(c=c), p.sibling())
        if step == 4:
            self.wait(unit, 7, view(c=1 - c))


class Scatter(Sender):
    stages = (0, 1, 2, 2.5, 3, 3.5, 4, 5)

    def __init__(self, place, send_sem, recv_sem, other, mine, twin, eight, four, zs, out, kinds):
        super().__init__(place, send_sem, recv_sem)
        self.other, self.mine, self.twin = other, mine, twin
        self.eight, self.four, self.zs, self.out, self.kinds = eight, four, zs, out, kinds

    def add(self, into, *terms):
        total = into[...].astype(f32)
        for term in terms:
            total = total + term[...].astype(f32)
        into[...] = total.astype(into.dtype)

    def along_z(self, unit):
        p, kind, mine = self.p, self.kinds[unit], self.mine(unit)
        if kind[0] == "p":
            return (lambda z: mine.at[p.y, z, p.x]), (lambda ref: ref.at[0])
        if kind == "rL":
            return (lambda z: mine.at[p.y, z]), (lambda ref: ref)
        return (lambda z: mine.at[:, z, p.x]), (lambda ref: ref)

    def z_send(self, unit):
        p, zs = self.p, self.zs(unit)
        part, slot = self.along_z(unit)
        for k in (1, 2, 3):
            there = lax.rem(p.z + k, 4)
            far = ((p.z == 0) & (there == 3)) | ((p.z == 3) & (there == 0))
            relayed = ((p.z == 2) & (there == 0)) | ((p.z == 1) & (there == 3))
            self.send(
                unit,
                4 + there,
                part(there),
                slot(zs.at[p.z]),
                p.at(z=there),
                jnp.logical_not(far | relayed),
                landing=4 + p.z,
            )
        self.send(unit, 8, part(3), slot(zs.at[1]), p.at(z=1), p.z == 0)
        self.send(unit, 8, part(0), slot(zs.at[2]), p.at(z=2), p.z == 3)

    def z_relay(self, unit):
        p, zs = self.p, self.zs(unit)
        part, slot = self.along_z(unit)
        for here, there in ((1, 3), (2, 0)):

            @pl.when(p.z == here)
            def _(here=here, there=there):
                self.wait(unit, 8, slot(zs.at[here]))
                self.add(part(there), slot(zs.at[here]))

            self.send(
                unit,
                4 + there,
                part(there),
                slot(zs.at[here]),
                p.at(z=there),
                p.z == here,
                landing=4 + here,
            )

    def z_sum(self, unit, store):
        p, zs = self.p, self.zs(unit)
        part, slot = self.along_z(unit)
        edge = (p.z == 0) | (p.z == 3)

        @pl.when(edge)
        def _():
            self.wait(unit, 5, slot(zs.at[1]))
            self.wait(unit, 6, slot(zs.at[2]))
            store(
                part(p.z)[...].astype(f32)
                + slot(zs.at[1])[...].astype(f32)
                + slot(zs.at[2])[...].astype(f32)
            )

        @pl.when(jnp.logical_not(edge))
        def _():
            inner = 3 - p.z
            self.wait(unit, 4, slot(zs.at[0]))
            self.wait(unit, 7, slot(zs.at[3]))
            self.wait(unit, 4 + inner, slot(zs.at[inner]))
            store(
                part(p.z)[...].astype(f32)
                + slot(zs.at[inner])[...].astype(f32)
                + slot(zs.at[0])[...].astype(f32)
                + slot(zs.at[3])[...].astype(f32)
            )

    def stage(self, unit, step):
        p, kind = self.p, self.kinds[unit]
        y, z, x = p.y, p.z, p.x
        mine, eight, four, out = self.mine(unit), self.eight(unit), self.four(unit), self.out(unit)
        send = lambda slot, src, dst, device: self.send(unit, slot, src, dst, device)
        if step == 0:
            send(0, self.other(unit), self.twin(unit), p.sibling())
        if step == 1:
            self.wait(unit, 0, self.twin(unit))
            for half in (0, 1):
                self.add(mine.at[half], self.twin(unit).at[half])
            self.finish(unit)
            if kind == "pL":
                send(1, mine.at[1 - y, :, 1 - x], eight.at[0], p.over_y())
                send(3, mine.at[1 - y, :, x], four, p.over_y())
            if kind == "pR":
                send(1, mine.at[1 - y, :, 1 - x], eight.at[0], p.over_x())
                send(3, mine.at[y, :, 1 - x], four, p.over_x())
            for half in (0, 1):
                if kind == "rL":
                    send(1 + half, mine.at[1 - y, :, half], eight.at[half], p.over_y())
                if kind == "rR":
                    send(1 + half, mine.at[half, :, 1 - x], eight.at[half], p.over_x())
        if step == 2:
            if kind[0] == "p":
                self.wait(unit, 1, eight.at[0])
                line = mine.at[y, :, 1 - x] if kind == "pL" else mine.at[1 - y, :, x]
                self.add(line, eight.at[0])
                send(2, line, eight.at[1], p.over_x() if kind == "pL" else p.over_y())
            else:
                for half in (0, 1):
                    self.wait(unit, 1 + half, eight.at[half])
                    self.add(
                        mine.at[y, :, half] if kind == "rL" else mine.at[half, :, x],
                        eight.at[half],
                    )
                self.z_send(unit)
        if step == 2.5 and kind[0] == "r":
            self.z_relay(unit)
        if step == 3:
            if kind[0] == "p":
                self.wait(unit, 3, four)
                self.wait(unit, 2, eight.at[1])
                self.add(mine.at[y, :, x], four, eight.at[1])
                self.z_send(unit)
            else:
                line = mine.at[y, z] if kind == "rL" else mine.at[:, z, x]

                def keep(value):
                    line[...] = value.astype(bf16)

                self.z_sum(unit, keep)
                if kind == "rL":
                    send(3, mine.at[y, z, 1 - x], four.at[0], p.over_x())
                else:
                    send(3, mine.at[1 - y, z, x], four.at[0], p.over_y())
        if step == 3.5 and kind[0] == "p":
            self.z_relay(unit)
        if step == 4:

            def result(value):
                out[...] = value

            if kind[0] == "p":
                self.z_sum(unit, result)
            else:
                self.wait(unit, 3, four.at[0])
                result(mine[y, z, x].astype(f32) + four[0].astype(f32))
        if step == 5:
            self.finish(unit)


def kinds_of(pattern, order):
    kinds = {}
    for place, unit in enumerate(order):
        kinds[unit] = pattern[(place // 2) % len(pattern)] + "LR"[place % 2]
    return kinds


NT = (((1,), (1,)), ((), ()))
NN = (((1,), (0,)), ((), ()))
TN = (((0,), (0,)), ((), ()))


def mm(a, b, dims=NN):
    return lax.dot_general(a, b, dims, preferred_element_type=f32)


def head_lanes(value, head):
    lane = lax.broadcasted_iota(jnp.int32, value.shape, 1)
    keep = lane < HEAD_DIM if head == 0 else lane >= HEAD_DIM
    return jnp.where(keep, value, jnp.zeros_like(value))


def key_ranges(causal):
    return ((0, 256), (0, 512)) if causal else ((0, 512), (0, 512))


def pair_lanes(pair):
    return pl.ds(pl.multiple_of(pair * 128, 128), 128)


def attend_pair(q, k, v, bias, mix, probs, pair, causal):
    lanes = pair_lanes(pair)
    keys, values_t = k[:, lanes], v[:, lanes].T
    for block, (low, high) in enumerate(key_ranges(causal)):
        rows = slice(block * 256, block * 256 + 256)
        start = sum(b - a for a, b in key_ranges(causal)[:block])
        queries = q[rows, lanes] * bf16(HEAD_DIM**-0.5)
        parts = []
        for head in (0, 1):
            scores = mm(keys[low:high], head_lanes(queries, head), NT) + bias[low:high, rows]
            powers = jnp.exp(scores - jnp.max(scores, axis=0, keepdims=True))
            total = jnp.sum(powers, axis=0, keepdims=True)
            chances = (powers * (1.0 / total)).astype(bf16)
            probs[head, start : start + high - low, :] = chances
            parts.append(mm(values_t[head * 64 : head * 64 + 64, low:high], chances))
        mix[rows, lanes] = jnp.concatenate(parts, axis=0).astype(bf16).T


def attend_pair_back(q, k, v, grad_mix, probs, grad_q, grad_k, grad_v, pair, causal):
    lanes = pair_lanes(pair)
    keys, values = k[:, lanes], v[:, lanes]
    keys_t = keys.T
    sums_k, sums_v = [], []
    for block, (low, high) in enumerate(key_ranges(causal)):
        rows = slice(block * 256, block * 256 + 256)
        start = sum(b - a for a, b in key_ranges(causal)[:block])
        queries, grads = q[rows, lanes], grad_mix[rows, lanes]
        part_k, part_v, part_q = 0.0, 0.0, []
        for head in (0, 1):
            grad_head = head_lanes(grads, head)
            low_chances = probs[head, start : start + high - low, :]
            chances = low_chances.astype(f32)
            part_v = part_v + mm(low_chances, grad_head)
            moved = mm(values[low:high], grad_head, NT)
            product = chances * moved
            inner = jnp.sum(product, axis=0, keepdims=True)
            grad_scores = (product - chances * inner).astype(bf16)
            part_k = part_k + mm(grad_scores, head_lanes(queries, head))
            part_q.append(mm(keys_t[head * 64 : head * 64 + 64, low:high], grad_scores))
        grad_q[rows, lanes] = (jnp.concatenate(part_q, axis=0) * HEAD_DIM**-0.5).astype(bf16).T
        sums_k.append(part_k)
        sums_v.append(part_v)
    for sums, out, scale in ((sums_k, grad_k, HEAD_DIM**-0.5), (sums_v, grad_v, 1.0)):
        if causal:
            out[0:256, lanes] = ((sums[0] + sums[1][0:256]) * scale).astype(bf16)
            out[256:512, lanes] = (sums[1][256:512] * scale).astype(bf16)
        else:
            out[:, lanes] = ((sums[0] + sums[1]) * scale).astype(bf16)


WHOLE_ORDER = [0, 1, 2, 16, 6, 4, 5, 3, 7, 8, 9, 10, 11, 12, 13, 14, 15]
GATHER_ORDER = [2 * u + h for u in WHOLE_ORDER for h in (0, 1) if u < 16 or h == 0]
GATHER_KINDS = kinds_of("rprrprpr", GATHER_ORDER)
GATHER_OFFSETS = {"p": (0, 2, 3, 4, 6, 9, 12), "r": (0, 2, 3, 4, 6, 9, 12)}
ALPHA = 300.0**0.25
ROWS = 32
GELU_ROOT = (2.0 / 3.141592653589793) ** 0.5
Q1, K1, V1, A1, Q2, K2, V2, A2, Y1, Y2 = range(10)


def arrange(events, pieces, had=()):
    order, have, now = [], set(had), 0.0
    events, pieces = list(events), list(pieces)
    while events or pieces:
        if events and events[0][0] <= now:
            _, run, gives, needs = events[0]
            if needs <= have:
                events.pop(0)
                order.append(run)
                have.add(gives)
                continue
        ready = next((k for k, piece in enumerate(pieces) if piece[1] <= have), None)
        if ready is not None:
            name, _, length, run = pieces.pop(ready)
            order.append(run)
            have.add(name)
            now += length
        else:
            assert events and events[0][3] <= have
            now = max(now, events[0][0])
    return order


def in_chunks(body, rows=ROWS, total=512):
    def step(k, carry):
        body(pl.ds(pl.multiple_of(k * rows, rows), rows))
        return carry

    lax.fori_loop(0, total // rows, step, 0)


def segment_at(lengths, positions):
    end, seg = jnp.int32(0), jnp.zeros_like(positions)
    for k in range(4):
        end = end + lengths[0, k]
        seg = seg + jnp.where(positions >= end, 1, 0)
    return seg


def make_bias(key_len, query_len, bias, causal):
    def body(rows):
        key_at = rows.start + lax.broadcasted_iota(jnp.int32, (ROWS, 512), 0)
        query_at = lax.broadcasted_iota(jnp.int32, (ROWS, 512), 1)
        allowed = segment_at(key_len, key_at) == segment_at(query_len, query_at)
        if causal:
            allowed = allowed & (key_at <= query_at)
        bias[rows, :] = jnp.where(allowed, 0.0, -1e30)

    in_chunks(body)


def normalize(total, rows, norm, scale):
    middle = jnp.mean(total, axis=-1, keepdims=True)
    centered = total - middle
    spread = jnp.mean(centered * centered, axis=-1, keepdims=True)
    inverse = lax.rsqrt(spread + 1e-05)
    normal = centered * inverse
    norm[rows, :] = normal
    scale[rows, :] = inverse
    return normal


def forward_kernel(
    tokens, memory, sent_len, mem_len, proj_in, proj_out, ffn_in, ffn_out, small,
    output, wide, deep, tiny, saved, saved_g, saved_dg, saved_n, saved_scale, saved_p1, saved_p2,
    affine_out,
    acts, y_full, act_g, act_dg, norms, scales, bias, probs, squares, tall, work, tiny_in, affine,
    send_sem, recv_sem, local_sem, load_sem, save_sem, probs_sem,
):
    place = Place()

    def whole(unit):
        return wide.at[unit] if unit < 12 else deep.at[unit - 12] if unit < 16 else tiny

    def own(unit):
        if unit < 6:
            return proj_in.at[unit]
        if unit < 8:
            return proj_out.at[unit - 6]
        if unit < 12:
            return ffn_in.at[:, pl.ds((unit - 8) * 1024, 1024)]
        if unit < 16:
            return ffn_out.at[:, pl.ds((unit - 12) * 256, 256)]
        return small

    def half_of(part):
        rows = 64 if 12 <= part // 2 < 16 else 16
        return pl.ds((part % 2) * rows, rows)

    gather = Gather(
        place, send_sem, recv_sem,
        lambda part: whole(part // 2).at[:, :, :, :, half_of(part)],
        lambda part: own(part // 2).at[half_of(part)],
        GATHER_KINDS,
    )
    copies = {}
    for unit in WHOLE_ORDER:
        copies[unit] = pltpu.make_async_copy(
            own(unit), whole(unit).at[place.y, place.z, place.x, place.c], local_sem.at[unit]
        )
        copies[unit].start()
    place.greet()

    use_square = [0, 1, 2, 4, 5, 6, 3, 7, 8, 9, 10, 11]
    use_tall = [12, 13, 14, 15]

    def slot_of(unit):
        if unit < 12:
            return squares.at[use_square.index(unit) % squares.shape[0]]
        return tall.at[use_tall.index(unit) % tall.shape[0]]

    def load(unit):
        return pltpu.make_async_copy(
            whole(unit) if unit < 16 else tiny,
            slot_of(unit) if unit < 16 else tiny_in,
            load_sem.at[unit],
        )

    def weight(unit):
        load(unit).wait()
        ref = slot_of(unit)
        return ref[...].reshape((1024, 1024) if unit < 12 else (4096, 256))

    saves = []

    def save(src, dst, sem):
        copy = pltpu.make_async_copy(src, dst, save_sem.at[sem])
        copy.start()
        saves.append(copy)

    def project(source, unit, act):
        acts[act] = mm(source(), weight(unit)).astype(bf16)
        save(acts.at[act], saved.at[act], act)

    def affine_rows():
        load(16).wait()
        for group in range(8):
            part = tiny_in[group // 4, group % 4].astype(f32)
            affine[:, group * 128 : group * 128 + 128] = (
                part[0, 0] + part[0, 1] + part[1, 0] + part[1, 1]
            )
        save(affine, affine_out, 20)

    prob_copies = {}

    def attend(layer, pair):
        step = layer * 8 + pair
        slot = step % probs.shape[0]
        if step - probs.shape[0] in prob_copies:
            prob_copies.pop(step - probs.shape[0]).wait()
        causal = layer == 0
        part = probs.at[slot, :, 0:768] if causal else probs.at[slot]
        base = layer * 4
        attend_pair(
            acts.at[base], acts.at[base + 1], acts.at[base + 2], bias.at[layer],
            acts.at[base + 3], part, pair, causal,
        )
        copy = pltpu.make_async_copy(
            part, (saved_p1 if causal else saved_p2).at[pair], probs_sem.at[slot]
        )
        copy.start()
        prob_copies[step] = copy
        if pair == 7:
            save(acts.at[base + 3], saved.at[base + 3], base + 3)

    def mix_out(layer, unit):
        work[...] = mm(acts[layer * 4 + 3], weight(unit))

        def body(rows):
            before = tokens[rows, :].astype(f32) if layer == 0 else y_full[0, rows, :]
            normal = normalize(
                ALPHA * before + work[rows, :], rows, norms.at[layer], scales.at[layer]
            )
            after = normal * affine[layer : layer + 1, :] + affine[3 + layer : 4 + layer, :]
            y_full[layer, rows, :] = after
            acts[Y1 + layer, rows, :] = after.astype(bf16)

        in_chunks(body)
        save(acts.at[Y1 + layer], saved.at[Y1 + layer], Y1 + layer)
        save(norms.at[layer], saved_n.at[layer], 10 + layer)
        save(scales.at[layer], saved_scale.at[layer], 13 + layer)

    def hidden(part):
        work[...] = mm(acts[Y2], weight(8 + part))

        def body(rows):
            h = work[rows, :]
            square = h * h
            bend = jnp.tanh(GELU_ROOT * h * (1.0 + 0.044715 * square))
            half = 0.5 * (1.0 + bend)
            act_g[part, rows, :] = (h * half).astype(bf16)
            slope = half + 0.5 * h * (1.0 - bend * bend) * (
                GELU_ROOT * (1.0 + 3.0 * 0.044715 * square)
            )
            act_dg[part, rows, :] = slope.astype(bf16)

        in_chunks(body)
        if part == 3:
            save(act_g, saved_g, 16)
            save(act_dg, saved_dg, 17)

    def last_out(part):
        value = weight(12 + part)
        total = mm(act_g[0], value[0:1024])
        for k in range(1, 4):
            total = total + mm(act_g[k], value[k * 1024 : k * 1024 + 1024])
        work[:, part * 256 : part * 256 + 256] = total

    def last_norm():
        def body(rows):
            normal = normalize(
                ALPHA * y_full[1, rows, :] + work[rows, :], rows, norms.at[2], scales.at[2]
            )
            after = normal * affine[2:3, :] + affine[5:6, :]
            output[rows, :] = after.astype(bf16)

        in_chunks(body)
        save(norms.at[2], saved_n.at[2], 12)
        save(scales.at[2], saved_scale.at[2], 15)

    do = functools.partial
    pieces = [
        ("bias0", set(), 1.5, do(make_bias, sent_len, sent_len, bias.at[0], True)),
        ("bias1", set(), 1.5, do(make_bias, mem_len, sent_len, bias.at[1], False)),
        ("q1", {"w0"}, 1.6, do(project, lambda: tokens[...], 0, Q1)),
        ("k1", {"w1"}, 1.6, do(project, lambda: tokens[...], 1, K1)),
        ("v1", {"w2"}, 1.6, do(project, lambda: tokens[...], 2, V1)),
        ("affine", {"w16"}, 0.3, affine_rows),
    ]
    pieces += [("A%d" % p, {"q1", "k1", "v1", "bias0"}, 2.1, do(attend, 0, p)) for p in range(8)]
    pieces += [
        ("o1", {"A7", "w6", "affine"}, 4.0, do(mix_out, 0, 6)),
        ("q2", {"w3", "o1"}, 1.6, do(project, lambda: acts[Y1], 3, Q2)),
        ("k2", {"w4"}, 1.6, do(project, lambda: memory[...], 4, K2)),
        ("v2", {"w5"}, 1.6, do(project, lambda: memory[...], 5, V2)),
    ]
    pieces += [("C%d" % p, {"q2", "k2", "v2", "bias1"}, 2.5, do(attend, 1, p)) for p in range(8)]
    pieces += [("o2", {"C7", "w7", "affine"}, 4.0, do(mix_out, 1, 7))]
    pieces += [("h%d" % k, {"w%d" % (8 + k), "o2"}, 4.0, do(hidden, k)) for k in range(4)]
    pieces += [
        ("f%d" % k, {"w%d" % (12 + k), "h0", "h1", "h2", "h3"}, 1.7, do(last_out, k))
        for k in range(4)
    ]
    pieces += [("n3", {"f0", "f1", "f2", "f3"}, 3.0, last_norm)]
    users = {0: "q1", 1: "k1", 2: "v1", 3: "q2", 4: "k2", 5: "v2", 6: "o1", 7: "o2"}
    users.update({8 + k: "h%d" % k for k in range(4)})
    users.update({12 + k: "f%d" % k for k in range(4)})

    def event(unit, step):
        if step == 1 and unit % 2 == 0:
            copies[unit // 2].wait()
        gather.stage(unit, step)

    events = []
    for turn, unit in enumerate(GATHER_ORDER):
        for step, offset in zip(Gather.stages, GATHER_OFFSETS[GATHER_KINDS[unit][0]]):
            key = turn + offset
            events.append((key * FWD_PACE, step, do(event, unit, step), (unit, step), set()))
    events.sort(key=lambda item: item[:2])
    events = [(time, run, gives, needs) for time, _, run, gives, needs in events]
    loads = []
    for unit in WHOLE_ORDER:
        needs = {(2 * unit, 4), (2 * unit + (unit < 16), 4)}
        if unit < 16:
            uses, ring = (use_square, squares) if unit < 12 else (use_tall, tall)
            before = uses.index(unit) - ring.shape[0]
            if before >= 0:
                needs.add(users[uses[before]])
        loads.append(("w%d" % unit, needs, 0.0, do(lambda unit: load(unit).start(), unit)))
    for run in arrange(events, loads + pieces):
        run()
    for unit in GATHER_ORDER:
        gather.finish(unit)
    for copy in saves + list(prob_copies.values()):
        copy.wait()


FWD_PACE = 3.0


def forward_call(tokens, memory, sent_len, mem_len, proj_in, proj_out, ffn_in, ffn_out, small):
    hbm = pl.BlockSpec(memory_space=pl.ANY)
    vmem = pl.BlockSpec(memory_space=pltpu.VMEM)
    smem = pl.BlockSpec(memory_space=pltpu.SMEM)
    shape = jax.ShapeDtypeStruct
    return pl.pallas_call(
        forward_kernel,
        out_shape=(
            shape((512, 1024), bf16),
            shape((12, 2, 4, 2, 2, 32, 1024), bf16),
            shape((4, 2, 4, 2, 2, 128, 256), bf16),
            shape((2, 4, 2, 2, 16, 128), bf16),
            shape((10, 512, 1024), bf16),
            shape((4, 512, 1024), bf16),
            shape((4, 512, 1024), bf16),
            shape((3, 512, 1024), f32),
            shape((3, 512, 1), f32),
            shape((8, 2, 768, 256), bf16),
            shape((8, 2, 1024, 256), bf16),
            shape((16, 1024), f32),
        ),
        in_specs=[vmem, vmem, smem, smem, vmem, vmem, vmem, vmem, vmem],
        out_specs=[vmem] + [hbm] * 11,
        scratch_shapes=[
            pltpu.VMEM((10, 512, 1024), bf16),
            pltpu.VMEM((2, 512, 1024), f32),
            pltpu.VMEM((4, 512, 1024), bf16),
            pltpu.VMEM((4, 512, 1024), bf16),
            pltpu.VMEM((3, 512, 1024), f32),
            pltpu.VMEM((3, 512, 1), f32),
            pltpu.VMEM((2, 512, 512), f32),
            pltpu.VMEM((2, 2, 1024, 256), bf16),
            pltpu.VMEM((3, 2, 4, 2, 2, 32, 1024), bf16),
            pltpu.VMEM((2, 2, 4, 2, 2, 128, 256), bf16),
            pltpu.VMEM((512, 1024), f32),
            pltpu.VMEM((2, 4, 2, 2, 16, 128), bf16),
            pltpu.VMEM((16, 1024), f32),
            pltpu.SemaphoreType.DMA((2 * UNITS, 9)),
            pltpu.SemaphoreType.DMA((2 * UNITS, 9)),
            pltpu.SemaphoreType.DMA((UNITS,)),
            pltpu.SemaphoreType.DMA((UNITS,)),
            pltpu.SemaphoreType.DMA((21,)),
            pltpu.SemaphoreType.DMA((2,)),
        ],
        compiler_params=pltpu.CompilerParams(
            collective_id=0, has_side_effects=True, vmem_limit_bytes=63 << 20
        ),
        cost_estimate=pl.CostEstimate(
            flops=20_000_000_000, bytes_accessed=120_000_000, transcendentals=10_000_000
        ),
    )(tokens, memory, sent_len, mem_len, proj_in, proj_out, ffn_in, ffn_out, small)


def small_rows(ln_gain, ln_bias):
    rows = jnp.concatenate([ln_gain, ln_bias, jnp.zeros((10, 32), bf16)], axis=0)
    spot = lax.axis_index("fsdp") % 4
    return jnp.concatenate(
        [jnp.where(spot == k, rows, jnp.zeros_like(rows)) for k in range(4)], axis=1
    )


GRAD_ORDER = [12, 13, 14, 15, 8, 9, 10, 11, 7, 3, 4, 5, 6, 16, 0, 1, 2]
SCATTER_ORDER = [2 * u + h for u in GRAD_ORDER for h in (0, 1) if u < 16 or h == 0]
SCATTER_KINDS = kinds_of("rpr", SCATTER_ORDER)
SCATTER_WAIT = 16.0
SCATTER_PACE = 3.6
DEPTH_OTHER, DEPTH_MINE, DEPTH_TWIN, DEPTH_REST = 4, 9, 5, 8


def arrange_back(units, stages, pieces, wait, pace, costs):
    order, have, now = [], set(), 0.0
    pieces = list(pieces)
    at = {unit: 0 for unit in units}
    ready = {unit: 0.0 for unit in units}
    last = {}
    while pieces or any(k < len(stages) for k in at.values()):
        options = []
        for place, unit in enumerate(units):
            if at[unit] == len(stages):
                continue
            stage, needs, run = stages[at[unit]](unit)
            if needs <= have:
                time = max(ready[unit], last.get(stage, -pace) + pace if stage in (0, 1, 2, 3) else 0.0)
                options.append((time, place, unit, stage, run))
        best = min(options, key=lambda item: item[:2]) if options else None
        piece = next((k for k, item in enumerate(pieces) if item[1] <= have), None)
        if best is not None and (best[0] <= now or piece is None):
            time, _, unit, stage, run = best
            now = max(now, time)
            order.append(run)
            have.add((unit, stage))
            last[stage] = now
            now += costs.get(stage, 0.0)
            ready[unit] = now + wait.get(stage, 0.0)
            at[unit] += 1
        else:
            assert piece is not None
            name, _, length, run = pieces.pop(piece)
            order.append(run)
            have.add(name)
            now += length
    return order


def backward_kernel(
    cotangent, wide, deep, affine, saved, saved_g, saved_dg, saved_n, saved_scale,
    saved_p1, saved_p2, tokens, memory,
    grad_tokens, grad_memory, out_in, out_out, out_fin, out_fout, out_tiny,
    pool, total, work, norm, scales, probs, squares, affine_grads,
    other, mine, twin, eight, four, zs,
    other_s, mine_s, twin_s, eight_s, four_s, zs_s,
    send_sem, recv_sem, credit, load_sem, act_sem, probs_sem,
):
    place = Place()
    turn = {unit: k for k, unit in enumerate([u for u in GRAD_ORDER if u != 16])}

    def slot_of(ref, tiny, unit):
        return tiny if unit == 16 else ref.at[turn[unit] % ref.shape[0]]

    def ring(ref, tiny, lead):
        def pick(part):
            slot = slot_of(ref, tiny, part // 2)
            if part // 2 == 16:
                return slot
            rows = pl.ds((part % 2) * 16, 16)
            return slot.at[:, :, :, rows] if lead == 3 else slot.at[:, :, rows] if lead == 2 else slot.at[:, rows]

        return pick

    def out(part):
        unit, rows = part // 2, pl.ds((part % 2) * 16, 16)
        if unit < 6:
            return out_in.at[unit, rows]
        if unit < 8:
            return out_out.at[unit - 6, rows]
        if unit < 12:
            return out_fin.at[rows, pl.ds((unit - 8) * 1024, 1024)]
        return out_tiny

    scatter = RingScatter(
        place, send_sem, recv_sem, ring(other, other_s, 3), ring(mine, mine_s, 3),
        ring(twin, twin_s, 3), ring(eight, eight_s, 2), ring(four, four_s, 1), ring(zs, zs_s, 2),
        out, SCATTER_KINDS, credit,
        {part: k for k, part in enumerate([p for p in SCATTER_ORDER if p != 32])},
    )
    scatter.tall = lambda unit, value: tall_out(unit, value)

    def tall_out(part, value):
        column, first = (part // 2 - 12) * 256, (part % 2) * 16
        for k in range(4):
            out_fout[k * 32 + first : k * 32 + first + 16, column : column + 256] = value[
                :, k * 256 : k * 256 + 256
            ]

    uses = [("t", 0), 8, ("t", 1), 9, ("t", 2), 10, ("t", 3), 11, 7, 3, 4, 5, 6, 0, 1, 2]

    def weight_copies(name):
        k = uses.index(name)
        slot = squares.at[k % squares.shape[0]]
        if isinstance(name, int):
            return [pltpu.make_async_copy(wide.at[name], slot, load_sem.at[k, 0])]
        rows = pl.ds(name[1] * 1024, 1024)
        return [
            pltpu.make_async_copy(
                deep.at[u, rows], slot.at[:, pl.ds(u * 256, 256)], load_sem.at[k, u]
            )
            for u in range(4)
        ]

    def load_weight(name):
        for copy in weight_copies(name):
            copy.start()

    def weight(name):
        for copy in weight_copies(name):
            copy.wait()
        return squares[uses.index(name) % squares.shape[0]]

    sources = {
        "n3": (saved_n.at[2], norm), "n2": (saved_n.at[1], norm), "n1": (saved_n.at[0], norm),
        "s": (saved_scale, scales),
        "y2": (saved.at[Y2], pool.at[7]), "y1": (saved.at[Y1], pool.at[9]),
        "m": (memory, pool.at[10]), "t": (tokens, pool.at[11]), "c": (cotangent, pool.at[6]),
        "a2": (saved.at[A2], pool.at[0]), "q2": (saved.at[Q2], pool.at[1]),
        "k2": (saved.at[K2], pool.at[2]), "v2": (saved.at[V2], pool.at[3]),
        "a1": (saved.at[A1], pool.at[0]), "q1": (saved.at[Q1], pool.at[1]),
        "k1": (saved.at[K1], pool.at[2]), "v1": (saved.at[V1], pool.at[3]),
    }
    for j in range(4):
        sources["g%d" % j] = (saved_g.at[j], pool.at[j])
        sources["dg%d" % j] = (saved_dg.at[j], pool.at[4 + j % 2])
    names = list(sources)

    def act_copy(name):
        src, dst = sources[name]
        return pltpu.make_async_copy(src, dst, act_sem.at[names.index(name)])

    arrived = set()

    def act(name):
        if name not in arrived:
            arrived.add(name)
            act_copy(name).wait()
        return sources[name][1]

    DO, DQ, DK, DV, EB = 4, 5, 6, 7, 8

    def norm_back(layer):
        grads = act("c") if layer == 2 else total
        norms = act("n%d" % (layer + 1))
        act("s")
        affine_grads[layer : layer + 1, :] = jnp.zeros((1, 1024), f32)
        affine_grads[3 + layer : 4 + layer, :] = jnp.zeros((1, 1024), f32)

        def body(rows):
            e, n = grads[rows, :].astype(f32), norms[rows, :]
            affine_grads[layer : layer + 1, :] += jnp.sum(e * n, axis=0, keepdims=True)
            affine_grads[3 + layer : 4 + layer, :] += jnp.sum(e, axis=0, keepdims=True)
            scaled = e * affine[layer : layer + 1, :]
            back = scaled - jnp.mean(scaled, axis=-1, keepdims=True)
            back = back - n * jnp.mean(scaled * n, axis=-1, keepdims=True)
            back = back * scales[layer, rows, :]
            pool[EB, rows, :] = back.astype(bf16)
            total[rows, :] = ALPHA * back

        in_chunks(body)

    def fill(unit, value):
        parts = value.astype(bf16).reshape(2, 4, 2, 2, 32, 1024)
        first = place.c == 0
        even, odd = parts[:, :, :, 0], parts[:, :, :, 1]
        slot_of(mine, mine_s, unit)[...] = jnp.where(first, even, odd)
        slot_of(other, other_s, unit)[...] = jnp.where(first, odd, even)

    def grad_tall(j):
        value = mm(act("g%d" % j)[...], pool[EB], TN).astype(bf16).reshape(2, 2, 2, 4, 32, 1024)
        first = place.c == 0
        even, odd = value[:, :, 0], value[:, :, 1]
        for ref, part in (
            (mine, jnp.where(first, even, odd)),
            (other, jnp.where(first, odd, even)),
        ):
            for u in range(4):
                for k in range(4):
                    ref[u, j // 2, 2 * (j % 2) : 2 * (j % 2) + 2, :, :, k * 256 : k * 256 + 256] = (
                        part[:, :, k, :, u * 256 : u * 256 + 256]
                    )

    def hidden_back(j):
        work[...] = mm(pool[EB], weight(("t", j)), NT)
        slope = act("dg%d" % j)

        def body(rows):
            pool[DK, rows, :] = (work[rows, :] * slope[rows, :].astype(f32)).astype(bf16)

        in_chunks(body)

    def accumulate(source, name):
        total[...] = total[...] + mm(pool[source], weight(name), NT)

    def mix_back(name):
        pool[DO] = mm(pool[EB], weight(name), NT).astype(bf16)

    def grad_matrix(unit, left, right):
        fill(unit, mm(left(), pool[right], TN))

    def grad_affine():
        value = affine_grads[...].astype(bf16)
        for group in range(8):
            for x in (0, 1):
                block = value[:, group * 128 : group * 128 + 128]
                mine_s[group // 4, group % 4, x] = block
                other_s[group // 4, group % 4, x] = block

    def probs_copy(layer, pair):
        slot = probs.at[pair % 2] if layer == 1 else probs.at[pair % 2, :, 0:768]
        src = (saved_p1 if layer == 0 else saved_p2).at[pair]
        return pltpu.make_async_copy(src, slot, probs_sem.at[layer, pair])

    def attend_back(layer, pair):
        causal = layer == 0
        for name in ("q%d", "k%d", "v%d"):
            act(name % (layer + 1))
        probs_copy(layer, pair).wait()
        attend_pair_back(
            pool.at[1], pool.at[2], pool.at[3], pool.at[DO], probs.at[pair % 2],
            pool.at[DQ], pool.at[DK], pool.at[DV], pair, causal,
        )

    def memory_back(first):
        if first:
            work[...] = mm(pool[DK], weight(4), NT)
        else:
            grad_memory[...] = (work[...] + mm(pool[DV], weight(5), NT)).astype(bf16)

    def tokens_back():
        grad_tokens[...] = (total[...] + mm(pool[DV], weight(2), NT)).astype(bf16)

    do = functools.partial
    start = lambda name: act_copy(name).start()
    order_of = [u for u in GRAD_ORDER if u != 16]

    def free(unit):
        k, needs = turn[unit], set()
        for ring_ref, step in ((mine, 5), (other, 1)):
            if k >= ring_ref.shape[0]:
                before = order_of[k - ring_ref.shape[0]]
                needs |= {(2 * before, step), (2 * before + 1, step)}
        return needs

    pieces = []

    def piece(name, needs, length, run):
        pieces.append((name, set(needs), length, run))

    def loads(name, needs=()):
        piece("L" + name, needs, 0.0, do(start, name))

    user = {("t", j): "dh%d" % j for j in range(4)}
    user.update({8 + j: "r%d" % j for j in range(4)})
    user.update({7: "o2", 3: "rq", 4: "m4", 5: "m5", 6: "o1", 0: "t0", 1: "t1", 2: "t2"})
    for name in ("n3", "s", "c", "g0", "g1", "g2", "g3", "dg0", "dg1", "y2", "m", "y1", "t"):
        loads(name)
    for k, name in enumerate(uses):
        needs = [user[uses[k - squares.shape[0]]]] if k >= squares.shape[0] else []
        piece(("W", name), needs, 0.0, do(load_weight, name))
    loads("dg2", ["dh0"])
    loads("dg3", ["dh1"])
    loads("n2", ["z3"])
    loads("n1", ["z2"])
    for k, name in enumerate(("a2", "q2", "k2", "v2")):
        loads(name, ["Gt%d" % k])
    loads("a1", ["G7"])
    for name in ("q1", "k1", "v1"):
        loads(name, ["B2_7"])
    for layer in (1, 0):
        for pair in range(8):
            if pair >= 2:
                needs = ["B%d_%d" % (layer + 1, pair - 2)]
            else:
                needs = [] if layer == 1 else ["B2_%d" % (6 + pair)]
            piece("P%d_%d" % (layer + 1, pair), needs, 0.0, lambda l=layer, p=pair: probs_copy(l, p).start())

    piece("z3", ["Ln3", "Ls", "Lc"], 2.5, do(norm_back, 2))
    for j in range(4):
        piece("Gt%d" % j, ["z3", "Lg%d" % j], 2.0, do(grad_tall, j))
    for j in range(4):
        piece("G%d" % (8 + j), ["r%d" % j, "Ly2"] + list(free(8 + j)), 2.0, do(grad_matrix, 8 + j, lambda: act("y2")[...], DK))
    piece("G7", ["z2", "La2"] + list(free(7)), 2.0, do(grad_matrix, 7, lambda: act("a2")[...], EB))
    piece("G3", ["B2_7", "Ly1"] + list(free(3)), 2.0, do(grad_matrix, 3, lambda: act("y1")[...], DQ))
    piece("G4", ["B2_7", "Lm", "G3"] + list(free(4)), 2.0, do(grad_matrix, 4, lambda: act("m")[...], DK))
    piece("G5", ["B2_7", "Lm", "G4"] + list(free(5)), 2.0, do(grad_matrix, 5, lambda: act("m")[...], DV))
    piece("G6", ["z1", "La1"] + list(free(6)), 2.0, do(grad_matrix, 6, lambda: act("a1")[...], EB))
    piece("G16", ["z1"], 0.3, grad_affine)
    for k, unit in enumerate((0, 1, 2)):
        piece("G%d" % unit, ["B1_7", "Lt"] + list(free(unit)), 2.0, do(grad_matrix, unit, lambda: act("t")[...], DQ + k))
    for j in range(4):
        needs = ["z3", "Ldg%d" % j, ("W", ("t", j))] + (["G%d" % (7 + j)] if j else [])
        piece("dh%d" % j, needs, 2.2, do(hidden_back, j))
        piece("r%d" % j, ["dh%d" % j, ("W", 8 + j)], 1.8, do(accumulate, DK, 8 + j))
    piece("z2", ["r3", "Gt0", "Gt1", "Gt2", "Gt3", "dh3", "Ln2"], 2.5, do(norm_back, 1))
    piece("o2", ["z2", ("W", 7), "dh2", "dh3"], 1.6, do(mix_back, 7))
    for pair in range(8):
        piece("B2_%d" % pair, ["B2_%d" % (pair - 1) if pair else "o2", "G11", "P2_%d" % pair, "Lq2", "Lk2", "Lv2"], 2.3, do(attend_back, 1, pair))
    piece("rq", ["B2_7", ("W", 3)], 1.8, do(accumulate, DQ, 3))
    piece("z1", ["rq", "G7", "Ln1"], 2.5, do(norm_back, 0))
    piece("m4", ["B2_7", ("W", 4)], 1.6, do(memory_back, True))
    piece("m5", ["m4", ("W", 5)], 1.8, do(memory_back, False))
    piece("o1", ["z1", "B2_7", ("W", 6)], 1.6, do(mix_back, 6))
    for pair in range(8):
        piece("B1_%d" % pair, ["B1_%d" % (pair - 1) if pair else "o1", "m5", "G3", "G4", "G5", "P1_%d" % pair, "Lq1", "Lk1", "Lv1"], 1.8, do(attend_back, 0, pair))
    piece("t0", ["B1_7", ("W", 0)], 1.8, do(accumulate, DQ, 0))
    piece("t1", ["B1_7", "t0", ("W", 1)], 1.8, do(accumulate, DK, 1))
    piece("t2", ["t1", ("W", 2)], 1.8, tokens_back)

    def stage(step):
        def at(part):
            unit, needs = part // 2, set()
            if step == 0:
                needs = {"Gt%d" % j for j in range(4)} if 12 <= unit < 16 else {"G%d" % unit}
            return step, needs | scatter.needs(part, step), do(scatter.stage, part, step)

        return at

    place.greet()
    waits = {step: SCATTER_WAIT for step in (0, 1, 2, 3)}
    waits.update({2.5: 3.0, 3.5: 3.0, 4: 1.0})
    costs = {1: 0.5, 2: 0.3, 3: 0.3, 4: 0.2}
    for run in arrange_back(
        SCATTER_ORDER, [stage(step) for step in Scatter.stages], pieces, waits, SCATTER_PACE, costs
    ):
        run()


class RingScatter(Scatter):
    def __init__(self, place, send_sem, recv_sem, other, mine, twin, eight, four, zs, out, kinds, credit, turn):
        super().__init__(place, send_sem, recv_sem, other, mine, twin, eight, four, zs, out, kinds)
        self.credit, self.turn = credit, turn
        self.count = len(turn)

    def needs(self, unit, step):
        if unit == 32 or step not in (0, 1, 4) or self.turn[unit] == 0:
            return set()
        before = next(u for u in self.turn if self.turn[u] == self.turn[unit] - 1)
        return {(before, step)}

    def give(self, slot, device):
        pl.semaphore_signal(self.credit.at[slot], inc=1, device_id=device, device_id_type=MESH)

    def stage(self, unit, step):
        p = self.p
        k = None if unit == 32 else self.turn[unit]
        if k is not None and step == 0 and k >= 2 * DEPTH_TWIN:
            pl.semaphore_wait(self.credit.at[0], 1)
        if k is not None and step == 1 and k >= 2 * DEPTH_REST:
            for slot in (1, 2):
                pl.semaphore_wait(self.credit.at[slot], 1)
            for far in (1, 2, 3):
                pl.semaphore_wait(self.credit.at[4 + lax.rem(p.z + far, 4)], 1)
        if step == 4 and 24 <= unit < 32:
            hold = self.out
            self.out = lambda u: TallOut(self.tall, u)
            super().stage(unit, step)
            self.out = hold
        else:
            super().stage(unit, step)
        if k is not None and step == 1 and k + 2 * DEPTH_TWIN < self.count:
            self.give(0, p.sibling())
        if k is not None and step == 4 and k + 2 * DEPTH_REST < self.count:
            self.give(1, p.over_x())
            self.give(2, p.over_y())
            for far in (1, 2, 3):
                self.give(4 + p.z, p.at(z=lax.rem(p.z + far, 4)))


class TallOut:
    def __init__(self, store, unit):
        self.store, self.unit = store, unit

    def __setitem__(self, _, value):
        self.store(self.unit, value)


def backward_call(cotangent, saved_all, tokens, memory):
    wide, deep, saved, saved_g, saved_dg, saved_n, saved_scale, saved_p1, saved_p2, affine = saved_all
    hbm = pl.BlockSpec(memory_space=pl.ANY)
    vmem = pl.BlockSpec(memory_space=pltpu.VMEM)
    shape = jax.ShapeDtypeStruct
    block = (32, 1024)
    tiny = (16, 128)
    return pl.pallas_call(
        backward_kernel,
        out_shape=(
            shape((512, 1024), bf16),
            shape((512, 1024), bf16),
            shape((6, 32, 1024), f32),
            shape((2, 32, 1024), f32),
            shape((32, 4096), f32),
            shape((128, 1024), f32),
            shape((16, 128), f32),
        ),
        in_specs=[hbm, hbm, hbm, vmem] + [hbm] * 9,
        out_specs=[vmem] * 7,
        scratch_shapes=[
            pltpu.VMEM((12, 512, 1024), bf16),
            pltpu.VMEM((512, 1024), f32),
            pltpu.VMEM((512, 1024), f32),
            pltpu.VMEM((512, 1024), f32),
            pltpu.VMEM((3, 512, 1), f32),
            pltpu.VMEM((2, 2, 1024, 256), bf16),
            pltpu.VMEM((2, 1024, 1024), bf16),
            pltpu.VMEM((16, 1024), f32),
            pltpu.VMEM((DEPTH_OTHER, 2, 4, 2, *block), bf16),
            pltpu.VMEM((DEPTH_MINE, 2, 4, 2, *block), bf16),
            pltpu.VMEM((DEPTH_TWIN, 2, 4, 2, *block), bf16),
            pltpu.VMEM((DEPTH_REST, 2, 4, *block), bf16),
            pltpu.VMEM((DEPTH_REST, 4, *block), bf16),
            pltpu.VMEM((DEPTH_REST, 4, 2, *block), bf16),
            pltpu.VMEM((2, 4, 2, *tiny), bf16),
            pltpu.VMEM((2, 4, 2, *tiny), bf16),
            pltpu.VMEM((2, 4, 2, *tiny), bf16),
            pltpu.VMEM((2, 4, *tiny), bf16),
            pltpu.VMEM((4, *tiny), bf16),
            pltpu.VMEM((4, 2, *tiny), bf16),
            pltpu.SemaphoreType.DMA((2 * UNITS, 9)),
            pltpu.SemaphoreType.DMA((2 * UNITS, 9)),
            pltpu.SemaphoreType.REGULAR((8,)),
            pltpu.SemaphoreType.DMA((16, 4)),
            pltpu.SemaphoreType.DMA((32,)),
            pltpu.SemaphoreType.DMA((2, 8)),
        ],
        compiler_params=pltpu.CompilerParams(
            collective_id=1, has_side_effects=True, vmem_limit_bytes=63 << 20
        ),
        cost_estimate=pl.CostEstimate(
            flops=40_000_000_000, bytes_accessed=120_000_000, transcendentals=0
        ),
    )(
        cotangent, wide.reshape(12, 1024, 1024), deep.reshape(4, 4096, 256),
        affine, saved, saved_g, saved_dg, saved_n, saved_scale, saved_p1, saved_p2, tokens, memory,
    )


def hand_over_kernel(*refs):
    count = (len(refs) - 1) // 2
    copies = [
        pltpu.make_async_copy(refs[k], refs[count + k], refs[-1].at[k]) for k in range(count)
    ]
    for copy in copies:
        copy.start()
    for copy in copies:
        copy.wait()


def hand_over(*results):
    return pl.pallas_call(
        hand_over_kernel,
        out_shape=[jax.ShapeDtypeStruct(r.shape, r.dtype) for r in results],
        in_specs=[pl.BlockSpec(memory_space=pltpu.VMEM)] * len(results),
        out_specs=[pl.BlockSpec(memory_space=pl.ANY)] * len(results),
        scratch_shapes=[pltpu.SemaphoreType.DMA((len(results),))],
        compiler_params=pltpu.CompilerParams(vmem_limit_bytes=32 << 20),
    )(*results)


def on_device(
    tokens, memory, cotangent, sent_len, mem_len, proj_in, proj_out, ffn_in, ffn_out, ln_gain, ln_bias
):
    small = small_rows(ln_gain, ln_bias)
    output, wide, deep, _, saved, g, dg, n, scale, p1, p2, affine = forward_call(
        tokens, memory, sent_len, mem_len, proj_in, proj_out, ffn_in, ffn_out, small
    )
    *results, g_small = backward_call(
        cotangent, (wide, deep, saved, g, dg, n, scale, p1, p2, affine), tokens, memory
    )
    spot = lax.axis_index("fsdp") % 4
    own = lax.dynamic_slice(g_small, (0, spot * 32), (16, 32))
    return (*hand_over(output, *results), own[0:3], own[3:6])


def on_any_mesh(
    tokens, memory, cotangent, sent_len, mem_len, proj_in, proj_out, ffn_in, ffn_out, ln_gain, ln_bias
):
    dims = (1, 1, 0, 0, 1, 1)
    shards = (proj_in, proj_out, ffn_in, ffn_out, ln_gain, ln_bias)
    weights = tuple(
        lax.all_gather(shard, BOTH, axis=dim, tiled=True) for shard, dim in zip(shards, dims)
    )
    sent_seg = segment_ids(sent_len[0], tokens.shape[0])
    mem_seg = segment_ids(mem_len[0], memory.shape[0])
    saved = run_forward(tokens, memory, sent_seg, mem_seg, weights)
    output = saved["o"].astype(bf16)
    grads = run_backward(saved, tokens, memory, sent_seg, mem_seg, weights, cotangent)
    summed = tuple(
        lax.psum_scatter(grad, BOTH, scatter_dimension=dim, tiled=True)
        for grad, dim in zip(grads[2:], dims)
    )
    return (output, *grads[:2], *summed)


def solution(mesh):
    placed = (
        P(BOTH, None),
        P(BOTH, None),
        P(BOTH, None),
        P(BOTH, None),
        P(BOTH, None),
        P(None, BOTH, None),
        P(None, BOTH, None),
        P(BOTH, None),
        P(BOTH, None),
        P(None, BOTH),
        P(None, BOTH),
    )
    routed = mesh.shape["dp"] == 2 and mesh.shape["fsdp"] == 16
    return jax.shard_map(
        on_device if routed else on_any_mesh,
        mesh=mesh,
        in_specs=placed,
        out_specs=(
            P(BOTH, None),
            P(BOTH, None),
            P(BOTH, None),
            P(None, BOTH, None),
            P(None, BOTH, None),
            P(BOTH, None),
            P(BOTH, None),
            P(None, BOTH),
            P(None, BOTH),
        ),
        check_vma=False,
    )
```

```python
import functools

import jax
import jax.numpy as jnp
from jax import lax
from jax.experimental import pallas as pl
from jax.experimental.pallas import tpu as pltpu
from jax.sharding import PartitionSpec as P

HEADS = 16
HEAD_DIM = 64


residual_scale = 300.0**0.25
masked_score = -1000000000.0


def layer_norm(summed, scale_row, shift_row):
    middle = jnp.mean(summed, axis=-1, keepdims=True)
    centered = summed - middle
    spread = jnp.mean(centered * centered, axis=-1, keepdims=True)
    return centered * lax.rsqrt(spread + 1e-05) * scale_row + shift_row


def segment_ids(lengths, seg_count):
    sent_ends = jnp.cumsum(lengths)
    positions = jnp.arange(seg_count, dtype=jnp.int32)
    return jnp.sum((positions[:, None] >= sent_ends[None, :]).astype(jnp.int32), axis=1)


def split_blocks(array, block_rows):
    return array.reshape((array.shape[0] // block_rows, block_rows) + array.shape[1:])


def block_scores(query_blk, key_heads, seg_blk, row_blk, key_seg, causal):
    scores = jnp.einsum(
        "qhd,khd->hqk", query_blk, key_heads, preferred_element_type=jnp.float32
    ) * HEAD_DIM ** (-0.5)
    allowed = seg_blk[:, None] == key_seg[None, :]
    if causal:
        allowed = allowed & (
            jnp.arange(key_seg.shape[0], dtype=jnp.int32)[None, :] <= row_blk[:, None]
        )
    return jnp.where(allowed[None], scores, masked_score)


def attend_forward(queries, key_rows, values, query_seg, key_seg, causal):
    row_count = queries.shape[0]
    block_rows = min(row_count, 512)
    key_heads = key_rows.reshape(key_rows.shape[0], HEADS, HEAD_DIM)
    value_heads = values.reshape(values.shape[0], HEADS, HEAD_DIM)
    positions = jnp.arange(row_count, dtype=jnp.int32)
    pieces = (
        split_blocks(queries.reshape(row_count, HEADS, HEAD_DIM), block_rows),
        split_blocks(query_seg, block_rows),
        split_blocks(positions, block_rows),
    )

    def one_block(piece):
        query_blk, seg_blk, row_blk = piece
        scores = block_scores(query_blk, key_heads, seg_blk, row_blk, key_seg, causal)
        peaks = jnp.max(scores, axis=-1, keepdims=True)
        powers = jnp.exp(scores - peaks)
        totals = jnp.sum(powers, axis=-1, keepdims=True)
        weights = (powers / totals).astype(jnp.bfloat16)
        mixture = jnp.einsum(
            "hqk,khd->qhd", weights, value_heads, preferred_element_type=jnp.float32
        )
        return (mixture, (peaks + jnp.log(totals))[..., 0])

    mixture, log_totals = lax.map(one_block, pieces)
    return (mixture.reshape(row_count, HEADS * HEAD_DIM).astype(jnp.bfloat16), log_totals)


def attend_backward(queries, key_rows, values, query_seg, key_seg, causal, log_totals, grad_mix):
    row_count = queries.shape[0]
    block_rows = min(row_count, 512)
    score_scale = HEAD_DIM ** (-0.5)
    key_heads = key_rows.reshape(key_rows.shape[0], HEADS, HEAD_DIM)
    value_heads = values.reshape(values.shape[0], HEADS, HEAD_DIM)
    positions = jnp.arange(row_count, dtype=jnp.int32)
    pieces = (
        split_blocks(queries.reshape(row_count, HEADS, HEAD_DIM), block_rows),
        split_blocks(query_seg, block_rows),
        split_blocks(positions, block_rows),
        log_totals,
        split_blocks(grad_mix.reshape(row_count, HEADS, HEAD_DIM), block_rows),
    )

    def one_block(carried, piece):
        grad_keys, grad_values = carried
        query_blk, seg_blk, row_blk, lse_blk, grad_blk = piece
        scores = block_scores(query_blk, key_heads, seg_blk, row_blk, key_seg, causal)
        probs = jnp.exp(scores - lse_blk[:, :, None])
        grad_values = grad_values + jnp.einsum(
            "hqk,qhd->khd", probs.astype(jnp.bfloat16), grad_blk, preferred_element_type=jnp.float32
        )
        grad_probs = jnp.einsum(
            "qhd,khd->hqk", grad_blk, value_heads, preferred_element_type=jnp.float32
        )
        inner = jnp.sum(grad_probs * probs, axis=-1, keepdims=True)
        grad_scores = (probs * (grad_probs - inner)).astype(jnp.bfloat16)
        grad_query = (
            jnp.einsum("hqk,khd->qhd", grad_scores, key_heads, preferred_element_type=jnp.float32)
            * score_scale
        )
        grad_keys = (
            grad_keys
            + jnp.einsum("hqk,qhd->khd", grad_scores, query_blk, preferred_element_type=jnp.float32)
            * score_scale
        )
        return ((grad_keys, grad_values), grad_query)

    zeros = jnp.zeros(key_heads.shape, jnp.float32)
    (grad_keys, grad_values), grad_query = lax.scan(one_block, (zeros, zeros), pieces)
    width = HEADS * HEAD_DIM
    return (
        grad_query.reshape(row_count, width).astype(jnp.bfloat16),
        grad_keys.reshape(-1, width).astype(jnp.bfloat16),
        grad_values.reshape(-1, width).astype(jnp.bfloat16),
    )


def run_forward(tokens, memory, sent_seg, mem_seg, weights):
    proj_in, proj_out, ffn_in, ffn_out, ln_gain, ln_bias = weights
    gains = ln_gain.astype(jnp.float32)
    shifts = ln_bias.astype(jnp.float32)
    self_qkv = jnp.einsum(
        "td,wde->wte", tokens, proj_in[0:3], preferred_element_type=jnp.float32
    ).astype(jnp.bfloat16)
    self_mix, self_lse = attend_forward(
        self_qkv[0], self_qkv[1], self_qkv[2], sent_seg, sent_seg, True
    )
    first_sum = residual_scale * tokens.astype(jnp.float32) + jnp.dot(
        self_mix, proj_out[0], preferred_element_type=jnp.float32
    )
    first_out = layer_norm(first_sum, gains[0], shifts[0])
    first_low = first_out.astype(jnp.bfloat16)
    cross_query = jnp.dot(first_low, proj_in[3], preferred_element_type=jnp.float32).astype(
        jnp.bfloat16
    )
    cross_kv = jnp.einsum(
        "td,wde->wte", memory, proj_in[4:6], preferred_element_type=jnp.float32
    ).astype(jnp.bfloat16)
    cross_mix, cross_lse = attend_forward(
        cross_query, cross_kv[0], cross_kv[1], sent_seg, mem_seg, False
    )
    second_sum = residual_scale * first_out + jnp.dot(
        cross_mix, proj_out[1], preferred_element_type=jnp.float32
    )
    second_out = layer_norm(second_sum, gains[1], shifts[1])
    second_low = second_out.astype(jnp.bfloat16)
    hidden_pre = jnp.dot(second_low, ffn_in, preferred_element_type=jnp.float32)
    hidden_act = jax.nn.gelu(hidden_pre).astype(jnp.bfloat16)
    third_sum = residual_scale * second_out + jnp.dot(
        hidden_act, ffn_out, preferred_element_type=jnp.float32
    )
    final = layer_norm(third_sum, gains[2], shifts[2])
    return {
        "a": self_qkv,
        "b": self_mix,
        "c": self_lse,
        "d": first_sum,
        "e": first_low,
        "f": cross_query,
        "g": cross_kv,
        "h": cross_mix,
        "i": cross_lse,
        "j": second_sum,
        "k": second_low,
        "l": hidden_pre,
        "m": hidden_act,
        "n": third_sum,
        "o": final,
    }


def run_backward(saved, tokens, memory, sent_seg, mem_seg, weights, cotangent):
    proj_in, proj_out, ffn_in, ffn_out, ln_gain, ln_bias = weights
    gains = ln_gain.astype(jnp.float32)
    shifts = ln_bias.astype(jnp.float32)
    _, pull_third = jax.vjp(layer_norm, saved["n"], gains[2], shifts[2])
    grad_third, gain_third, shift_third = pull_third(cotangent.astype(jnp.float32))
    third_low = grad_third.astype(jnp.bfloat16)
    grad_ffn_out = jnp.einsum(
        "tf,td->fd", saved["m"], third_low, preferred_element_type=jnp.float32
    )
    grad_act = jnp.einsum("td,fd->tf", third_low, ffn_out, preferred_element_type=jnp.float32)
    _, pull_gelu = jax.vjp(jax.nn.gelu, saved["l"])
    grad_pre = pull_gelu(grad_act)[0].astype(jnp.bfloat16)
    grad_ffn_in = jnp.einsum(
        "td,tf->df", saved["k"], grad_pre, preferred_element_type=jnp.float32
    )
    grad_second = residual_scale * grad_third + jnp.einsum(
        "tf,df->td", grad_pre, ffn_in, preferred_element_type=jnp.float32
    )
    ffn_grads = (grad_ffn_in, grad_ffn_out, gain_third, shift_third)
    _, pull_second = jax.vjp(layer_norm, saved["j"], gains[1], shifts[1])
    grad_two, gain_second, shift_second = pull_second(grad_second)
    two_low = grad_two.astype(jnp.bfloat16)
    grad_cross_out = jnp.einsum(
        "te,td->ed", saved["h"], two_low, preferred_element_type=jnp.float32
    )
    grad_cross_mix = jnp.einsum(
        "td,ed->te", two_low, proj_out[1], preferred_element_type=jnp.float32
    ).astype(jnp.bfloat16)
    grad_cq, grad_ck, grad_cv = attend_backward(
        saved["f"],
        saved["g"][0],
        saved["g"][1],
        sent_seg,
        mem_seg,
        False,
        saved["i"],
        grad_cross_mix,
    )
    grad_ckv = jnp.stack([grad_ck, grad_cv])
    grad_cross_in = jnp.concatenate(
        [
            jnp.einsum(
                "td,te->de", saved["e"], grad_cq, preferred_element_type=jnp.float32
            )[None],
            jnp.einsum("td,wte->wde", memory, grad_ckv, preferred_element_type=jnp.float32),
        ],
        axis=0,
    )
    grad_memory = jnp.einsum(
        "wte,wde->td", grad_ckv, proj_in[4:6], preferred_element_type=jnp.float32
    ).astype(jnp.bfloat16)
    grad_first = residual_scale * grad_two + jnp.einsum(
        "te,de->td", grad_cq, proj_in[3], preferred_element_type=jnp.float32
    )
    cross_grads = (grad_cross_in, grad_cross_out, gain_second, shift_second)
    _, pull_first = jax.vjp(layer_norm, saved["d"], gains[0], shifts[0])
    grad_one, gain_first, shift_first = pull_first(grad_first)
    one_low = grad_one.astype(jnp.bfloat16)
    grad_self_out = jnp.einsum(
        "te,td->ed", saved["b"], one_low, preferred_element_type=jnp.float32
    )
    grad_self_mix = jnp.einsum(
        "td,ed->te", one_low, proj_out[0], preferred_element_type=jnp.float32
    ).astype(jnp.bfloat16)
    self_qkv = saved["a"]
    grad_sq, grad_sk, grad_sv = attend_backward(
        self_qkv[0],
        self_qkv[1],
        self_qkv[2],
        sent_seg,
        sent_seg,
        True,
        saved["c"],
        grad_self_mix,
    )
    grad_sqkv = jnp.stack([grad_sq, grad_sk, grad_sv])
    grad_self_in = jnp.einsum("td,wte->wde", tokens, grad_sqkv, preferred_element_type=jnp.float32)
    grad_tokens = (
        residual_scale * grad_one
        + jnp.einsum("wte,wde->td", grad_sqkv, proj_in[0:3], preferred_element_type=jnp.float32)
    ).astype(jnp.bfloat16)
    self_grads = (grad_self_in, grad_self_out, gain_first, shift_first)
    all_in = jnp.concatenate([self_grads[0], cross_grads[0]], axis=0)
    all_out = jnp.stack([self_grads[1], cross_grads[1]])
    all_gain = jnp.stack([self_grads[2], cross_grads[2], ffn_grads[2]])
    all_bias = jnp.stack([self_grads[3], cross_grads[3], ffn_grads[3]])
    return (
        grad_tokens,
        grad_memory,
        all_in,
        all_out,
        ffn_grads[0],
        ffn_grads[1],
        all_gain,
        all_bias,
    )


MESH = pl.DeviceIdType.MESH
BOTH = ("dp", "fsdp")
f32 = jnp.float32
bf16 = jnp.bfloat16
UNITS = 17
def shard_of(unit):
    if unit < 12:
        return (32, 1024)
    return (128, 256) if unit < 16 else (16, 128)


class Place:
    def __init__(self):
        inner = lax.axis_index("fsdp")
        self.y = lax.axis_index("dp")
        self.z = inner // 4
        self.x = (inner // 2) % 2
        self.c = inner % 2

    def at(self, y=None, z=None, x=None, c=None):
        y = self.y if y is None else y
        z = self.z if z is None else z
        x = self.x if x is None else x
        c = self.c if c is None else c
        return (y, (z * 2 + x) * 2 + c)

    def over_x(self):
        return self.at(x=1 - self.x)

    def over_y(self):
        return self.at(y=1 - self.y)

    def sibling(self):
        return self.at(c=1 - self.c)

    def greet(self):
        barrier = pltpu.get_barrier_semaphore()
        friends = [self.at(z=lax.rem(self.z + k, 4)) for k in (1, 2, 3)]
        friends += [self.over_x(), self.over_y(), self.sibling()]
        for friend in friends:
            pl.semaphore_signal(barrier, inc=1, device_id=friend, device_id_type=MESH)
        pl.semaphore_wait(barrier, len(friends))


class Sender:
    def __init__(self, place, send_sem, recv_sem):
        self.p, self.send_sem, self.recv_sem = place, send_sem, recv_sem
        self.pending = {}

    def copy(self, unit, slot, src, dst, device, landing=None):
        return pltpu.make_async_remote_copy(
            src_ref=src,
            dst_ref=dst,
            send_sem=self.send_sem.at[unit, slot],
            recv_sem=self.recv_sem.at[unit, slot if landing is None else landing],
            device_id=device,
            device_id_type=MESH,
        )

    def send(self, unit, slot, src, dst, device, cond=None, landing=None):
        make = lambda: self.copy(unit, slot, src, dst, device, landing)
        if cond is None:
            make().start()
            self.pending.setdefault(unit, []).append(lambda: make().wait_send())
        else:
            pl.when(cond)(lambda: make().start())
            self.pending.setdefault(unit, []).append(
                lambda: pl.when(cond)(lambda: make().wait_send())
            )

    def wait(self, unit, slot, ref):
        self.copy(unit, slot, ref, ref, self.p.sibling()).wait_recv()

    def finish(self, unit):
        for done in self.pending.pop(unit, []):
            done()


class Gather(Sender):
    stages = (0, 0.5, 1, 1.5, 2, 3, 4)

    def __init__(self, place, send_sem, recv_sem, whole, own, kinds):
        super().__init__(place, send_sem, recv_sem)
        self.whole, self.own, self.kinds = whole, own, kinds

    def view(self, unit, y=None, z=None, x=None, c=None):
        every = slice(None)
        pick = lambda v: every if v is None else v
        return self.whole(unit).at[pick(y), pick(z), pick(x), pick(c)]

    def along_z(self, unit):
        p, kind = self.p, self.kinds[unit]
        if kind[0] == "p":
            return lambda z: self.view(unit, y=p.y, z=z, x=p.x, c=p.c)
        if kind == "rL":
            return lambda z: self.view(unit, y=p.y, z=z, c=p.c)
        return lambda z: self.view(unit, z=z, x=p.x, c=p.c)

    def z_send(self, unit):
        p, part = self.p, self.along_z(unit)
        for k in (1, 2, 3):
            there = lax.rem(p.z + k, 4)
            near = jnp.logical_not(
                ((p.z == 0) & (there == 3)) | ((p.z == 3) & (there == 0))
            )
            source = self.own(unit) if self.kinds[unit][0] == "p" else part(p.z)
            self.send(unit, there, source, part(p.z), p.at(z=there), near, landing=p.z)

    def z_relay(self, unit):
        p, part = self.p, self.along_z(unit)
        for here, source, there in ((2, 0, 3), (1, 3, 0)):
            pl.when(p.z == here)(lambda source=source: self.wait(unit, source, part(source)))
            self.send(
                unit, 8, part(source), part(source), p.at(z=there), p.z == here, landing=source
            )

    def z_wait(self, unit):
        p, part = self.p, self.along_z(unit)
        for k in (1, 2, 3):
            source = lax.rem(p.z + 4 - k, 4)
            relayed = ((p.z == 2) & (source == 0)) | ((p.z == 1) & (source == 3))
            pl.when(jnp.logical_not(relayed))(
                lambda source=source: self.wait(unit, source, part(source))
            )

    def stage(self, unit, step):
        p, kind = self.p, self.kinds[unit]
        y, z, x, c = p.y, p.z, p.x, p.c
        view = lambda **at: self.view(unit, **at)
        send = lambda slot, ref, device: self.send(unit, slot, ref, ref, device)
        if kind[0] == "p":
            if step == 0:
                self.z_send(unit)
            if step == 0.5:
                self.z_relay(unit)
            if step == 1:
                self.z_wait(unit)
                line = view(y=y, x=x, c=c)
                send(4, line, p.over_x())
                send(5, line, p.over_y())
            if step == 2:
                if kind == "pL":
                    line = view(y=y, x=1 - x, c=c)
                    self.wait(unit, 4, line)
                    send(6, line, p.over_y())
                else:
                    line = view(y=1 - y, x=x, c=c)
                    self.wait(unit, 5, line)
                    send(6, line, p.over_x())
            if step == 3:
                if kind == "pL":
                    self.wait(unit, 5, view(y=1 - y, x=x, c=c))
                else:
                    self.wait(unit, 4, view(y=y, x=1 - x, c=c))
                self.wait(unit, 6, view(y=1 - y, x=1 - x, c=c))
                send(7, view(c=c), p.sibling())
        else:
            left = kind == "rL"
            first, last = (p.over_x(), p.over_y()) if left else (p.over_y(), p.over_x())
            if step == 0:
                self.send(unit, 4, self.own(unit), view(y=y, z=z, x=x, c=c), first)
            if step == 1:
                self.wait(
                    unit,
                    4,
                    view(y=y, z=z, x=1 - x, c=c) if left else view(y=1 - y, z=z, x=x, c=c),
                )
                self.z_send(unit)
            if step == 1.5:
                self.z_relay(unit)
            if step == 2:
                self.z_wait(unit)
                send(5, view(y=y, c=c) if left else view(x=x, c=c), last)
            if step == 3:
                self.wait(unit, 5, view(y=1 - y, c=c) if left else view(x=1 - x, c=c))
                send(7, view(c=c), p.sibling())
        if step == 4:
            self.wait(unit, 7, view(c=1 - c))


class Scatter(Sender):
    stages = (0, 1, 2, 2.5, 3, 3.5, 4, 5)

    def __init__(self, place, send_sem, recv_sem, other, mine, twin, eight, four, zs, out, kinds):
        super().__init__(place, send_sem, recv_sem)
        self.other, self.mine, self.twin = other, mine, twin
        self.eight, self.four, self.zs, self.out, self.kinds = eight, four, zs, out, kinds

    def add(self, into, *terms):
        total = into[...].astype(f32)
        for term in terms:
            total = total + term[...].astype(f32)
        into[...] = total.astype(into.dtype)

    def along_z(self, unit):
        p, kind, mine = self.p, self.kinds[unit], self.mine(unit)
        if kind[0] == "p":
            return (lambda z: mine.at[p.y, z, p.x]), (lambda ref: ref.at[0])
        if kind == "rL":
            return (lambda z: mine.at[p.y, z]), (lambda ref: ref)
        return (lambda z: mine.at[:, z, p.x]), (lambda ref: ref)

    def z_send(self, unit):
        p, zs = self.p, self.zs(unit)
        part, slot = self.along_z(unit)
        for k in (1, 2, 3):
            there = lax.rem(p.z + k, 4)
            far = ((p.z == 0) & (there == 3)) | ((p.z == 3) & (there == 0))
            relayed = ((p.z == 2) & (there == 0)) | ((p.z == 1) & (there == 3))
            self.send(
                unit,
                4 + there,
                part(there),
                slot(zs.at[p.z]),
                p.at(z=there),
                jnp.logical_not(far | relayed),
                landing=4 + p.z,
            )
        self.send(unit, 8, part(3), slot(zs.at[1]), p.at(z=1), p.z == 0)
        self.send(unit, 8, part(0), slot(zs.at[2]), p.at(z=2), p.z == 3)

    def z_relay(self, unit):
        p, zs = self.p, self.zs(unit)
        part, slot = self.along_z(unit)
        for here, there in ((1, 3), (2, 0)):

            @pl.when(p.z == here)
            def _(here=here, there=there):
                self.wait(unit, 8, slot(zs.at[here]))
                self.add(part(there), slot(zs.at[here]))

            self.send(
                unit,
                4 + there,
                part(there),
                slot(zs.at[here]),
                p.at(z=there),
                p.z == here,
                landing=4 + here,
            )

    def z_sum(self, unit, store):
        p, zs = self.p, self.zs(unit)
        part, slot = self.along_z(unit)
        edge = (p.z == 0) | (p.z == 3)

        @pl.when(edge)
        def _():
            self.wait(unit, 5, slot(zs.at[1]))
            self.wait(unit, 6, slot(zs.at[2]))
            store(
                part(p.z)[...].astype(f32)
                + slot(zs.at[1])[...].astype(f32)
                + slot(zs.at[2])[...].astype(f32)
            )

        @pl.when(jnp.logical_not(edge))
        def _():
            inner = 3 - p.z
            self.wait(unit, 4, slot(zs.at[0]))
            self.wait(unit, 7, slot(zs.at[3]))
            self.wait(unit, 4 + inner, slot(zs.at[inner]))
            store(
                part(p.z)[...].astype(f32)
                + slot(zs.at[inner])[...].astype(f32)
                + slot(zs.at[0])[...].astype(f32)
                + slot(zs.at[3])[...].astype(f32)
            )

    def stage(self, unit, step):
        p, kind = self.p, self.kinds[unit]
        y, z, x = p.y, p.z, p.x
        mine, eight, four, out = self.mine(unit), self.eight(unit), self.four(unit), self.out(unit)
        send = lambda slot, src, dst, device: self.send(unit, slot, src, dst, device)
        if step == 0:
            send(0, self.other(unit), self.twin(unit), p.sibling())
        if step == 1:
            self.wait(unit, 0, self.twin(unit))
            for half in (0, 1):
                self.add(mine.at[half], self.twin(unit).at[half])
            self.finish(unit)
            if kind == "pL":
                send(1, mine.at[1 - y, :, 1 - x], eight.at[0], p.over_y())
                send(3, mine.at[1 - y, :, x], four, p.over_y())
            if kind == "pR":
                send(1, mine.at[1 - y, :, 1 - x], eight.at[0], p.over_x())
                send(3, mine.at[y, :, 1 - x], four, p.over_x())
            for half in (0, 1):
                if kind == "rL":
                    send(1 + half, mine.at[1 - y, :, half], eight.at[half], p.over_y())
                if kind == "rR":
                    send(1 + half, mine.at[half, :, 1 - x], eight.at[half], p.over_x())
        if step == 2:
            if kind[0] == "p":
                self.wait(unit, 1, eight.at[0])
                line = mine.at[y, :, 1 - x] if kind == "pL" else mine.at[1 - y, :, x]
                self.add(line, eight.at[0])
                send(2, line, eight.at[1], p.over_x() if kind == "pL" else p.over_y())
            else:
                for half in (0, 1):
                    self.wait(unit, 1 + half, eight.at[half])
                    self.add(
                        mine.at[y, :, half] if kind == "rL" else mine.at[half, :, x],
                        eight.at[half],
                    )
                self.z_send(unit)
        if step == 2.5 and kind[0] == "r":
            self.z_relay(unit)
        if step == 3:
            if kind[0] == "p":
                self.wait(unit, 3, four)
                self.wait(unit, 2, eight.at[1])
                self.add(mine.at[y, :, x], four, eight.at[1])
                self.z_send(unit)
            else:
                line = mine.at[y, z] if kind == "rL" else mine.at[:, z, x]

                def keep(value):
                    line[...] = value.astype(bf16)

                self.z_sum(unit, keep)
                if kind == "rL":
                    send(3, mine.at[y, z, 1 - x], four.at[0], p.over_x())
                else:
                    send(3, mine.at[1 - y, z, x], four.at[0], p.over_y())
        if step == 3.5 and kind[0] == "p":
            self.z_relay(unit)
        if step == 4:

            def result(value):
                out[...] = value

            if kind[0] == "p":
                self.z_sum(unit, result)
            else:
                self.wait(unit, 3, four.at[0])
                result(mine[y, z, x].astype(f32) + four[0].astype(f32))
        if step == 5:
            self.finish(unit)


def kinds_of(pattern, order):
    kinds = {}
    for place, unit in enumerate(order):
        kinds[unit] = pattern[(place // 2) % len(pattern)] + "LR"[place % 2]
    return kinds


NT = (((1,), (1,)), ((), ()))
NN = (((1,), (0,)), ((), ()))
TN = (((0,), (0,)), ((), ()))


def mm(a, b, dims=NN):
    return lax.dot_general(a, b, dims, preferred_element_type=f32)


def head_lanes(value, head):
    lane = lax.broadcasted_iota(jnp.int32, value.shape, 1)
    keep = lane < HEAD_DIM if head == 0 else lane >= HEAD_DIM
    return jnp.where(keep, value, jnp.zeros_like(value))


def key_ranges(causal):
    return ((0, 256), (0, 512)) if causal else ((0, 512), (0, 512))


def pair_lanes(pair):
    return pl.ds(pl.multiple_of(pair * 128, 128), 128)


def attend_pair(q, k, v, bias, mix, probs, pair, causal):
    lanes = pair_lanes(pair)
    keys, values_t = k[:, lanes], v[:, lanes].T
    for block, (low, high) in enumerate(key_ranges(causal)):
        rows = slice(block * 256, block * 256 + 256)
        start = sum(b - a for a, b in key_ranges(causal)[:block])
        queries = q[rows, lanes] * bf16(HEAD_DIM**-0.5)
        parts = []
        for head in (0, 1):
            scores = mm(keys[low:high], head_lanes(queries, head), NT) + bias[low:high, rows]
            powers = jnp.exp(scores - jnp.max(scores, axis=0, keepdims=True))
            total = jnp.sum(powers, axis=0, keepdims=True)
            chances = (powers * (1.0 / total)).astype(bf16)
            probs[head, start : start + high - low, :] = chances
            parts.append(mm(values_t[head * 64 : head * 64 + 64, low:high], chances))
        mix[rows, lanes] = jnp.concatenate(parts, axis=0).astype(bf16).T


def attend_pair_back(q, k, v, grad_mix, probs, grad_q, grad_k, grad_v, pair, causal):
    lanes = pair_lanes(pair)
    keys, values = k[:, lanes], v[:, lanes]
    keys_t = keys.T
    sums_k, sums_v = [], []
    for block, (low, high) in enumerate(key_ranges(causal)):
        rows = slice(block * 256, block * 256 + 256)
        start = sum(b - a for a, b in key_ranges(causal)[:block])
        queries, grads = q[rows, lanes], grad_mix[rows, lanes]
        part_k, part_v, part_q = 0.0, 0.0, []
        for head in (0, 1):
            grad_head = head_lanes(grads, head)
            low_chances = probs[head, start : start + high - low, :]
            chances = low_chances.astype(f32)
            part_v = part_v + mm(low_chances, grad_head)
            moved = mm(values[low:high], grad_head, NT)
            product = chances * moved
            inner = jnp.sum(product, axis=0, keepdims=True)
            grad_scores = (product - chances * inner).astype(bf16)
            part_k = part_k + mm(grad_scores, head_lanes(queries, head))
            part_q.append(mm(keys_t[head * 64 : head * 64 + 64, low:high], grad_scores))
        grad_q[rows, lanes] = (jnp.concatenate(part_q, axis=0) * HEAD_DIM**-0.5).astype(bf16).T
        sums_k.append(part_k)
        sums_v.append(part_v)
    for sums, out, scale in ((sums_k, grad_k, HEAD_DIM**-0.5), (sums_v, grad_v, 1.0)):
        if causal:
            out[0:256, lanes] = ((sums[0] + sums[1][0:256]) * scale).astype(bf16)
            out[256:512, lanes] = (sums[1][256:512] * scale).astype(bf16)
        else:
            out[:, lanes] = ((sums[0] + sums[1]) * scale).astype(bf16)


WHOLE_ORDER = [0, 1, 2, 16, 6, 4, 5, 3, 7, 8, 9, 10, 11, 12, 13, 14, 15]
GATHER_ORDER = [2 * u + h for u in WHOLE_ORDER for h in (0, 1) if u < 16 or h == 0]
GATHER_KINDS = kinds_of("rprrprpr", GATHER_ORDER)
GATHER_OFFSETS = {"p": (0, 2, 3, 4, 6, 9, 12), "r": (0, 2, 3, 4, 6, 9, 12)}
ALPHA = 300.0**0.25
ROWS = 32
GELU_ROOT = (2.0 / 3.141592653589793) ** 0.5
Q1, K1, V1, A1, Q2, K2, V2, A2, Y1, Y2 = range(10)


def arrange(events, pieces, had=()):
    order, have, now = [], set(had), 0.0
    events, pieces = list(events), list(pieces)
    while events or pieces:
        if events and events[0][0] <= now:
            _, run, gives, needs = events[0]
            if needs <= have:
                events.pop(0)
                order.append(run)
                have.add(gives)
                continue
        ready = next((k for k, piece in enumerate(pieces) if piece[1] <= have), None)
        if ready is not None:
            name, _, length, run = pieces.pop(ready)
            order.append(run)
            have.add(name)
            now += length
        else:
            assert events and events[0][3] <= have
            now = max(now, events[0][0])
    return order


def in_chunks(body, rows=ROWS, total=512):
    def step(k, carry):
        body(pl.ds(pl.multiple_of(k * rows, rows), rows))
        return carry

    lax.fori_loop(0, total // rows, step, 0)


def segment_at(lengths, positions):
    end, seg = jnp.int32(0), jnp.zeros_like(positions)
    for k in range(4):
        end = end + lengths[0, k]
        seg = seg + jnp.where(positions >= end, 1, 0)
    return seg


def make_bias(key_len, query_len, bias, causal):
    def body(rows):
        key_at = rows.start + lax.broadcasted_iota(jnp.int32, (ROWS, 512), 0)
        query_at = lax.broadcasted_iota(jnp.int32, (ROWS, 512), 1)
        allowed = segment_at(key_len, key_at) == segment_at(query_len, query_at)
        if causal:
            allowed = allowed & (key_at <= query_at)
        bias[rows, :] = jnp.where(allowed, 0.0, -1e30)

    in_chunks(body)


def normalize(total, rows, norm, scale):
    middle = jnp.mean(total, axis=-1, keepdims=True)
    centered = total - middle
    spread = jnp.mean(centered * centered, axis=-1, keepdims=True)
    inverse = lax.rsqrt(spread + 1e-05)
    normal = centered * inverse
    norm[rows, :] = normal
    scale[rows, :] = inverse
    return normal


def forward_kernel(
    tokens_from, memory_from, sent_len, mem_len, proj_in, proj_out, ffn_in, ffn_out, small,
    output, wide, deep, tiny, saved, saved_g, saved_dg, saved_n, saved_scale, saved_p1, saved_p2,
    affine_out,
    acts, y_full, act_g, act_dg, norms, scales, bias, probs, squares, tall, work, tiny_in, affine,
    inputs, send_sem, recv_sem, local_sem, load_sem, save_sem, probs_sem, input_sem,
):
    place = Place()
    tokens, memory = inputs.at[0], inputs.at[1]

    def whole(unit):
        return wide.at[unit] if unit < 12 else deep.at[unit - 12] if unit < 16 else tiny

    def own(unit):
        if unit < 6:
            return proj_in.at[unit]
        if unit < 8:
            return proj_out.at[unit - 6]
        if unit < 12:
            return ffn_in.at[:, pl.ds((unit - 8) * 1024, 1024)]
        if unit < 16:
            return ffn_out.at[:, pl.ds((unit - 12) * 256, 256)]
        return small

    def half_of(part):
        rows = 64 if 12 <= part // 2 < 16 else 16
        return pl.ds((part % 2) * rows, rows)

    gather = Gather(
        place, send_sem, recv_sem,
        lambda part: whole(part // 2).at[:, :, :, :, half_of(part)],
        lambda part: own(part // 2).at[half_of(part)],
        GATHER_KINDS,
    )
    copies = {}
    for unit in WHOLE_ORDER:
        copies[unit] = pltpu.make_async_copy(
            own(unit), whole(unit).at[place.y, place.z, place.x, place.c], local_sem.at[unit]
        )
        copies[unit].start()
    place.greet()
    reads = [
        pltpu.make_async_copy(source, inputs.at[k], input_sem.at[k])
        for k, source in enumerate((tokens_from, memory_from))
    ]
    for copy in reads:
        copy.start()

    use_square = [0, 1, 2, 4, 5, 6, 3, 7, 8, 9, 10, 11]
    use_tall = [12, 13, 14, 15]

    def slot_of(unit):
        if unit < 12:
            return squares.at[use_square.index(unit) % squares.shape[0]]
        return tall.at[use_tall.index(unit) % tall.shape[0]]

    def load(unit):
        return pltpu.make_async_copy(
            whole(unit) if unit < 16 else tiny,
            slot_of(unit) if unit < 16 else tiny_in,
            load_sem.at[unit],
        )

    def weight(unit):
        load(unit).wait()
        ref = slot_of(unit)
        return ref[...].reshape((1024, 1024) if unit < 12 else (4096, 256))

    saves = []

    def save(src, dst, sem):
        copy = pltpu.make_async_copy(src, dst, save_sem.at[sem])
        copy.start()
        saves.append(copy)

    def project(source, unit, act):
        acts[act] = mm(source(), weight(unit)).astype(bf16)
        save(acts.at[act], saved.at[act], act)

    def affine_rows():
        load(16).wait()
        for group in range(8):
            part = tiny_in[group // 4, group % 4].astype(f32)
            affine[:, group * 128 : group * 128 + 128] = (
                part[0, 0] + part[0, 1] + part[1, 0] + part[1, 1]
            )
        save(affine, affine_out, 20)

    prob_copies = {}

    def attend(layer, pair):
        step = layer * 8 + pair
        slot = step % probs.shape[0]
        if step - probs.shape[0] in prob_copies:
            prob_copies.pop(step - probs.shape[0]).wait()
        causal = layer == 0
        part = probs.at[slot, :, 0:768] if causal else probs.at[slot]
        base = layer * 4
        attend_pair(
            acts.at[base], acts.at[base + 1], acts.at[base + 2], bias.at[layer],
            acts.at[base + 3], part, pair, causal,
        )
        copy = pltpu.make_async_copy(
            part, (saved_p1 if causal else saved_p2).at[pair], probs_sem.at[slot]
        )
        copy.start()
        prob_copies[step] = copy
        if pair == 7:
            save(acts.at[base + 3], saved.at[base + 3], base + 3)

    def mix_out(layer, unit):
        work[...] = mm(acts[layer * 4 + 3], weight(unit))

        def body(rows):
            before = tokens[rows, :].astype(f32) if layer == 0 else y_full[0, rows, :]
            normal = normalize(
                ALPHA * before + work[rows, :], rows, norms.at[layer], scales.at[layer]
            )
            after = normal * affine[layer : layer + 1, :] + affine[3 + layer : 4 + layer, :]
            y_full[layer, rows, :] = after
            acts[Y1 + layer, rows, :] = after.astype(bf16)

        in_chunks(body)
        save(acts.at[Y1 + layer], saved.at[Y1 + layer], Y1 + layer)
        save(norms.at[layer], saved_n.at[layer], 10 + layer)
        save(scales.at[layer], saved_scale.at[layer], 13 + layer)

    def hidden(part):
        work[...] = mm(acts[Y2], weight(8 + part))

        def body(rows):
            h = work[rows, :]
            square = h * h
            bend = jnp.tanh(GELU_ROOT * h * (1.0 + 0.044715 * square))
            half = 0.5 * (1.0 + bend)
            act_g[part, rows, :] = (h * half).astype(bf16)
            slope = half + 0.5 * h * (1.0 - bend * bend) * (
                GELU_ROOT * (1.0 + 3.0 * 0.044715 * square)
            )
            act_dg[part, rows, :] = slope.astype(bf16)

        in_chunks(body)
        if part == 3:
            save(act_g, saved_g, 16)
            save(act_dg, saved_dg, 17)

    def last_out(part):
        value = weight(12 + part)
        total = mm(act_g[0], value[0:1024])
        for k in range(1, 4):
            total = total + mm(act_g[k], value[k * 1024 : k * 1024 + 1024])
        work[:, part * 256 : part * 256 + 256] = total

    def last_norm():
        def body(rows):
            normal = normalize(
                ALPHA * y_full[1, rows, :] + work[rows, :], rows, norms.at[2], scales.at[2]
            )
            after = normal * affine[2:3, :] + affine[5:6, :]
            output[rows, :] = after.astype(bf16)

        in_chunks(body)
        save(norms.at[2], saved_n.at[2], 12)
        save(scales.at[2], saved_scale.at[2], 15)

    do = functools.partial
    pieces = [
        ("bias0", set(), 1.5, do(make_bias, sent_len, sent_len, bias.at[0], True)),
        ("bias1", set(), 1.5, do(make_bias, mem_len, sent_len, bias.at[1], False)),
        ("x", set(), 0.1, reads[0].wait),
        ("m", set(), 0.1, reads[1].wait),
        ("q1", {"w0", "x"}, 1.6, do(project, lambda: tokens[...], 0, Q1)),
        ("k1", {"w1", "x"}, 1.6, do(project, lambda: tokens[...], 1, K1)),
        ("v1", {"w2", "x"}, 1.6, do(project, lambda: tokens[...], 2, V1)),
        ("affine", {"w16"}, 0.3, affine_rows),
    ]
    pieces += [("A%d" % p, {"q1", "k1", "v1", "bias0"}, 2.1, do(attend, 0, p)) for p in range(8)]
    pieces += [
        ("o1", {"A7", "w6", "affine"}, 4.0, do(mix_out, 0, 6)),
        ("q2", {"w3", "o1"}, 1.6, do(project, lambda: acts[Y1], 3, Q2)),
        ("k2", {"w4", "m"}, 1.6, do(project, lambda: memory[...], 4, K2)),
        ("v2", {"w5", "m"}, 1.6, do(project, lambda: memory[...], 5, V2)),
    ]
    pieces += [("C%d" % p, {"q2", "k2", "v2", "bias1"}, 2.5, do(attend, 1, p)) for p in range(8)]
    pieces += [("o2", {"C7", "w7", "affine"}, 4.0, do(mix_out, 1, 7))]
    pieces += [("h%d" % k, {"w%d" % (8 + k), "o2"}, 4.0, do(hidden, k)) for k in range(4)]
    pieces += [
        ("f%d" % k, {"w%d" % (12 + k), "h0", "h1", "h2", "h3"}, 1.7, do(last_out, k))
        for k in range(4)
    ]
    pieces += [("n3", {"f0", "f1", "f2", "f3"}, 3.0, last_norm)]
    users = {0: "q1", 1: "k1", 2: "v1", 3: "q2", 4: "k2", 5: "v2", 6: "o1", 7: "o2"}
    users.update({8 + k: "h%d" % k for k in range(4)})
    users.update({12 + k: "f%d" % k for k in range(4)})

    def event(unit, step):
        if step == 1 and unit % 2 == 0:
            copies[unit // 2].wait()
        gather.stage(unit, step)

    events = []
    for turn, unit in enumerate(GATHER_ORDER):
        for step, offset in zip(Gather.stages, GATHER_OFFSETS[GATHER_KINDS[unit][0]]):
            key = turn + offset
            events.append((key * FWD_PACE, step, do(event, unit, step), (unit, step), set()))
    events.sort(key=lambda item: item[:2])
    events = [(time, run, gives, needs) for time, _, run, gives, needs in events]
    loads = []
    for unit in WHOLE_ORDER:
        needs = {(2 * unit, 4), (2 * unit + (unit < 16), 4)}
        if unit < 16:
            uses, ring = (use_square, squares) if unit < 12 else (use_tall, tall)
            before = uses.index(unit) - ring.shape[0]
            if before >= 0:
                needs.add(users[uses[before]])
        loads.append(("w%d" % unit, needs, 0.0, do(lambda unit: load(unit).start(), unit)))
    for run in arrange(events, loads + pieces):
        run()
    for unit in GATHER_ORDER:
        gather.finish(unit)
    for copy in saves + list(prob_copies.values()):
        copy.wait()


FWD_PACE = 3.0


def forward_call(tokens, memory, sent_len, mem_len, proj_in, proj_out, ffn_in, ffn_out, small):
    hbm = pl.BlockSpec(memory_space=pl.ANY)
    vmem = pl.BlockSpec(memory_space=pltpu.VMEM)
    smem = pl.BlockSpec(memory_space=pltpu.SMEM)
    shape = jax.ShapeDtypeStruct
    return pl.pallas_call(
        forward_kernel,
        out_shape=(
            shape((512, 1024), bf16),
            shape((12, 2, 4, 2, 2, 32, 1024), bf16),
            shape((4, 2, 4, 2, 2, 128, 256), bf16),
            shape((2, 4, 2, 2, 16, 128), bf16),
            shape((10, 512, 1024), bf16),
            shape((4, 512, 1024), bf16),
            shape((4, 512, 1024), bf16),
            shape((3, 512, 1024), f32),
            shape((3, 512, 1), f32),
            shape((8, 2, 768, 256), bf16),
            shape((8, 2, 1024, 256), bf16),
            shape((16, 1024), f32),
        ),
        in_specs=[hbm, hbm, smem, smem, vmem, vmem, vmem, vmem, vmem],
        out_specs=[vmem] + [hbm] * 11,
        scratch_shapes=[
            pltpu.VMEM((10, 512, 1024), bf16),
            pltpu.VMEM((2, 512, 1024), f32),
            pltpu.VMEM((4, 512, 1024), bf16),
            pltpu.VMEM((4, 512, 1024), bf16),
            pltpu.VMEM((3, 512, 1024), f32),
            pltpu.VMEM((3, 512, 1), f32),
            pltpu.VMEM((2, 512, 512), f32),
            pltpu.VMEM((2, 2, 1024, 256), bf16),
            pltpu.VMEM((3, 2, 4, 2, 2, 32, 1024), bf16),
            pltpu.VMEM((2, 2, 4, 2, 2, 128, 256), bf16),
            pltpu.VMEM((512, 1024), f32),
            pltpu.VMEM((2, 4, 2, 2, 16, 128), bf16),
            pltpu.VMEM((16, 1024), f32),
            pltpu.VMEM((2, 512, 1024), bf16),
            pltpu.SemaphoreType.DMA((2 * UNITS, 9)),
            pltpu.SemaphoreType.DMA((2 * UNITS, 9)),
            pltpu.SemaphoreType.DMA((UNITS,)),
            pltpu.SemaphoreType.DMA((UNITS,)),
            pltpu.SemaphoreType.DMA((21,)),
            pltpu.SemaphoreType.DMA((2,)),
            pltpu.SemaphoreType.DMA((2,)),
        ],
        compiler_params=pltpu.CompilerParams(
            collective_id=0, has_side_effects=True, vmem_limit_bytes=63 << 20
        ),
        cost_estimate=pl.CostEstimate(
            flops=20_000_000_000, bytes_accessed=120_000_000, transcendentals=10_000_000
        ),
    )(tokens, memory, sent_len, mem_len, proj_in, proj_out, ffn_in, ffn_out, small)


def small_rows(ln_gain, ln_bias):
    rows = jnp.concatenate([ln_gain, ln_bias, jnp.zeros((10, 32), bf16)], axis=0)
    spot = lax.axis_index("fsdp") % 4
    return jnp.concatenate(
        [jnp.where(spot == k, rows, jnp.zeros_like(rows)) for k in range(4)], axis=1
    )


GRAD_ORDER = [12, 13, 14, 15, 8, 9, 10, 11, 7, 3, 4, 5, 6, 16, 0, 1, 2]
SCATTER_ORDER = [2 * u + h for u in GRAD_ORDER for h in (0, 1) if u < 16 or h == 0]
SCATTER_KINDS = kinds_of("rpr", SCATTER_ORDER)
SCATTER_WAIT = 16.0
SCATTER_PACE = 3.6
DEPTH_OTHER, DEPTH_MINE, DEPTH_TWIN, DEPTH_REST = 4, 9, 5, 8


def arrange_back(units, stages, pieces, wait, pace, costs):
    order, have, now = [], set(), 0.0
    pieces = list(pieces)
    at = {unit: 0 for unit in units}
    ready = {unit: 0.0 for unit in units}
    last = {}
    while pieces or any(k < len(stages) for k in at.values()):
        options = []
        for place, unit in enumerate(units):
            if at[unit] == len(stages):
                continue
            stage, needs, run = stages[at[unit]](unit)
            if needs <= have:
                time = max(ready[unit], last.get(stage, -pace) + pace if stage in (0, 1, 2, 3) else 0.0)
                options.append((time, place, unit, stage, run))
        best = min(options, key=lambda item: item[:2]) if options else None
        piece = next((k for k, item in enumerate(pieces) if item[1] <= have), None)
        if best is not None and (best[0] <= now or piece is None):
            time, _, unit, stage, run = best
            now = max(now, time)
            order.append(run)
            have.add((unit, stage))
            last[stage] = now
            now += costs.get(stage, 0.0)
            ready[unit] = now + wait.get(stage, 0.0)
            at[unit] += 1
        else:
            assert piece is not None
            name, _, length, run = pieces.pop(piece)
            order.append(run)
            have.add(name)
            now += length
    return order


def backward_kernel(
    cotangent, wide, deep, affine, saved, saved_g, saved_dg, saved_n, saved_scale,
    saved_p1, saved_p2, tokens, memory,
    grad_tokens, grad_memory, out_in, out_out, out_fin, out_fout, out_tiny,
    pool, total, work, norm, scales, probs, squares, affine_grads,
    other, mine, twin, eight, four, zs,
    other_s, mine_s, twin_s, eight_s, four_s, zs_s,
    send_sem, recv_sem, credit, load_sem, act_sem, probs_sem,
):
    place = Place()
    turn = {unit: k for k, unit in enumerate([u for u in GRAD_ORDER if u != 16])}

    def slot_of(ref, tiny, unit):
        return tiny if unit == 16 else ref.at[turn[unit] % ref.shape[0]]

    def ring(ref, tiny, lead):
        def pick(part):
            slot = slot_of(ref, tiny, part // 2)
            if part // 2 == 16:
                return slot
            rows = pl.ds((part % 2) * 16, 16)
            return slot.at[:, :, :, rows] if lead == 3 else slot.at[:, :, rows] if lead == 2 else slot.at[:, rows]

        return pick

    def out(part):
        unit, rows = part // 2, pl.ds((part % 2) * 16, 16)
        if unit < 6:
            return out_in.at[unit, rows]
        if unit < 8:
            return out_out.at[unit - 6, rows]
        if unit < 12:
            return out_fin.at[rows, pl.ds((unit - 8) * 1024, 1024)]
        return out_tiny

    scatter = RingScatter(
        place, send_sem, recv_sem, ring(other, other_s, 3), ring(mine, mine_s, 3),
        ring(twin, twin_s, 3), ring(eight, eight_s, 2), ring(four, four_s, 1), ring(zs, zs_s, 2),
        out, SCATTER_KINDS, credit,
        {part: k for k, part in enumerate([p for p in SCATTER_ORDER if p != 32])},
    )
    scatter.tall = lambda unit, value: tall_out(unit, value)

    def tall_out(part, value):
        column, first = (part // 2 - 12) * 256, (part % 2) * 16
        for k in range(4):
            out_fout[k * 32 + first : k * 32 + first + 16, column : column + 256] = value[
                :, k * 256 : k * 256 + 256
            ]

    uses = [("t", 0), 8, ("t", 1), 9, ("t", 2), 10, ("t", 3), 11, 7, 3, 4, 5, 6, 0, 1, 2]

    def weight_copies(name):
        k = uses.index(name)
        slot = squares.at[k % squares.shape[0]]
        if isinstance(name, int):
            return [pltpu.make_async_copy(wide.at[name], slot, load_sem.at[k, 0])]
        rows = pl.ds(name[1] * 1024, 1024)
        return [
            pltpu.make_async_copy(
                deep.at[u, rows], slot.at[:, pl.ds(u * 256, 256)], load_sem.at[k, u]
            )
            for u in range(4)
        ]

    def load_weight(name):
        for copy in weight_copies(name):
            copy.start()

    def weight(name):
        for copy in weight_copies(name):
            copy.wait()
        return squares[uses.index(name) % squares.shape[0]]

    sources = {
        "n3": (saved_n.at[2], norm), "n2": (saved_n.at[1], norm), "n1": (saved_n.at[0], norm),
        "s": (saved_scale, scales),
        "y2": (saved.at[Y2], pool.at[7]), "y1": (saved.at[Y1], pool.at[9]),
        "m": (memory, pool.at[10]), "t": (tokens, pool.at[11]), "c": (cotangent, pool.at[6]),
        "a2": (saved.at[A2], pool.at[0]), "q2": (saved.at[Q2], pool.at[1]),
        "k2": (saved.at[K2], pool.at[2]), "v2": (saved.at[V2], pool.at[3]),
        "a1": (saved.at[A1], pool.at[0]), "q1": (saved.at[Q1], pool.at[1]),
        "k1": (saved.at[K1], pool.at[2]), "v1": (saved.at[V1], pool.at[3]),
    }
    for j in range(4):
        sources["g%d" % j] = (saved_g.at[j], pool.at[j])
        sources["dg%d" % j] = (saved_dg.at[j], pool.at[4 + j % 2])
    names = list(sources)

    def act_copy(name):
        src, dst = sources[name]
        return pltpu.make_async_copy(src, dst, act_sem.at[names.index(name)])

    arrived = set()

    def act(name):
        if name not in arrived:
            arrived.add(name)
            act_copy(name).wait()
        return sources[name][1]

    DO, DQ, DK, DV, EB = 4, 5, 6, 7, 8

    def norm_back(layer):
        grads = act("c") if layer == 2 else total
        norms = act("n%d" % (layer + 1))
        act("s")
        affine_grads[layer : layer + 1, :] = jnp.zeros((1, 1024), f32)
        affine_grads[3 + layer : 4 + layer, :] = jnp.zeros((1, 1024), f32)

        def body(rows):
            e, n = grads[rows, :].astype(f32), norms[rows, :]
            affine_grads[layer : layer + 1, :] += jnp.sum(e * n, axis=0, keepdims=True)
            affine_grads[3 + layer : 4 + layer, :] += jnp.sum(e, axis=0, keepdims=True)
            scaled = e * affine[layer : layer + 1, :]
            back = scaled - jnp.mean(scaled, axis=-1, keepdims=True)
            back = back - n * jnp.mean(scaled * n, axis=-1, keepdims=True)
            back = back * scales[layer, rows, :]
            pool[EB, rows, :] = back.astype(bf16)
            total[rows, :] = ALPHA * back

        in_chunks(body)

    def fill(unit, value):
        parts = value.astype(bf16).reshape(2, 4, 2, 2, 32, 1024)
        first = place.c == 0
        even, odd = parts[:, :, :, 0], parts[:, :, :, 1]
        slot_of(mine, mine_s, unit)[...] = jnp.where(first, even, odd)
        slot_of(other, other_s, unit)[...] = jnp.where(first, odd, even)

    def grad_tall(j, first_unit, last_unit):
        columns = slice(first_unit * 256, last_unit * 256)
        value = mm(act("g%d" % j)[...], pool[EB, :, columns], TN).astype(bf16)
        value = value.reshape(2, 2, 2, 4, 32, columns.stop - columns.start)
        first = place.c == 0
        even, odd = value[:, :, 0], value[:, :, 1]
        for ref, part in (
            (mine, jnp.where(first, even, odd)),
            (other, jnp.where(first, odd, even)),
        ):
            for u in range(first_unit, last_unit):
                at = (u - first_unit) * 256
                for k in range(4):
                    ref[u, j // 2, 2 * (j % 2) : 2 * (j % 2) + 2, :, :, k * 256 : k * 256 + 256] = (
                        part[:, :, k, :, at : at + 256]
                    )

    def hidden_back(j):
        work[...] = mm(pool[EB], weight(("t", j)), NT)
        slope = act("dg%d" % j)

        def body(rows):
            pool[DK, rows, :] = (work[rows, :] * slope[rows, :].astype(f32)).astype(bf16)

        in_chunks(body)

    def accumulate(source, name):
        total[...] = total[...] + mm(pool[source], weight(name), NT)

    def mix_back(name):
        pool[DO] = mm(pool[EB], weight(name), NT).astype(bf16)

    def grad_matrix(unit, left, right):
        fill(unit, mm(left(), pool[right], TN))

    def grad_affine():
        value = affine_grads[...].astype(bf16)
        for group in range(8):
            for x in (0, 1):
                block = value[:, group * 128 : group * 128 + 128]
                mine_s[group // 4, group % 4, x] = block
                other_s[group // 4, group % 4, x] = block

    def probs_copy(layer, pair):
        slot = probs.at[pair % 2] if layer == 1 else probs.at[pair % 2, :, 0:768]
        src = (saved_p1 if layer == 0 else saved_p2).at[pair]
        return pltpu.make_async_copy(src, slot, probs_sem.at[layer, pair])

    def attend_back(layer, pair):
        causal = layer == 0
        for name in ("q%d", "k%d", "v%d"):
            act(name % (layer + 1))
        probs_copy(layer, pair).wait()
        attend_pair_back(
            pool.at[1], pool.at[2], pool.at[3], pool.at[DO], probs.at[pair % 2],
            pool.at[DQ], pool.at[DK], pool.at[DV], pair, causal,
        )

    def memory_back(first):
        if first:
            work[...] = mm(pool[DK], weight(4), NT)
        else:
            grad_memory[...] = (work[...] + mm(pool[DV], weight(5), NT)).astype(bf16)

    def tokens_back():
        grad_tokens[...] = (total[...] + mm(pool[DV], weight(2), NT)).astype(bf16)

    do = functools.partial
    start = lambda name: act_copy(name).start()
    order_of = [u for u in GRAD_ORDER if u != 16]

    def free(unit):
        k, needs = turn[unit], set()
        for ring_ref, step in ((mine, 5), (other, 1)):
            if k >= ring_ref.shape[0]:
                before = order_of[k - ring_ref.shape[0]]
                needs |= {(2 * before, step), (2 * before + 1, step)}
        return needs

    pieces = []

    def piece(name, needs, length, run):
        pieces.append((name, set(needs), length, run))

    def loads(name, needs=()):
        piece("L" + name, needs, 0.0, do(start, name))

    user = {("t", j): "dh%d" % j for j in range(4)}
    user.update({8 + j: "r%d" % j for j in range(4)})
    user.update({7: "o2", 3: "rq", 4: "m4", 5: "m5", 6: "o1", 0: "t0", 1: "t1", 2: "t2"})
    for name in ("n3", "s", "c", "g0", "g1", "g2", "g3", "dg0", "dg1", "y2", "m", "y1", "t"):
        loads(name)
    for k, name in enumerate(uses):
        needs = [user[uses[k - squares.shape[0]]]] if k >= squares.shape[0] else []
        piece(("W", name), needs, 0.0, do(load_weight, name))
    loads("dg2", ["dh0"])
    loads("dg3", ["dh1"])
    loads("n2", ["z3"])
    loads("n1", ["z2"])
    for k, name in enumerate(("a2", "q2", "k2", "v2")):
        loads(name, ["Gt%d" % k])
    loads("a1", ["G7"])
    for name in ("q1", "k1", "v1"):
        loads(name, ["B2_7"])
    for layer in (1, 0):
        for pair in range(8):
            if pair >= 2:
                needs = ["B%d_%d" % (layer + 1, pair - 2)]
            else:
                needs = [] if layer == 1 else ["B2_%d" % (6 + pair)]
            piece("P%d_%d" % (layer + 1, pair), needs, 0.0, lambda l=layer, p=pair: probs_copy(l, p).start())

    piece("z3", ["Ln3", "Ls", "Lc"], 2.5, do(norm_back, 2))
    for j in range(4):
        piece("Gf%d" % j, ["z3", "Lg%d" % j], 0.9, do(grad_tall, j, 0, 1))
    for j in range(4):
        piece("Gt%d" % j, ["z3", "Gf%d" % j], 1.6, do(grad_tall, j, 1, 4))
    for j in range(4):
        piece("G%d" % (8 + j), ["r%d" % j, "Ly2"] + list(free(8 + j)), 2.0, do(grad_matrix, 8 + j, lambda: act("y2")[...], DK))
    piece("G7", ["z2", "La2"] + list(free(7)), 2.0, do(grad_matrix, 7, lambda: act("a2")[...], EB))
    piece("G3", ["B2_7", "Ly1"] + list(free(3)), 2.0, do(grad_matrix, 3, lambda: act("y1")[...], DQ))
    piece("G4", ["B2_7", "Lm", "G3"] + list(free(4)), 2.0, do(grad_matrix, 4, lambda: act("m")[...], DK))
    piece("G5", ["B2_7", "Lm", "G4"] + list(free(5)), 2.0, do(grad_matrix, 5, lambda: act("m")[...], DV))
    piece("G6", ["z1", "La1"] + list(free(6)), 2.0, do(grad_matrix, 6, lambda: act("a1")[...], EB))
    piece("G16", ["z1"], 0.3, grad_affine)
    for k, unit in enumerate((0, 1, 2)):
        piece("G%d" % unit, ["B1_7", "Lt"] + list(free(unit)), 2.0, do(grad_matrix, unit, lambda: act("t")[...], DQ + k))
    for j in range(4):
        needs = ["z3", "Ldg%d" % j, ("W", ("t", j))] + (["G%d" % (7 + j)] if j else [])
        piece("dh%d" % j, needs, 2.2, do(hidden_back, j))
        piece("r%d" % j, ["dh%d" % j, ("W", 8 + j)], 1.8, do(accumulate, DK, 8 + j))
    piece("z2", ["r3", "Gt0", "Gt1", "Gt2", "Gt3", "dh3", "Ln2"], 2.5, do(norm_back, 1))
    piece("o2", ["z2", ("W", 7), "dh2", "dh3"], 1.6, do(mix_back, 7))
    for pair in range(8):
        piece("B2_%d" % pair, ["B2_%d" % (pair - 1) if pair else "o2", "G11", "P2_%d" % pair, "Lq2", "Lk2", "Lv2"], 2.3, do(attend_back, 1, pair))
    piece("rq", ["B2_7", ("W", 3)], 1.8, do(accumulate, DQ, 3))
    piece("z1", ["rq", "G7", "Ln1"], 2.5, do(norm_back, 0))
    piece("m4", ["B2_7", ("W", 4)], 1.6, do(memory_back, True))
    piece("m5", ["m4", ("W", 5)], 1.8, do(memory_back, False))
    piece("o1", ["z1", "B2_7", ("W", 6)], 1.6, do(mix_back, 6))
    for pair in range(8):
        piece("B1_%d" % pair, ["B1_%d" % (pair - 1) if pair else "o1", "m5", "G3", "G4", "G5", "P1_%d" % pair, "Lq1", "Lk1", "Lv1"], 1.8, do(attend_back, 0, pair))
    piece("t0", ["B1_7", ("W", 0)], 1.8, do(accumulate, DQ, 0))
    piece("t1", ["B1_7", "t0", ("W", 1)], 1.8, do(accumulate, DK, 1))
    piece("t2", ["t1", ("W", 2)], 1.8, tokens_back)

    def stage(step):
        def at(part):
            unit, needs = part // 2, set()
            if step == 0:
                needs = {"G%d" % unit}
                if 12 <= unit < 16:
                    needs = {("Gf%d" if unit == 12 else "Gt%d") % j for j in range(4)}
            return step, needs | scatter.needs(part, step), do(scatter.stage, part, step)

        return at

    place.greet()
    waits = {step: SCATTER_WAIT for step in (0, 1, 2, 3)}
    waits.update({2.5: 3.0, 3.5: 3.0, 4: 1.0})
    costs = {1: 0.5, 2: 0.3, 3: 0.3, 4: 0.2}
    for run in arrange_back(
        SCATTER_ORDER, [stage(step) for step in Scatter.stages], pieces, waits, SCATTER_PACE, costs
    ):
        run()


class RingScatter(Scatter):
    def __init__(self, place, send_sem, recv_sem, other, mine, twin, eight, four, zs, out, kinds, credit, turn):
        super().__init__(place, send_sem, recv_sem, other, mine, twin, eight, four, zs, out, kinds)
        self.credit, self.turn = credit, turn
        self.count = len(turn)

    def needs(self, unit, step):
        if unit == 32 or step not in (0, 1, 4):
            return set()
        k, needs = self.turn[unit], set()
        part_at = {turn: part for part, turn in self.turn.items()}
        if k >= 1:
            needs.add((part_at[k - 1], step))
        if step == 0 and k >= 2 * DEPTH_TWIN:
            needs.add((part_at[k - 2 * DEPTH_TWIN], 1))
        if step == 1 and k >= 2 * DEPTH_REST:
            needs.add((part_at[k - 2 * DEPTH_REST], 4))
        return needs

    def give(self, slot, device):
        pl.semaphore_signal(self.credit.at[slot], inc=1, device_id=device, device_id_type=MESH)

    def stage(self, unit, step):
        p = self.p
        k = None if unit == 32 else self.turn[unit]
        if k is not None and step == 0 and k >= 2 * DEPTH_TWIN:
            pl.semaphore_wait(self.credit.at[0], 1)
        if k is not None and step == 1 and k >= 2 * DEPTH_REST:
            for slot in (1, 2):
                pl.semaphore_wait(self.credit.at[slot], 1)
            for far in (1, 2, 3):
                pl.semaphore_wait(self.credit.at[4 + lax.rem(p.z + far, 4)], 1)
        if step == 4 and 24 <= unit < 32:
            hold = self.out
            self.out = lambda u: TallOut(self.tall, u)
            super().stage(unit, step)
            self.out = hold
        else:
            super().stage(unit, step)
        if k is not None and step == 1 and k + 2 * DEPTH_TWIN < self.count:
            self.give(0, p.sibling())
        if k is not None and step == 4 and k + 2 * DEPTH_REST < self.count:
            self.give(1, p.over_x())
            self.give(2, p.over_y())
            for far in (1, 2, 3):
                self.give(4 + p.z, p.at(z=lax.rem(p.z + far, 4)))


class TallOut:
    def __init__(self, store, unit):
        self.store, self.unit = store, unit

    def __setitem__(self, _, value):
        self.store(self.unit, value)


def backward_call(cotangent, saved_all, tokens, memory):
    wide, deep, saved, saved_g, saved_dg, saved_n, saved_scale, saved_p1, saved_p2, affine = saved_all
    hbm = pl.BlockSpec(memory_space=pl.ANY)
    vmem = pl.BlockSpec(memory_space=pltpu.VMEM)
    shape = jax.ShapeDtypeStruct
    block = (32, 1024)
    tiny = (16, 128)
    return pl.pallas_call(
        backward_kernel,
        out_shape=(
            shape((512, 1024), bf16),
            shape((512, 1024), bf16),
            shape((6, 32, 1024), f32),
            shape((2, 32, 1024), f32),
            shape((32, 4096), f32),
            shape((128, 1024), f32),
            shape((16, 128), f32),
        ),
        in_specs=[hbm, hbm, hbm, vmem] + [hbm] * 9,
        out_specs=[vmem] * 7,
        scratch_shapes=[
            pltpu.VMEM((12, 512, 1024), bf16),
            pltpu.VMEM((512, 1024), f32),
            pltpu.VMEM((512, 1024), f32),
            pltpu.VMEM((512, 1024), f32),
            pltpu.VMEM((3, 512, 1), f32),
            pltpu.VMEM((2, 2, 1024, 256), bf16),
            pltpu.VMEM((2, 1024, 1024), bf16),
            pltpu.VMEM((16, 1024), f32),
            pltpu.VMEM((DEPTH_OTHER, 2, 4, 2, *block), bf16),
            pltpu.VMEM((DEPTH_MINE, 2, 4, 2, *block), bf16),
            pltpu.VMEM((DEPTH_TWIN, 2, 4, 2, *block), bf16),
            pltpu.VMEM((DEPTH_REST, 2, 4, *block), bf16),
            pltpu.VMEM((DEPTH_REST, 4, *block), bf16),
            pltpu.VMEM((DEPTH_REST, 4, 2, *block), bf16),
            pltpu.VMEM((2, 4, 2, *tiny), bf16),
            pltpu.VMEM((2, 4, 2, *tiny), bf16),
            pltpu.VMEM((2, 4, 2, *tiny), bf16),
            pltpu.VMEM((2, 4, *tiny), bf16),
            pltpu.VMEM((4, *tiny), bf16),
            pltpu.VMEM((4, 2, *tiny), bf16),
            pltpu.SemaphoreType.DMA((2 * UNITS, 9)),
            pltpu.SemaphoreType.DMA((2 * UNITS, 9)),
            pltpu.SemaphoreType.REGULAR((8,)),
            pltpu.SemaphoreType.DMA((16, 4)),
            pltpu.SemaphoreType.DMA((32,)),
            pltpu.SemaphoreType.DMA((2, 8)),
        ],
        compiler_params=pltpu.CompilerParams(
            collective_id=1, has_side_effects=True, vmem_limit_bytes=63 << 20
        ),
        cost_estimate=pl.CostEstimate(
            flops=40_000_000_000, bytes_accessed=120_000_000, transcendentals=0
        ),
    )(
        cotangent, wide.reshape(12, 1024, 1024), deep.reshape(4, 4096, 256),
        affine, saved, saved_g, saved_dg, saved_n, saved_scale, saved_p1, saved_p2, tokens, memory,
    )


def hand_over_kernel(*refs):
    count = (len(refs) - 1) // 3
    given, taken, held, sem = refs[:count], refs[count : 2 * count], refs[2 * count : -1], refs[-1]
    reads = [pltpu.make_async_copy(given[k], held[k], sem.at[0, k]) for k in range(count)]
    writes = [pltpu.make_async_copy(held[k], taken[k], sem.at[1, k]) for k in range(count)]
    for copy in reads:
        copy.start()
    for read, write in zip(reads, writes):
        read.wait()
        write.start()
    for copy in writes:
        copy.wait()


def hand_over(*results):
    count = len(results)
    return pl.pallas_call(
        hand_over_kernel,
        out_shape=[jax.ShapeDtypeStruct(r.shape, r.dtype) for r in results],
        in_specs=[pl.BlockSpec(memory_space=pl.ANY)] * count,
        out_specs=[pl.BlockSpec(memory_space=pl.ANY)] * count,
        scratch_shapes=[pltpu.VMEM(r.shape, r.dtype) for r in results]
        + [pltpu.SemaphoreType.DMA((2, count))],
        compiler_params=pltpu.CompilerParams(vmem_limit_bytes=60 << 20),
    )(*results)


def on_device(
    tokens, memory, cotangent, sent_len, mem_len, proj_in, proj_out, ffn_in, ffn_out, ln_gain, ln_bias
):
    small = small_rows(ln_gain, ln_bias)
    output, wide, deep, _, saved, g, dg, n, scale, p1, p2, affine = forward_call(
        tokens, memory, sent_len, mem_len, proj_in, proj_out, ffn_in, ffn_out, small
    )
    *results, g_small = backward_call(
        cotangent, (wide, deep, saved, g, dg, n, scale, p1, p2, affine), tokens, memory
    )
    spot = lax.axis_index("fsdp") % 4
    own = lax.dynamic_slice(g_small, (0, spot * 32), (16, 32))
    return (*hand_over(output, *results), own[0:3], own[3:6])


def on_any_mesh(
    tokens, memory, cotangent, sent_len, mem_len, proj_in, proj_out, ffn_in, ffn_out, ln_gain, ln_bias
):
    dims = (1, 1, 0, 0, 1, 1)
    shards = (proj_in, proj_out, ffn_in, ffn_out, ln_gain, ln_bias)
    weights = tuple(
        lax.all_gather(shard, BOTH, axis=dim, tiled=True) for shard, dim in zip(shards, dims)
    )
    sent_seg = segment_ids(sent_len[0], tokens.shape[0])
    mem_seg = segment_ids(mem_len[0], memory.shape[0])
    saved = run_forward(tokens, memory, sent_seg, mem_seg, weights)
    output = saved["o"].astype(bf16)
    grads = run_backward(saved, tokens, memory, sent_seg, mem_seg, weights, cotangent)
    summed = tuple(
        lax.psum_scatter(grad, BOTH, scatter_dimension=dim, tiled=True)
        for grad, dim in zip(grads[2:], dims)
    )
    return (output, *grads[:2], *summed)


def solution(mesh):
    placed = (
        P(BOTH, None),
        P(BOTH, None),
        P(BOTH, None),
        P(BOTH, None),
        P(BOTH, None),
        P(None, BOTH, None),
        P(None, BOTH, None),
        P(BOTH, None),
        P(BOTH, None),
        P(None, BOTH),
        P(None, BOTH),
    )
    routed = mesh.shape["dp"] == 2 and mesh.shape["fsdp"] == 16
    return jax.shard_map(
        on_device if routed else on_any_mesh,
        mesh=mesh,
        in_specs=placed,
        out_specs=(
            P(BOTH, None),
            P(BOTH, None),
            P(BOTH, None),
            P(None, BOTH, None),
            P(None, BOTH, None),
            P(BOTH, None),
            P(BOTH, None),
            P(None, BOTH),
            P(None, BOTH),
        ),
        check_vma=False,
    )
```

```python
import functools

import jax
import jax.numpy as jnp
from jax import lax
from jax.experimental import pallas as pl
from jax.experimental.pallas import tpu as pltpu
from jax.sharding import PartitionSpec as P

HEADS = 16
HEAD_DIM = 64


residual_scale = 300.0**0.25
masked_score = -1000000000.0


def layer_norm(summed, scale_row, shift_row):
    middle = jnp.mean(summed, axis=-1, keepdims=True)
    centered = summed - middle
    spread = jnp.mean(centered * centered, axis=-1, keepdims=True)
    return centered * lax.rsqrt(spread + 1e-05) * scale_row + shift_row


def segment_ids(lengths, seg_count):
    sent_ends = jnp.cumsum(lengths)
    positions = jnp.arange(seg_count, dtype=jnp.int32)
    return jnp.sum((positions[:, None] >= sent_ends[None, :]).astype(jnp.int32), axis=1)


def split_blocks(array, block_rows):
    return array.reshape((array.shape[0] // block_rows, block_rows) + array.shape[1:])


def block_scores(query_blk, key_heads, seg_blk, row_blk, key_seg, causal):
    scores = jnp.einsum(
        "qhd,khd->hqk", query_blk, key_heads, preferred_element_type=jnp.float32
    ) * HEAD_DIM ** (-0.5)
    allowed = seg_blk[:, None] == key_seg[None, :]
    if causal:
        allowed = allowed & (
            jnp.arange(key_seg.shape[0], dtype=jnp.int32)[None, :] <= row_blk[:, None]
        )
    return jnp.where(allowed[None], scores, masked_score)


def attend_forward(queries, key_rows, values, query_seg, key_seg, causal):
    row_count = queries.shape[0]
    block_rows = min(row_count, 512)
    key_heads = key_rows.reshape(key_rows.shape[0], HEADS, HEAD_DIM)
    value_heads = values.reshape(values.shape[0], HEADS, HEAD_DIM)
    positions = jnp.arange(row_count, dtype=jnp.int32)
    pieces = (
        split_blocks(queries.reshape(row_count, HEADS, HEAD_DIM), block_rows),
        split_blocks(query_seg, block_rows),
        split_blocks(positions, block_rows),
    )

    def one_block(piece):
        query_blk, seg_blk, row_blk = piece
        scores = block_scores(query_blk, key_heads, seg_blk, row_blk, key_seg, causal)
        peaks = jnp.max(scores, axis=-1, keepdims=True)
        powers = jnp.exp(scores - peaks)
        totals = jnp.sum(powers, axis=-1, keepdims=True)
        weights = (powers / totals).astype(jnp.bfloat16)
        mixture = jnp.einsum(
            "hqk,khd->qhd", weights, value_heads, preferred_element_type=jnp.float32
        )
        return (mixture, (peaks + jnp.log(totals))[..., 0])

    mixture, log_totals = lax.map(one_block, pieces)
    return (mixture.reshape(row_count, HEADS * HEAD_DIM).astype(jnp.bfloat16), log_totals)


def attend_backward(queries, key_rows, values, query_seg, key_seg, causal, log_totals, grad_mix):
    row_count = queries.shape[0]
    block_rows = min(row_count, 512)
    score_scale = HEAD_DIM ** (-0.5)
    key_heads = key_rows.reshape(key_rows.shape[0], HEADS, HEAD_DIM)
    value_heads = values.reshape(values.shape[0], HEADS, HEAD_DIM)
    positions = jnp.arange(row_count, dtype=jnp.int32)
    pieces = (
        split_blocks(queries.reshape(row_count, HEADS, HEAD_DIM), block_rows),
        split_blocks(query_seg, block_rows),
        split_blocks(positions, block_rows),
        log_totals,
        split_blocks(grad_mix.reshape(row_count, HEADS, HEAD_DIM), block_rows),
    )

    def one_block(carried, piece):
        grad_keys, grad_values = carried
        query_blk, seg_blk, row_blk, lse_blk, grad_blk = piece
        scores = block_scores(query_blk, key_heads, seg_blk, row_blk, key_seg, causal)
        probs = jnp.exp(scores - lse_blk[:, :, None])
        grad_values = grad_values + jnp.einsum(
            "hqk,qhd->khd", probs.astype(jnp.bfloat16), grad_blk, preferred_element_type=jnp.float32
        )
        grad_probs = jnp.einsum(
            "qhd,khd->hqk", grad_blk, value_heads, preferred_element_type=jnp.float32
        )
        inner = jnp.sum(grad_probs * probs, axis=-1, keepdims=True)
        grad_scores = (probs * (grad_probs - inner)).astype(jnp.bfloat16)
        grad_query = (
            jnp.einsum("hqk,khd->qhd", grad_scores, key_heads, preferred_element_type=jnp.float32)
            * score_scale
        )
        grad_keys = (
            grad_keys
            + jnp.einsum("hqk,qhd->khd", grad_scores, query_blk, preferred_element_type=jnp.float32)
            * score_scale
        )
        return ((grad_keys, grad_values), grad_query)

    zeros = jnp.zeros(key_heads.shape, jnp.float32)
    (grad_keys, grad_values), grad_query = lax.scan(one_block, (zeros, zeros), pieces)
    width = HEADS * HEAD_DIM
    return (
        grad_query.reshape(row_count, width).astype(jnp.bfloat16),
        grad_keys.reshape(-1, width).astype(jnp.bfloat16),
        grad_values.reshape(-1, width).astype(jnp.bfloat16),
    )


def run_forward(tokens, memory, sent_seg, mem_seg, weights):
    proj_in, proj_out, ffn_in, ffn_out, ln_gain, ln_bias = weights
    gains = ln_gain.astype(jnp.float32)
    shifts = ln_bias.astype(jnp.float32)
    self_qkv = jnp.einsum(
        "td,wde->wte", tokens, proj_in[0:3], preferred_element_type=jnp.float32
    ).astype(jnp.bfloat16)
    self_mix, self_lse = attend_forward(
        self_qkv[0], self_qkv[1], self_qkv[2], sent_seg, sent_seg, True
    )
    first_sum = residual_scale * tokens.astype(jnp.float32) + jnp.dot(
        self_mix, proj_out[0], preferred_element_type=jnp.float32
    )
    first_out = layer_norm(first_sum, gains[0], shifts[0])
    first_low = first_out.astype(jnp.bfloat16)
    cross_query = jnp.dot(first_low, proj_in[3], preferred_element_type=jnp.float32).astype(
        jnp.bfloat16
    )
    cross_kv = jnp.einsum(
        "td,wde->wte", memory, proj_in[4:6], preferred_element_type=jnp.float32
    ).astype(jnp.bfloat16)
    cross_mix, cross_lse = attend_forward(
        cross_query, cross_kv[0], cross_kv[1], sent_seg, mem_seg, False
    )
    second_sum = residual_scale * first_out + jnp.dot(
        cross_mix, proj_out[1], preferred_element_type=jnp.float32
    )
    second_out = layer_norm(second_sum, gains[1], shifts[1])
    second_low = second_out.astype(jnp.bfloat16)
    hidden_pre = jnp.dot(second_low, ffn_in, preferred_element_type=jnp.float32)
    hidden_act = jax.nn.gelu(hidden_pre).astype(jnp.bfloat16)
    third_sum = residual_scale * second_out + jnp.dot(
        hidden_act, ffn_out, preferred_element_type=jnp.float32
    )
    final = layer_norm(third_sum, gains[2], shifts[2])
    return {
        "a": self_qkv,
        "b": self_mix,
        "c": self_lse,
        "d": first_sum,
        "e": first_low,
        "f": cross_query,
        "g": cross_kv,
        "h": cross_mix,
        "i": cross_lse,
        "j": second_sum,
        "k": second_low,
        "l": hidden_pre,
        "m": hidden_act,
        "n": third_sum,
        "o": final,
    }


def run_backward(saved, tokens, memory, sent_seg, mem_seg, weights, cotangent):
    proj_in, proj_out, ffn_in, ffn_out, ln_gain, ln_bias = weights
    gains = ln_gain.astype(jnp.float32)
    shifts = ln_bias.astype(jnp.float32)
    _, pull_third = jax.vjp(layer_norm, saved["n"], gains[2], shifts[2])
    grad_third, gain_third, shift_third = pull_third(cotangent.astype(jnp.float32))
    third_low = grad_third.astype(jnp.bfloat16)
    grad_ffn_out = jnp.einsum(
        "tf,td->fd", saved["m"], third_low, preferred_element_type=jnp.float32
    )
    grad_act = jnp.einsum("td,fd->tf", third_low, ffn_out, preferred_element_type=jnp.float32)
    _, pull_gelu = jax.vjp(jax.nn.gelu, saved["l"])
    grad_pre = pull_gelu(grad_act)[0].astype(jnp.bfloat16)
    grad_ffn_in = jnp.einsum(
        "td,tf->df", saved["k"], grad_pre, preferred_element_type=jnp.float32
    )
    grad_second = residual_scale * grad_third + jnp.einsum(
        "tf,df->td", grad_pre, ffn_in, preferred_element_type=jnp.float32
    )
    ffn_grads = (grad_ffn_in, grad_ffn_out, gain_third, shift_third)
    _, pull_second = jax.vjp(layer_norm, saved["j"], gains[1], shifts[1])
    grad_two, gain_second, shift_second = pull_second(grad_second)
    two_low = grad_two.astype(jnp.bfloat16)
    grad_cross_out = jnp.einsum(
        "te,td->ed", saved["h"], two_low, preferred_element_type=jnp.float32
    )
    grad_cross_mix = jnp.einsum(
        "td,ed->te", two_low, proj_out[1], preferred_element_type=jnp.float32
    ).astype(jnp.bfloat16)
    grad_cq, grad_ck, grad_cv = attend_backward(
        saved["f"],
        saved["g"][0],
        saved["g"][1],
        sent_seg,
        mem_seg,
        False,
        saved["i"],
        grad_cross_mix,
    )
    grad_ckv = jnp.stack([grad_ck, grad_cv])
    grad_cross_in = jnp.concatenate(
        [
            jnp.einsum(
                "td,te->de", saved["e"], grad_cq, preferred_element_type=jnp.float32
            )[None],
            jnp.einsum("td,wte->wde", memory, grad_ckv, preferred_element_type=jnp.float32),
        ],
        axis=0,
    )
    grad_memory = jnp.einsum(
        "wte,wde->td", grad_ckv, proj_in[4:6], preferred_element_type=jnp.float32
    ).astype(jnp.bfloat16)
    grad_first = residual_scale * grad_two + jnp.einsum(
        "te,de->td", grad_cq, proj_in[3], preferred_element_type=jnp.float32
    )
    cross_grads = (grad_cross_in, grad_cross_out, gain_second, shift_second)
    _, pull_first = jax.vjp(layer_norm, saved["d"], gains[0], shifts[0])
    grad_one, gain_first, shift_first = pull_first(grad_first)
    one_low = grad_one.astype(jnp.bfloat16)
    grad_self_out = jnp.einsum(
        "te,td->ed", saved["b"], one_low, preferred_element_type=jnp.float32
    )
    grad_self_mix = jnp.einsum(
        "td,ed->te", one_low, proj_out[0], preferred_element_type=jnp.float32
    ).astype(jnp.bfloat16)
    self_qkv = saved["a"]
    grad_sq, grad_sk, grad_sv = attend_backward(
        self_qkv[0],
        self_qkv[1],
        self_qkv[2],
        sent_seg,
        sent_seg,
        True,
        saved["c"],
        grad_self_mix,
    )
    grad_sqkv = jnp.stack([grad_sq, grad_sk, grad_sv])
    grad_self_in = jnp.einsum("td,wte->wde", tokens, grad_sqkv, preferred_element_type=jnp.float32)
    grad_tokens = (
        residual_scale * grad_one
        + jnp.einsum("wte,wde->td", grad_sqkv, proj_in[0:3], preferred_element_type=jnp.float32)
    ).astype(jnp.bfloat16)
    self_grads = (grad_self_in, grad_self_out, gain_first, shift_first)
    all_in = jnp.concatenate([self_grads[0], cross_grads[0]], axis=0)
    all_out = jnp.stack([self_grads[1], cross_grads[1]])
    all_gain = jnp.stack([self_grads[2], cross_grads[2], ffn_grads[2]])
    all_bias = jnp.stack([self_grads[3], cross_grads[3], ffn_grads[3]])
    return (
        grad_tokens,
        grad_memory,
        all_in,
        all_out,
        ffn_grads[0],
        ffn_grads[1],
        all_gain,
        all_bias,
    )


MESH = pl.DeviceIdType.MESH
BOTH = ("dp", "fsdp")
f32 = jnp.float32
bf16 = jnp.bfloat16
UNITS = 17
def shard_of(unit):
    if unit < 12:
        return (32, 1024)
    return (128, 256) if unit < 16 else (16, 128)


class Place:
    def __init__(self):
        inner = lax.axis_index("fsdp")
        self.y = lax.axis_index("dp")
        self.z = inner // 4
        self.x = (inner // 2) % 2
        self.c = inner % 2

    def at(self, y=None, z=None, x=None, c=None):
        y = self.y if y is None else y
        z = self.z if z is None else z
        x = self.x if x is None else x
        c = self.c if c is None else c
        return (y, (z * 2 + x) * 2 + c)

    def over_x(self):
        return self.at(x=1 - self.x)

    def over_y(self):
        return self.at(y=1 - self.y)

    def sibling(self):
        return self.at(c=1 - self.c)

    def greet(self):
        barrier = pltpu.get_barrier_semaphore()
        friends = [self.at(z=lax.rem(self.z + k, 4)) for k in (1, 2, 3)]
        friends += [self.over_x(), self.over_y(), self.sibling()]
        for friend in friends:
            pl.semaphore_signal(barrier, inc=1, device_id=friend, device_id_type=MESH)
        pl.semaphore_wait(barrier, len(friends))


class Sender:
    def __init__(self, place, send_sem, recv_sem):
        self.p, self.send_sem, self.recv_sem = place, send_sem, recv_sem
        self.pending = {}

    def copy(self, unit, slot, src, dst, device, landing=None):
        return pltpu.make_async_remote_copy(
            src_ref=src,
            dst_ref=dst,
            send_sem=self.send_sem.at[unit, slot],
            recv_sem=self.recv_sem.at[unit, slot if landing is None else landing],
            device_id=device,
            device_id_type=MESH,
        )

    def send(self, unit, slot, src, dst, device, cond=None, landing=None):
        make = lambda: self.copy(unit, slot, src, dst, device, landing)
        if cond is None:
            make().start()
            self.pending.setdefault(unit, []).append(lambda: make().wait_send())
        else:
            pl.when(cond)(lambda: make().start())
            self.pending.setdefault(unit, []).append(
                lambda: pl.when(cond)(lambda: make().wait_send())
            )

    def wait(self, unit, slot, ref):
        self.copy(unit, slot, ref, ref, self.p.sibling()).wait_recv()

    def finish(self, unit):
        for done in self.pending.pop(unit, []):
            done()


class Gather(Sender):
    stages = (0, 0.5, 1, 1.5, 2, 3, 4)

    def __init__(self, place, send_sem, recv_sem, whole, own, kinds):
        super().__init__(place, send_sem, recv_sem)
        self.whole, self.own, self.kinds = whole, own, kinds

    def view(self, unit, y=None, z=None, x=None, c=None):
        every = slice(None)
        pick = lambda v: every if v is None else v
        return self.whole(unit).at[pick(y), pick(z), pick(x), pick(c)]

    def along_z(self, unit):
        p, kind = self.p, self.kinds[unit]
        if kind[0] == "p":
            return lambda z: self.view(unit, y=p.y, z=z, x=p.x, c=p.c)
        if kind == "rL":
            return lambda z: self.view(unit, y=p.y, z=z, c=p.c)
        return lambda z: self.view(unit, z=z, x=p.x, c=p.c)

    def z_send(self, unit):
        p, part = self.p, self.along_z(unit)
        for k in (1, 2, 3):
            there = lax.rem(p.z + k, 4)
            near = jnp.logical_not(
                ((p.z == 0) & (there == 3)) | ((p.z == 3) & (there == 0))
            )
            source = self.own(unit) if self.kinds[unit][0] == "p" else part(p.z)
            self.send(unit, there, source, part(p.z), p.at(z=there), near, landing=p.z)

    def z_relay(self, unit):
        p, part = self.p, self.along_z(unit)
        for here, source, there in ((2, 0, 3), (1, 3, 0)):
            pl.when(p.z == here)(lambda source=source: self.wait(unit, source, part(source)))
            self.send(
                unit, 8, part(source), part(source), p.at(z=there), p.z == here, landing=source
            )

    def z_wait(self, unit):
        p, part = self.p, self.along_z(unit)
        for k in (1, 2, 3):
            source = lax.rem(p.z + 4 - k, 4)
            relayed = ((p.z == 2) & (source == 0)) | ((p.z == 1) & (source == 3))
            pl.when(jnp.logical_not(relayed))(
                lambda source=source: self.wait(unit, source, part(source))
            )

    def stage(self, unit, step):
        p, kind = self.p, self.kinds[unit]
        y, z, x, c = p.y, p.z, p.x, p.c
        view = lambda **at: self.view(unit, **at)
        send = lambda slot, ref, device: self.send(unit, slot, ref, ref, device)
        if kind[0] == "p":
            if step == 0:
                self.z_send(unit)
            if step == 0.5:
                self.z_relay(unit)
            if step == 1:
                self.z_wait(unit)
                line = view(y=y, x=x, c=c)
                send(4, line, p.over_x())
                send(5, line, p.over_y())
            if step == 2:
                if kind == "pL":
                    line = view(y=y, x=1 - x, c=c)
                    self.wait(unit, 4, line)
                    send(6, line, p.over_y())
                else:
                    line = view(y=1 - y, x=x, c=c)
                    self.wait(unit, 5, line)
                    send(6, line, p.over_x())
            if step == 3:
                if kind == "pL":
                    self.wait(unit, 5, view(y=1 - y, x=x, c=c))
                else:
                    self.wait(unit, 4, view(y=y, x=1 - x, c=c))
                self.wait(unit, 6, view(y=1 - y, x=1 - x, c=c))
                send(7, view(c=c), p.sibling())
        else:
            left = kind == "rL"
            first, last = (p.over_x(), p.over_y()) if left else (p.over_y(), p.over_x())
            if step == 0:
                self.send(unit, 4, self.own(unit), view(y=y, z=z, x=x, c=c), first)
            if step == 1:
                self.wait(
                    unit,
                    4,
                    view(y=y, z=z, x=1 - x, c=c) if left else view(y=1 - y, z=z, x=x, c=c),
                )
                self.z_send(unit)
            if step == 1.5:
                self.z_relay(unit)
            if step == 2:
                self.z_wait(unit)
                send(5, view(y=y, c=c) if left else view(x=x, c=c), last)
            if step == 3:
                self.wait(unit, 5, view(y=1 - y, c=c) if left else view(x=1 - x, c=c))
                send(7, view(c=c), p.sibling())
        if step == 4:
            self.wait(unit, 7, view(c=1 - c))


class Scatter(Sender):
    stages = (0, 1, 2, 2.5, 3, 3.5, 4, 5)

    def __init__(self, place, send_sem, recv_sem, other, mine, twin, eight, four, zs, out, kinds):
        super().__init__(place, send_sem, recv_sem)
        self.other, self.mine, self.twin = other, mine, twin
        self.eight, self.four, self.zs, self.out, self.kinds = eight, four, zs, out, kinds

    def add(self, into, *terms):
        total = into[...].astype(f32)
        for term in terms:
            total = total + term[...].astype(f32)
        into[...] = total.astype(into.dtype)

    def along_z(self, unit):
        p, kind, mine = self.p, self.kinds[unit], self.mine(unit)
        if kind[0] == "p":
            return (lambda z: mine.at[p.y, z, p.x]), (lambda ref: ref.at[0])
        if kind == "rL":
            return (lambda z: mine.at[p.y, z]), (lambda ref: ref)
        return (lambda z: mine.at[:, z, p.x]), (lambda ref: ref)

    def z_send(self, unit):
        p, zs = self.p, self.zs(unit)
        part, slot = self.along_z(unit)
        for k in (1, 2, 3):
            there = lax.rem(p.z + k, 4)
            far = ((p.z == 0) & (there == 3)) | ((p.z == 3) & (there == 0))
            relayed = ((p.z == 2) & (there == 0)) | ((p.z == 1) & (there == 3))
            self.send(
                unit,
                4 + there,
                part(there),
                slot(zs.at[p.z]),
                p.at(z=there),
                jnp.logical_not(far | relayed),
                landing=4 + p.z,
            )
        self.send(unit, 8, part(3), slot(zs.at[1]), p.at(z=1), p.z == 0)
        self.send(unit, 8, part(0), slot(zs.at[2]), p.at(z=2), p.z == 3)

    def z_relay(self, unit):
        p, zs = self.p, self.zs(unit)
        part, slot = self.along_z(unit)
        for here, there in ((1, 3), (2, 0)):

            @pl.when(p.z == here)
            def _(here=here, there=there):
                self.wait(unit, 8, slot(zs.at[here]))
                self.add(part(there), slot(zs.at[here]))

            self.send(
                unit,
                4 + there,
                part(there),
                slot(zs.at[here]),
                p.at(z=there),
                p.z == here,
                landing=4 + here,
            )

    def z_sum(self, unit, store):
        p, zs = self.p, self.zs(unit)
        part, slot = self.along_z(unit)
        edge = (p.z == 0) | (p.z == 3)

        @pl.when(edge)
        def _():
            self.wait(unit, 5, slot(zs.at[1]))
            self.wait(unit, 6, slot(zs.at[2]))
            store(
                part(p.z)[...].astype(f32)
                + slot(zs.at[1])[...].astype(f32)
                + slot(zs.at[2])[...].astype(f32)
            )

        @pl.when(jnp.logical_not(edge))
        def _():
            inner = 3 - p.z
            self.wait(unit, 4, slot(zs.at[0]))
            self.wait(unit, 7, slot(zs.at[3]))
            self.wait(unit, 4 + inner, slot(zs.at[inner]))
            store(
                part(p.z)[...].astype(f32)
                + slot(zs.at[inner])[...].astype(f32)
                + slot(zs.at[0])[...].astype(f32)
                + slot(zs.at[3])[...].astype(f32)
            )

    def stage(self, unit, step):
        p, kind = self.p, self.kinds[unit]
        y, z, x = p.y, p.z, p.x
        mine, eight, four, out = self.mine(unit), self.eight(unit), self.four(unit), self.out(unit)
        send = lambda slot, src, dst, device: self.send(unit, slot, src, dst, device)
        if step == 0:
            send(0, self.other(unit), self.twin(unit), p.sibling())
        if step == 1:
            self.wait(unit, 0, self.twin(unit))
            for half in (0, 1):
                self.add(mine.at[half], self.twin(unit).at[half])
            self.finish(unit)
            if kind == "pL":
                send(1, mine.at[1 - y, :, 1 - x], eight.at[0], p.over_y())
                send(3, mine.at[1 - y, :, x], four, p.over_y())
            if kind == "pR":
                send(1, mine.at[1 - y, :, 1 - x], eight.at[0], p.over_x())
                send(3, mine.at[y, :, 1 - x], four, p.over_x())
            for half in (0, 1):
                if kind == "rL":
                    send(1 + half, mine.at[1 - y, :, half], eight.at[half], p.over_y())
                if kind == "rR":
                    send(1 + half, mine.at[half, :, 1 - x], eight.at[half], p.over_x())
        if step == 2:
            if kind[0] == "p":
                self.wait(unit, 1, eight.at[0])
                line = mine.at[y, :, 1 - x] if kind == "pL" else mine.at[1 - y, :, x]
                self.add(line, eight.at[0])
                send(2, line, eight.at[1], p.over_x() if kind == "pL" else p.over_y())
            else:
                for half in (0, 1):
                    self.wait(unit, 1 + half, eight.at[half])
                    self.add(
                        mine.at[y, :, half] if kind == "rL" else mine.at[half, :, x],
                        eight.at[half],
                    )
                self.z_send(unit)
        if step == 2.5 and kind[0] == "r":
            self.z_relay(unit)
        if step == 3:
            if kind[0] == "p":
                self.wait(unit, 3, four)
                self.wait(unit, 2, eight.at[1])
                self.add(mine.at[y, :, x], four, eight.at[1])
                self.z_send(unit)
            else:
                line = mine.at[y, z] if kind == "rL" else mine.at[:, z, x]

                def keep(value):
                    line[...] = value.astype(bf16)

                self.z_sum(unit, keep)
                if kind == "rL":
                    send(3, mine.at[y, z, 1 - x], four.at[0], p.over_x())
                else:
                    send(3, mine.at[1 - y, z, x], four.at[0], p.over_y())
        if step == 3.5 and kind[0] == "p":
            self.z_relay(unit)
        if step == 4:

            def result(value):
                out[...] = value

            if kind[0] == "p":
                self.z_sum(unit, result)
            else:
                self.wait(unit, 3, four.at[0])
                result(mine[y, z, x].astype(f32) + four[0].astype(f32))
        if step == 5:
            self.finish(unit)


def kinds_of(pattern, order):
    kinds = {}
    for place, unit in enumerate(order):
        kinds[unit] = pattern[(place // 2) % len(pattern)] + "LR"[place % 2]
    return kinds


NT = (((1,), (1,)), ((), ()))
NN = (((1,), (0,)), ((), ()))
TN = (((0,), (0,)), ((), ()))


def mm(a, b, dims=NN):
    return lax.dot_general(a, b, dims, preferred_element_type=f32)


def head_lanes(value, head):
    lane = lax.broadcasted_iota(jnp.int32, value.shape, 1)
    keep = lane < HEAD_DIM if head == 0 else lane >= HEAD_DIM
    return jnp.where(keep, value, jnp.zeros_like(value))


def key_ranges(causal):
    return ((0, 256), (0, 512)) if causal else ((0, 512), (0, 512))


def pair_lanes(pair):
    return pl.ds(pl.multiple_of(pair * 128, 128), 128)


def attend_pair(q, k, v, bias, mix, probs, pair, causal):
    lanes = pair_lanes(pair)
    keys, values_t = k[:, lanes], v[:, lanes].T
    for block, (low, high) in enumerate(key_ranges(causal)):
        rows = slice(block * 256, block * 256 + 256)
        start = sum(b - a for a, b in key_ranges(causal)[:block])
        queries = q[rows, lanes] * bf16(HEAD_DIM**-0.5)
        parts = []
        for head in (0, 1):
            scores = mm(keys[low:high], head_lanes(queries, head), NT) + bias[low:high, rows]
            powers = jnp.exp(scores - jnp.max(scores, axis=0, keepdims=True))
            total = jnp.sum(powers, axis=0, keepdims=True)
            chances = (powers * (1.0 / total)).astype(bf16)
            probs[head, start : start + high - low, :] = chances
            parts.append(mm(values_t[head * 64 : head * 64 + 64, low:high], chances))
        mix[rows, lanes] = jnp.concatenate(parts, axis=0).astype(bf16).T


def attend_pair_back(q, k, v, grad_mix, probs, grad_q, grad_k, grad_v, pair, causal):
    lanes = pair_lanes(pair)
    keys, values = k[:, lanes], v[:, lanes]
    keys_t = keys.T
    sums_k, sums_v = [], []
    for block, (low, high) in enumerate(key_ranges(causal)):
        rows = slice(block * 256, block * 256 + 256)
        start = sum(b - a for a, b in key_ranges(causal)[:block])
        queries, grads = q[rows, lanes], grad_mix[rows, lanes]
        part_k, part_v, part_q = 0.0, 0.0, []
        for head in (0, 1):
            grad_head = head_lanes(grads, head)
            low_chances = probs[head, start : start + high - low, :]
            chances = low_chances.astype(f32)
            part_v = part_v + mm(low_chances, grad_head)
            moved = mm(values[low:high], grad_head, NT)
            product = chances * moved
            inner = jnp.sum(product, axis=0, keepdims=True)
            grad_scores = (product - chances * inner).astype(bf16)
            part_k = part_k + mm(grad_scores, head_lanes(queries, head))
            part_q.append(mm(keys_t[head * 64 : head * 64 + 64, low:high], grad_scores))
        grad_q[rows, lanes] = (jnp.concatenate(part_q, axis=0) * HEAD_DIM**-0.5).astype(bf16).T
        sums_k.append(part_k)
        sums_v.append(part_v)
    for sums, out, scale in ((sums_k, grad_k, HEAD_DIM**-0.5), (sums_v, grad_v, 1.0)):
        if causal:
            out[0:256, lanes] = ((sums[0] + sums[1][0:256]) * scale).astype(bf16)
            out[256:512, lanes] = (sums[1][256:512] * scale).astype(bf16)
        else:
            out[:, lanes] = ((sums[0] + sums[1]) * scale).astype(bf16)


WHOLE_ORDER = [0, 1, 2, 16, 6, 4, 5, 3, 7, 8, 9, 10, 11, 12, 13, 14, 15]
GATHER_ORDER = [2 * u + h for u in WHOLE_ORDER for h in (0, 1) if u < 16 or h == 0]
GATHER_KINDS = kinds_of("rprrprpr", GATHER_ORDER)
GATHER_OFFSETS = {"p": (0, 2, 3, 4, 6, 9, 12), "r": (0, 2, 3, 4, 6, 9, 12)}
ALPHA = 300.0**0.25
ROWS = 32
GELU_ROOT = (2.0 / 3.141592653589793) ** 0.5
Q1, K1, V1, A1, Q2, K2, V2, A2, Y1, Y2 = range(10)


def arrange(events, pieces, had=()):
    order, have, now = [], set(had), 0.0
    events, pieces = list(events), list(pieces)
    while events or pieces:
        if events and events[0][0] <= now:
            _, run, gives, needs = events[0]
            if needs <= have:
                events.pop(0)
                order.append(run)
                have.add(gives)
                continue
        ready = next((k for k, piece in enumerate(pieces) if piece[1] <= have), None)
        if ready is not None:
            name, _, length, run = pieces.pop(ready)
            order.append(run)
            have.add(name)
            now += length
        else:
            assert events and events[0][3] <= have
            now = max(now, events[0][0])
    return order


def in_chunks(body, rows=ROWS, total=512):
    def step(k, carry):
        body(pl.ds(pl.multiple_of(k * rows, rows), rows))
        return carry

    lax.fori_loop(0, total // rows, step, 0)


def segment_at(lengths, positions):
    end, seg = jnp.int32(0), jnp.zeros_like(positions)
    for k in range(4):
        end = end + lengths[0, k]
        seg = seg + jnp.where(positions >= end, 1, 0)
    return seg


def make_bias(key_len, query_len, bias, causal):
    def body(rows):
        key_at = rows.start + lax.broadcasted_iota(jnp.int32, (ROWS, 512), 0)
        query_at = lax.broadcasted_iota(jnp.int32, (ROWS, 512), 1)
        allowed = segment_at(key_len, key_at) == segment_at(query_len, query_at)
        if causal:
            allowed = allowed & (key_at <= query_at)
        bias[rows, :] = jnp.where(allowed, 0.0, -1e30)

    in_chunks(body)


def normalize(total, rows, norm, scale):
    middle = jnp.mean(total, axis=-1, keepdims=True)
    centered = total - middle
    spread = jnp.mean(centered * centered, axis=-1, keepdims=True)
    inverse = lax.rsqrt(spread + 1e-05)
    normal = centered * inverse
    norm[rows, :] = normal
    scale[rows, :] = inverse
    return normal


def forward_kernel(
    tokens_from, memory_from, sent_len, mem_len, proj_in, proj_out, ffn_in, ffn_out, small,
    output, wide, deep, tiny, saved, saved_g, saved_dg, saved_n, saved_scale, saved_p1, saved_p2,
    affine_out,
    acts, y_full, act_g, act_dg, norms, scales, bias, probs, squares, tall, work, tiny_in, affine,
    inputs, send_sem, recv_sem, local_sem, load_sem, save_sem, probs_sem, input_sem,
):
    place = Place()
    tokens, memory = inputs.at[0], inputs.at[1]

    def whole(unit):
        return wide.at[unit] if unit < 12 else deep.at[unit - 12] if unit < 16 else tiny

    def own(unit):
        if unit < 6:
            return proj_in.at[unit]
        if unit < 8:
            return proj_out.at[unit - 6]
        if unit < 12:
            return ffn_in.at[:, pl.ds((unit - 8) * 1024, 1024)]
        if unit < 16:
            return ffn_out.at[:, pl.ds((unit - 12) * 256, 256)]
        return small

    def half_of(part):
        rows = 64 if 12 <= part // 2 < 16 else 16
        return pl.ds((part % 2) * rows, rows)

    gather = Gather(
        place, send_sem, recv_sem,
        lambda part: whole(part // 2).at[:, :, :, :, half_of(part)],
        lambda part: own(part // 2).at[half_of(part)],
        GATHER_KINDS,
    )
    copies = {}
    for unit in WHOLE_ORDER:
        copies[unit] = pltpu.make_async_copy(
            own(unit), whole(unit).at[place.y, place.z, place.x, place.c], local_sem.at[unit]
        )
        copies[unit].start()
    place.greet()
    reads = [
        pltpu.make_async_copy(source, inputs.at[k], input_sem.at[k])
        for k, source in enumerate((tokens_from, memory_from))
    ]
    for copy in reads:
        copy.start()

    use_square = [0, 1, 2, 4, 5, 6, 3, 7, 8, 9, 10, 11]
    use_tall = [12, 13, 14, 15]

    def slot_of(unit):
        if unit < 12:
            return squares.at[use_square.index(unit) % squares.shape[0]]
        return tall.at[use_tall.index(unit) % tall.shape[0]]

    def load(unit):
        return pltpu.make_async_copy(
            whole(unit) if unit < 16 else tiny,
            slot_of(unit) if unit < 16 else tiny_in,
            load_sem.at[unit],
        )

    def weight(unit):
        load(unit).wait()
        ref = slot_of(unit)
        return ref[...].reshape((1024, 1024) if unit < 12 else (4096, 256))

    saves = []

    def save(src, dst, sem):
        copy = pltpu.make_async_copy(src, dst, save_sem.at[sem])
        copy.start()
        saves.append(copy)

    def project(source, unit, act):
        acts[act] = mm(source(), weight(unit)).astype(bf16)
        save(acts.at[act], saved.at[act], act)

    def affine_rows():
        load(16).wait()
        for group in range(8):
            part = tiny_in[group // 4, group % 4].astype(f32)
            affine[:, group * 128 : group * 128 + 128] = (
                part[0, 0] + part[0, 1] + part[1, 0] + part[1, 1]
            )
        save(affine, affine_out, 20)

    prob_copies = {}

    def attend(layer, pair):
        step = layer * 8 + pair
        slot = step % probs.shape[0]
        if step - probs.shape[0] in prob_copies:
            prob_copies.pop(step - probs.shape[0]).wait()
        causal = layer == 0
        part = probs.at[slot, :, 0:768] if causal else probs.at[slot]
        base = layer * 4
        attend_pair(
            acts.at[base], acts.at[base + 1], acts.at[base + 2], bias.at[layer],
            acts.at[base + 3], part, pair, causal,
        )
        copy = pltpu.make_async_copy(
            part, (saved_p1 if causal else saved_p2).at[pair], probs_sem.at[slot]
        )
        copy.start()
        prob_copies[step] = copy
        if pair == 7:
            save(acts.at[base + 3], saved.at[base + 3], base + 3)

    def mix_out(layer, unit):
        work[...] = mm(acts[layer * 4 + 3], weight(unit))

        def body(rows):
            before = tokens[rows, :].astype(f32) if layer == 0 else y_full[0, rows, :]
            normal = normalize(
                ALPHA * before + work[rows, :], rows, norms.at[layer], scales.at[layer]
            )
            after = normal * affine[layer : layer + 1, :] + affine[3 + layer : 4 + layer, :]
            y_full[layer, rows, :] = after
            acts[Y1 + layer, rows, :] = after.astype(bf16)

        in_chunks(body)
        save(acts.at[Y1 + layer], saved.at[Y1 + layer], Y1 + layer)
        save(norms.at[layer], saved_n.at[layer], 10 + layer)
        save(scales.at[layer], saved_scale.at[layer], 13 + layer)

    def hidden(part):
        work[...] = mm(acts[Y2], weight(8 + part))

        def body(rows):
            h = work[rows, :]
            square = h * h
            bend = jnp.tanh(GELU_ROOT * h * (1.0 + 0.044715 * square))
            half = 0.5 * (1.0 + bend)
            act_g[part, rows, :] = (h * half).astype(bf16)
            slope = half + 0.5 * h * (1.0 - bend * bend) * (
                GELU_ROOT * (1.0 + 3.0 * 0.044715 * square)
            )
            act_dg[part, rows, :] = slope.astype(bf16)

        in_chunks(body)
        if part == 3:
            save(act_g, saved_g, 16)
            save(act_dg, saved_dg, 17)

    def last_out(part):
        value = weight(12 + part)
        total = mm(act_g[0], value[0:1024])
        for k in range(1, 4):
            total = total + mm(act_g[k], value[k * 1024 : k * 1024 + 1024])
        work[:, part * 256 : part * 256 + 256] = total

    def last_norm():
        def body(rows):
            normal = normalize(
                ALPHA * y_full[1, rows, :] + work[rows, :], rows, norms.at[2], scales.at[2]
            )
            after = normal * affine[2:3, :] + affine[5:6, :]
            output[rows, :] = after.astype(bf16)

        in_chunks(body)
        save(norms.at[2], saved_n.at[2], 12)
        save(scales.at[2], saved_scale.at[2], 15)

    do = functools.partial
    pieces = [
        ("bias0", set(), 1.5, do(make_bias, sent_len, sent_len, bias.at[0], True)),
        ("bias1", set(), 1.5, do(make_bias, mem_len, sent_len, bias.at[1], False)),
        ("x", set(), 0.1, reads[0].wait),
        ("m", set(), 0.1, reads[1].wait),
        ("q1", {"w0", "x"}, 1.6, do(project, lambda: tokens[...], 0, Q1)),
        ("k1", {"w1", "x"}, 1.6, do(project, lambda: tokens[...], 1, K1)),
        ("v1", {"w2", "x"}, 1.6, do(project, lambda: tokens[...], 2, V1)),
        ("affine", {"w16"}, 0.3, affine_rows),
    ]
    pieces += [("A%d" % p, {"q1", "k1", "v1", "bias0"}, 2.1, do(attend, 0, p)) for p in range(8)]
    pieces += [
        ("o1", {"A7", "w6", "affine"}, 4.0, do(mix_out, 0, 6)),
        ("q2", {"w3", "o1"}, 1.6, do(project, lambda: acts[Y1], 3, Q2)),
        ("k2", {"w4", "m"}, 1.6, do(project, lambda: memory[...], 4, K2)),
        ("v2", {"w5", "m"}, 1.6, do(project, lambda: memory[...], 5, V2)),
    ]
    pieces += [("C%d" % p, {"q2", "k2", "v2", "bias1"}, 2.5, do(attend, 1, p)) for p in range(8)]
    pieces += [("o2", {"C7", "w7", "affine"}, 4.0, do(mix_out, 1, 7))]
    pieces += [("h%d" % k, {"w%d" % (8 + k), "o2"}, 4.0, do(hidden, k)) for k in range(4)]
    pieces += [
        ("f%d" % k, {"w%d" % (12 + k), "h0", "h1", "h2", "h3"}, 1.7, do(last_out, k))
        for k in range(4)
    ]
    pieces += [("n3", {"f0", "f1", "f2", "f3"}, 3.0, last_norm)]
    users = {0: "q1", 1: "k1", 2: "v1", 3: "q2", 4: "k2", 5: "v2", 6: "o1", 7: "o2"}
    users.update({8 + k: "h%d" % k for k in range(4)})
    users.update({12 + k: "f%d" % k for k in range(4)})

    def event(unit, step):
        if step == 1 and unit % 2 == 0:
            copies[unit // 2].wait()
        gather.stage(unit, step)

    events = []
    for turn, unit in enumerate(GATHER_ORDER):
        for step, offset in zip(Gather.stages, GATHER_OFFSETS[GATHER_KINDS[unit][0]]):
            key = turn + offset
            events.append((key * FWD_PACE, step, do(event, unit, step), (unit, step), set()))
    events.sort(key=lambda item: item[:2])
    events = [(time, run, gives, needs) for time, _, run, gives, needs in events]
    loads = []
    for unit in WHOLE_ORDER:
        needs = {(2 * unit, 4), (2 * unit + (unit < 16), 4)}
        if unit < 16:
            uses, ring = (use_square, squares) if unit < 12 else (use_tall, tall)
            before = uses.index(unit) - ring.shape[0]
            if before >= 0:
                needs.add(users[uses[before]])
        loads.append(("w%d" % unit, needs, 0.0, do(lambda unit: load(unit).start(), unit)))
    for run in arrange(events, loads + pieces):
        run()
    for unit in GATHER_ORDER:
        gather.finish(unit)
    for copy in saves + list(prob_copies.values()):
        copy.wait()


FWD_PACE = 3.0


def forward_call(tokens, memory, sent_len, mem_len, proj_in, proj_out, ffn_in, ffn_out, small):
    hbm = pl.BlockSpec(memory_space=pl.ANY)
    vmem = pl.BlockSpec(memory_space=pltpu.VMEM)
    smem = pl.BlockSpec(memory_space=pltpu.SMEM)
    shape = jax.ShapeDtypeStruct
    return pl.pallas_call(
        forward_kernel,
        out_shape=(
            shape((512, 1024), bf16),
            shape((12, 2, 4, 2, 2, 32, 1024), bf16),
            shape((4, 2, 4, 2, 2, 128, 256), bf16),
            shape((2, 4, 2, 2, 16, 128), bf16),
            shape((10, 512, 1024), bf16),
            shape((4, 512, 1024), bf16),
            shape((4, 512, 1024), bf16),
            shape((3, 512, 1024), f32),
            shape((3, 512, 1), f32),
            shape((8, 2, 768, 256), bf16),
            shape((8, 2, 1024, 256), bf16),
            shape((16, 1024), f32),
        ),
        in_specs=[hbm, hbm, smem, smem, vmem, vmem, vmem, vmem, vmem],
        out_specs=[vmem] + [hbm] * 11,
        scratch_shapes=[
            pltpu.VMEM((10, 512, 1024), bf16),
            pltpu.VMEM((2, 512, 1024), f32),
            pltpu.VMEM((4, 512, 1024), bf16),
            pltpu.VMEM((4, 512, 1024), bf16),
            pltpu.VMEM((3, 512, 1024), f32),
            pltpu.VMEM((3, 512, 1), f32),
            pltpu.VMEM((2, 512, 512), f32),
            pltpu.VMEM((2, 2, 1024, 256), bf16),
            pltpu.VMEM((3, 2, 4, 2, 2, 32, 1024), bf16),
            pltpu.VMEM((2, 2, 4, 2, 2, 128, 256), bf16),
            pltpu.VMEM((512, 1024), f32),
            pltpu.VMEM((2, 4, 2, 2, 16, 128), bf16),
            pltpu.VMEM((16, 1024), f32),
            pltpu.VMEM((2, 512, 1024), bf16),
            pltpu.SemaphoreType.DMA((2 * UNITS, 9)),
            pltpu.SemaphoreType.DMA((2 * UNITS, 9)),
            pltpu.SemaphoreType.DMA((UNITS,)),
            pltpu.SemaphoreType.DMA((UNITS,)),
            pltpu.SemaphoreType.DMA((21,)),
            pltpu.SemaphoreType.DMA((2,)),
            pltpu.SemaphoreType.DMA((2,)),
        ],
        compiler_params=pltpu.CompilerParams(
            collective_id=0, has_side_effects=True, vmem_limit_bytes=63 << 20
        ),
        cost_estimate=pl.CostEstimate(
            flops=20_000_000_000, bytes_accessed=120_000_000, transcendentals=10_000_000
        ),
    )(tokens, memory, sent_len, mem_len, proj_in, proj_out, ffn_in, ffn_out, small)


def small_rows(ln_gain, ln_bias):
    rows = jnp.concatenate([ln_gain, ln_bias, jnp.zeros((10, 32), bf16)], axis=0)
    spot = lax.axis_index("fsdp") % 4
    return jnp.concatenate(
        [jnp.where(spot == k, rows, jnp.zeros_like(rows)) for k in range(4)], axis=1
    )


GRAD_ORDER = [12, 13, 14, 15, 8, 9, 10, 11, 7, 3, 4, 5, 6, 16, 0, 1, 2]
SCATTER_ORDER = [2 * u + h for u in GRAD_ORDER for h in (0, 1) if u < 16 or h == 0]
SCATTER_KINDS = kinds_of("rprrprpr", SCATTER_ORDER)
SCATTER_WAIT = 16.0
SCATTER_PACE = 3.6
DEPTH_OTHER, DEPTH_MINE, DEPTH_TWIN, DEPTH_REST = 4, 9, 5, 8


def arrange_back(units, stages, pieces, wait, pace, costs):
    order, have, now = [], set(), 0.0
    pieces = list(pieces)
    at = {unit: 0 for unit in units}
    ready = {unit: 0.0 for unit in units}
    last = {}
    while pieces or any(k < len(stages) for k in at.values()):
        options = []
        for place, unit in enumerate(units):
            if at[unit] == len(stages):
                continue
            stage, needs, run = stages[at[unit]](unit)
            if needs <= have:
                time = max(ready[unit], last.get(stage, -pace) + pace if stage in (0, 1, 2, 3) else 0.0)
                options.append((time, place, unit, stage, run))
        best = min(options, key=lambda item: item[:2]) if options else None
        piece = next((k for k, item in enumerate(pieces) if item[1] <= have), None)
        if best is not None and (best[0] <= now or piece is None):
            time, _, unit, stage, run = best
            now = max(now, time)
            order.append(run)
            have.add((unit, stage))
            last[stage] = now
            now += costs.get(stage, 0.0)
            ready[unit] = now + wait.get(stage, 0.0)
            at[unit] += 1
        else:
            assert piece is not None
            name, _, length, run = pieces.pop(piece)
            order.append(run)
            have.add(name)
            now += length
    return order


def backward_kernel(
    cotangent, wide, deep, affine, saved, saved_g, saved_dg, saved_n, saved_scale,
    saved_p1, saved_p2, tokens, memory,
    grad_tokens, grad_memory, out_in, out_out, out_fin, out_fout, out_tiny,
    pool, total, work, norm, scales, probs, squares, affine_grads,
    other, mine, twin, eight, four, zs,
    other_s, mine_s, twin_s, eight_s, four_s, zs_s,
    send_sem, recv_sem, credit, load_sem, act_sem, probs_sem,
):
    place = Place()
    turn = {unit: k for k, unit in enumerate([u for u in GRAD_ORDER if u != 16])}

    def slot_of(ref, tiny, unit):
        return tiny if unit == 16 else ref.at[turn[unit] % ref.shape[0]]

    def ring(ref, tiny, lead):
        def pick(part):
            slot = slot_of(ref, tiny, part // 2)
            if part // 2 == 16:
                return slot
            rows = pl.ds((part % 2) * 16, 16)
            return slot.at[:, :, :, rows] if lead == 3 else slot.at[:, :, rows] if lead == 2 else slot.at[:, rows]

        return pick

    def out(part):
        unit, rows = part // 2, pl.ds((part % 2) * 16, 16)
        if unit < 6:
            return out_in.at[unit, rows]
        if unit < 8:
            return out_out.at[unit - 6, rows]
        if unit < 12:
            return out_fin.at[rows, pl.ds((unit - 8) * 1024, 1024)]
        return out_tiny

    scatter = RingScatter(
        place, send_sem, recv_sem, ring(other, other_s, 3), ring(mine, mine_s, 3),
        ring(twin, twin_s, 3), ring(eight, eight_s, 2), ring(four, four_s, 1), ring(zs, zs_s, 2),
        out, SCATTER_KINDS, credit,
        {part: k for k, part in enumerate([p for p in SCATTER_ORDER if p != 32])},
    )
    scatter.tall = lambda unit, value: tall_out(unit, value)

    def tall_out(part, value):
        column, first = (part // 2 - 12) * 256, (part % 2) * 16
        for k in range(4):
            out_fout[k * 32 + first : k * 32 + first + 16, column : column + 256] = value[
                :, k * 256 : k * 256 + 256
            ]

    uses = [("t", 0), 8, ("t", 1), 9, ("t", 2), 10, ("t", 3), 11, 7, 3, 4, 5, 6, 0, 1, 2]

    def weight_copies(name):
        k = uses.index(name)
        slot = squares.at[k % squares.shape[0]]
        if isinstance(name, int):
            return [pltpu.make_async_copy(wide.at[name], slot, load_sem.at[k, 0])]
        rows = pl.ds(name[1] * 1024, 1024)
        return [
            pltpu.make_async_copy(
                deep.at[u, rows], slot.at[:, pl.ds(u * 256, 256)], load_sem.at[k, u]
            )
            for u in range(4)
        ]

    def load_weight(name):
        for copy in weight_copies(name):
            copy.start()

    def weight(name):
        for copy in weight_copies(name):
            copy.wait()
        return squares[uses.index(name) % squares.shape[0]]

    sources = {
        "n3": (saved_n.at[2], norm), "n2": (saved_n.at[1], norm), "n1": (saved_n.at[0], norm),
        "s": (saved_scale, scales),
        "y2": (saved.at[Y2], pool.at[7]), "y1": (saved.at[Y1], pool.at[9]),
        "m": (memory, pool.at[10]), "t": (tokens, pool.at[11]), "c": (cotangent, pool.at[6]),
        "a2": (saved.at[A2], pool.at[0]), "q2": (saved.at[Q2], pool.at[1]),
        "k2": (saved.at[K2], pool.at[2]), "v2": (saved.at[V2], pool.at[3]),
        "a1": (saved.at[A1], pool.at[0]), "q1": (saved.at[Q1], pool.at[1]),
        "k1": (saved.at[K1], pool.at[2]), "v1": (saved.at[V1], pool.at[3]),
    }
    for j in range(4):
        sources["g%d" % j] = (saved_g.at[j], pool.at[j])
        sources["dg%d" % j] = (saved_dg.at[j], pool.at[4 + j % 2])
    names = list(sources)

    def act_copy(name):
        src, dst = sources[name]
        return pltpu.make_async_copy(src, dst, act_sem.at[names.index(name)])

    arrived = set()

    def act(name):
        if name not in arrived:
            arrived.add(name)
            act_copy(name).wait()
        return sources[name][1]

    DO, DQ, DK, DV, EB = 4, 5, 6, 7, 8

    def norm_back(layer):
        grads = act("c") if layer == 2 else total
        norms = act("n%d" % (layer + 1))
        act("s")
        affine_grads[layer : layer + 1, :] = jnp.zeros((1, 1024), f32)
        affine_grads[3 + layer : 4 + layer, :] = jnp.zeros((1, 1024), f32)

        def body(rows):
            e, n = grads[rows, :].astype(f32), norms[rows, :]
            affine_grads[layer : layer + 1, :] += jnp.sum(e * n, axis=0, keepdims=True)
            affine_grads[3 + layer : 4 + layer, :] += jnp.sum(e, axis=0, keepdims=True)
            scaled = e * affine[layer : layer + 1, :]
            back = scaled - jnp.mean(scaled, axis=-1, keepdims=True)
            back = back - n * jnp.mean(scaled * n, axis=-1, keepdims=True)
            back = back * scales[layer, rows, :]
            pool[EB, rows, :] = back.astype(bf16)
            total[rows, :] = ALPHA * back

        in_chunks(body)

    def fill(unit, value):
        parts = value.astype(bf16).reshape(2, 4, 2, 2, 32, 1024)
        first = place.c == 0
        even, odd = parts[:, :, :, 0], parts[:, :, :, 1]
        slot_of(mine, mine_s, unit)[...] = jnp.where(first, even, odd)
        slot_of(other, other_s, unit)[...] = jnp.where(first, odd, even)

    def grad_tall(j, first_unit, last_unit):
        columns = slice(first_unit * 256, last_unit * 256)
        value = mm(act("g%d" % j)[...], pool[EB, :, columns], TN).astype(bf16)
        value = value.reshape(2, 2, 2, 4, 32, columns.stop - columns.start)
        first = place.c == 0
        even, odd = value[:, :, 0], value[:, :, 1]
        for ref, part in (
            (mine, jnp.where(first, even, odd)),
            (other, jnp.where(first, odd, even)),
        ):
            for u in range(first_unit, last_unit):
                at = (u - first_unit) * 256
                for k in range(4):
                    ref[u, j // 2, 2 * (j % 2) : 2 * (j % 2) + 2, :, :, k * 256 : k * 256 + 256] = (
                        part[:, :, k, :, at : at + 256]
                    )

    def hidden_back(j):
        work[...] = mm(pool[EB], weight(("t", j)), NT)
        slope = act("dg%d" % j)

        def body(rows):
            pool[DK, rows, :] = (work[rows, :] * slope[rows, :].astype(f32)).astype(bf16)

        in_chunks(body)

    def accumulate(source, name):
        total[...] = total[...] + mm(pool[source], weight(name), NT)

    def mix_back(name):
        pool[DO] = mm(pool[EB], weight(name), NT).astype(bf16)

    def grad_matrix(unit, left, right):
        fill(unit, mm(left(), pool[right], TN))

    def grad_affine():
        value = affine_grads[...].astype(bf16)
        for group in range(8):
            for x in (0, 1):
                block = value[:, group * 128 : group * 128 + 128]
                mine_s[group // 4, group % 4, x] = block
                other_s[group // 4, group % 4, x] = block

    def probs_copy(layer, pair):
        slot = probs.at[pair % 2] if layer == 1 else probs.at[pair % 2, :, 0:768]
        src = (saved_p1 if layer == 0 else saved_p2).at[pair]
        return pltpu.make_async_copy(src, slot, probs_sem.at[layer, pair])

    def attend_back(layer, pair):
        causal = layer == 0
        for name in ("q%d", "k%d", "v%d"):
            act(name % (layer + 1))
        probs_copy(layer, pair).wait()
        attend_pair_back(
            pool.at[1], pool.at[2], pool.at[3], pool.at[DO], probs.at[pair % 2],
            pool.at[DQ], pool.at[DK], pool.at[DV], pair, causal,
        )

    def memory_back(first):
        if first:
            work[...] = mm(pool[DK], weight(4), NT)
        else:
            grad_memory[...] = (work[...] + mm(pool[DV], weight(5), NT)).astype(bf16)

    def tokens_back():
        grad_tokens[...] = (total[...] + mm(pool[DV], weight(2), NT)).astype(bf16)

    do = functools.partial
    start = lambda name: act_copy(name).start()
    order_of = [u for u in GRAD_ORDER if u != 16]

    def free(unit):
        k, needs = turn[unit], set()
        for ring_ref, step in ((mine, 5), (other, 1)):
            if k >= ring_ref.shape[0]:
                before = order_of[k - ring_ref.shape[0]]
                needs |= {(2 * before, step), (2 * before + 1, step)}
        return needs

    pieces = []

    def piece(name, needs, length, run):
        pieces.append((name, set(needs), length, run))

    def loads(name, needs=()):
        piece("L" + name, needs, 0.0, do(start, name))

    user = {("t", j): "dh%d" % j for j in range(4)}
    user.update({8 + j: "r%d" % j for j in range(4)})
    user.update({7: "o2", 3: "rq", 4: "m4", 5: "m5", 6: "o1", 0: "t0", 1: "t1", 2: "t2"})
    for name in ("n3", "s", "c", "g0", "g1", "g2", "g3", "dg0", "dg1", "y2", "m", "y1", "t"):
        loads(name)
    for k, name in enumerate(uses):
        needs = [user[uses[k - squares.shape[0]]]] if k >= squares.shape[0] else []
        piece(("W", name), needs, 0.0, do(load_weight, name))
    loads("dg2", ["dh0"])
    loads("dg3", ["dh1"])
    loads("n2", ["z3"])
    loads("n1", ["z2"])
    for k, name in enumerate(("a2", "q2", "k2", "v2")):
        loads(name, ["Gt%d" % k])
    loads("a1", ["G7"])
    for name in ("q1", "k1", "v1"):
        loads(name, ["B2_7"])
    for layer in (1, 0):
        for pair in range(8):
            if pair >= 2:
                needs = ["B%d_%d" % (layer + 1, pair - 2)]
            else:
                needs = [] if layer == 1 else ["B2_%d" % (6 + pair)]
            piece("P%d_%d" % (layer + 1, pair), needs, 0.0, lambda l=layer, p=pair: probs_copy(l, p).start())

    piece("z3", ["Ln3", "Ls", "Lc"], 2.5, do(norm_back, 2))
    for j in range(4):
        piece("Gf%d" % j, ["z3", "Lg%d" % j], 0.9, do(grad_tall, j, 0, 1))
    for j in range(4):
        piece("Gt%d" % j, ["z3", "Gf%d" % j], 1.6, do(grad_tall, j, 1, 4))
    for j in range(4):
        piece("G%d" % (8 + j), ["r%d" % j, "Ly2"] + list(free(8 + j)), 2.0, do(grad_matrix, 8 + j, lambda: act("y2")[...], DK))
    piece("G7", ["z2", "La2"] + list(free(7)), 2.0, do(grad_matrix, 7, lambda: act("a2")[...], EB))
    piece("G3", ["B2_7", "Ly1"] + list(free(3)), 2.0, do(grad_matrix, 3, lambda: act("y1")[...], DQ))
    piece("G4", ["B2_7", "Lm", "G3"] + list(free(4)), 2.0, do(grad_matrix, 4, lambda: act("m")[...], DK))
    piece("G5", ["B2_7", "Lm", "G4"] + list(free(5)), 2.0, do(grad_matrix, 5, lambda: act("m")[...], DV))
    piece("G6", ["z1", "La1"] + list(free(6)), 2.0, do(grad_matrix, 6, lambda: act("a1")[...], EB))
    piece("G16", ["z1"], 0.3, grad_affine)
    for k, unit in enumerate((0, 1, 2)):
        piece("G%d" % unit, ["B1_7", "Lt"] + list(free(unit)), 2.0, do(grad_matrix, unit, lambda: act("t")[...], DQ + k))
    for j in range(4):
        needs = ["z3", "Ldg%d" % j, ("W", ("t", j))] + (["G%d" % (7 + j)] if j else [])
        piece("dh%d" % j, needs, 2.2, do(hidden_back, j))
        piece("r%d" % j, ["dh%d" % j, ("W", 8 + j)], 1.8, do(accumulate, DK, 8 + j))
    piece("z2", ["r3", "Gt0", "Gt1", "Gt2", "Gt3", "dh3", "Ln2"], 2.5, do(norm_back, 1))
    piece("o2", ["z2", ("W", 7), "dh2", "dh3"], 1.6, do(mix_back, 7))
    for pair in range(8):
        piece("B2_%d" % pair, ["B2_%d" % (pair - 1) if pair else "o2", "G11", "P2_%d" % pair, "Lq2", "Lk2", "Lv2"], 2.3, do(attend_back, 1, pair))
    piece("rq", ["B2_7", ("W", 3)], 1.8, do(accumulate, DQ, 3))
    piece("z1", ["rq", "G7", "Ln1"], 2.5, do(norm_back, 0))
    piece("m4", ["B2_7", ("W", 4)], 1.6, do(memory_back, True))
    piece("m5", ["m4", ("W", 5)], 1.8, do(memory_back, False))
    piece("o1", ["z1", "B2_7", ("W", 6)], 1.6, do(mix_back, 6))
    for pair in range(8):
        piece("B1_%d" % pair, ["B1_%d" % (pair - 1) if pair else "o1", "m5", "G3", "G4", "G5", "P1_%d" % pair, "Lq1", "Lk1", "Lv1"], 1.8, do(attend_back, 0, pair))
    piece("t0", ["B1_7", ("W", 0)], 1.8, do(accumulate, DQ, 0))
    piece("t1", ["B1_7", "t0", ("W", 1)], 1.8, do(accumulate, DK, 1))
    piece("t2", ["t1", ("W", 2)], 1.8, tokens_back)

    def stage(step):
        def at(part):
            unit, needs = part // 2, set()
            if step == 0:
                needs = {"G%d" % unit}
                if 12 <= unit < 16:
                    needs = {("Gf%d" if unit == 12 else "Gt%d") % j for j in range(4)}
            return step, needs | scatter.needs(part, step), do(scatter.stage, part, step)

        return at

    place.greet()
    waits = {step: SCATTER_WAIT for step in (0, 1, 2, 3)}
    waits.update({2.5: 3.0, 3.5: 3.0, 4: 1.0})
    costs = {1: 0.5, 2: 0.3, 3: 0.3, 4: 0.2}
    for run in arrange_back(
        SCATTER_ORDER, [stage(step) for step in Scatter.stages], pieces, waits, SCATTER_PACE, costs
    ):
        run()


class RingScatter(Scatter):
    def __init__(self, place, send_sem, recv_sem, other, mine, twin, eight, four, zs, out, kinds, credit, turn):
        super().__init__(place, send_sem, recv_sem, other, mine, twin, eight, four, zs, out, kinds)
        self.credit, self.turn = credit, turn
        self.count = len(turn)

    def needs(self, unit, step):
        if unit == 32 or step not in (0, 1, 4):
            return set()
        k, needs = self.turn[unit], set()
        part_at = {turn: part for part, turn in self.turn.items()}
        if k >= 1:
            needs.add((part_at[k - 1], step))
        if step == 0 and k >= 2 * DEPTH_TWIN:
            needs.add((part_at[k - 2 * DEPTH_TWIN], 1))
        if step == 1 and k >= 2 * DEPTH_REST:
            needs.add((part_at[k - 2 * DEPTH_REST], 4))
        return needs

    def give(self, slot, device):
        pl.semaphore_signal(self.credit.at[slot], inc=1, device_id=device, device_id_type=MESH)

    def stage(self, unit, step):
        p = self.p
        k = None if unit == 32 else self.turn[unit]
        if k is not None and step == 0 and k >= 2 * DEPTH_TWIN:
            pl.semaphore_wait(self.credit.at[0], 1)
        if k is not None and step == 1 and k >= 2 * DEPTH_REST:
            for slot in (1, 2):
                pl.semaphore_wait(self.credit.at[slot], 1)
            for far in (1, 2, 3):
                pl.semaphore_wait(self.credit.at[4 + lax.rem(p.z + far, 4)], 1)
        if step == 4 and 24 <= unit < 32:
            hold = self.out
            self.out = lambda u: TallOut(self.tall, u)
            super().stage(unit, step)
            self.out = hold
        else:
            super().stage(unit, step)
        if k is not None and step == 1 and k + 2 * DEPTH_TWIN < self.count:
            self.give(0, p.sibling())
        if k is not None and step == 4 and k + 2 * DEPTH_REST < self.count:
            self.give(1, p.over_x())
            self.give(2, p.over_y())
            for far in (1, 2, 3):
                self.give(4 + p.z, p.at(z=lax.rem(p.z + far, 4)))


class TallOut:
    def __init__(self, store, unit):
        self.store, self.unit = store, unit

    def __setitem__(self, _, value):
        self.store(self.unit, value)


def backward_call(cotangent, saved_all, tokens, memory):
    wide, deep, saved, saved_g, saved_dg, saved_n, saved_scale, saved_p1, saved_p2, affine = saved_all
    hbm = pl.BlockSpec(memory_space=pl.ANY)
    vmem = pl.BlockSpec(memory_space=pltpu.VMEM)
    shape = jax.ShapeDtypeStruct
    block = (32, 1024)
    tiny = (16, 128)
    return pl.pallas_call(
        backward_kernel,
        out_shape=(
            shape((512, 1024), bf16),
            shape((512, 1024), bf16),
            shape((6, 32, 1024), f32),
            shape((2, 32, 1024), f32),
            shape((32, 4096), f32),
            shape((128, 1024), f32),
            shape((16, 128), f32),
        ),
        in_specs=[hbm, hbm, hbm, vmem] + [hbm] * 9,
        out_specs=[vmem] * 7,
        scratch_shapes=[
            pltpu.VMEM((12, 512, 1024), bf16),
            pltpu.VMEM((512, 1024), f32),
            pltpu.VMEM((512, 1024), f32),
            pltpu.VMEM((512, 1024), f32),
            pltpu.VMEM((3, 512, 1), f32),
            pltpu.VMEM((2, 2, 1024, 256), bf16),
            pltpu.VMEM((2, 1024, 1024), bf16),
            pltpu.VMEM((16, 1024), f32),
            pltpu.VMEM((DEPTH_OTHER, 2, 4, 2, *block), bf16),
            pltpu.VMEM((DEPTH_MINE, 2, 4, 2, *block), bf16),
            pltpu.VMEM((DEPTH_TWIN, 2, 4, 2, *block), bf16),
            pltpu.VMEM((DEPTH_REST, 2, 4, *block), bf16),
            pltpu.VMEM((DEPTH_REST, 4, *block), bf16),
            pltpu.VMEM((DEPTH_REST, 4, 2, *block), bf16),
            pltpu.VMEM((2, 4, 2, *tiny), bf16),
            pltpu.VMEM((2, 4, 2, *tiny), bf16),
            pltpu.VMEM((2, 4, 2, *tiny), bf16),
            pltpu.VMEM((2, 4, *tiny), bf16),
            pltpu.VMEM((4, *tiny), bf16),
            pltpu.VMEM((4, 2, *tiny), bf16),
            pltpu.SemaphoreType.DMA((2 * UNITS, 9)),
            pltpu.SemaphoreType.DMA((2 * UNITS, 9)),
            pltpu.SemaphoreType.REGULAR((8,)),
            pltpu.SemaphoreType.DMA((16, 4)),
            pltpu.SemaphoreType.DMA((32,)),
            pltpu.SemaphoreType.DMA((2, 8)),
        ],
        compiler_params=pltpu.CompilerParams(
            collective_id=1, has_side_effects=True, vmem_limit_bytes=63 << 20
        ),
        cost_estimate=pl.CostEstimate(
            flops=40_000_000_000, bytes_accessed=120_000_000, transcendentals=0
        ),
    )(
        cotangent, wide.reshape(12, 1024, 1024), deep.reshape(4, 4096, 256),
        affine, saved, saved_g, saved_dg, saved_n, saved_scale, saved_p1, saved_p2, tokens, memory,
    )


def hand_over_kernel(*refs):
    count = (len(refs) - 1) // 3
    given, taken, held, sem = refs[:count], refs[count : 2 * count], refs[2 * count : -1], refs[-1]
    reads = [pltpu.make_async_copy(given[k], held[k], sem.at[0, k]) for k in range(count)]
    writes = [pltpu.make_async_copy(held[k], taken[k], sem.at[1, k]) for k in range(count)]
    for copy in reads:
        copy.start()
    for read, write in zip(reads, writes):
        read.wait()
        write.start()
    for copy in writes:
        copy.wait()


def hand_over(*results):
    count = len(results)
    return pl.pallas_call(
        hand_over_kernel,
        out_shape=[jax.ShapeDtypeStruct(r.shape, r.dtype) for r in results],
        in_specs=[pl.BlockSpec(memory_space=pl.ANY)] * count,
        out_specs=[pl.BlockSpec(memory_space=pl.ANY)] * count,
        scratch_shapes=[pltpu.VMEM(r.shape, r.dtype) for r in results]
        + [pltpu.SemaphoreType.DMA((2, count))],
        compiler_params=pltpu.CompilerParams(vmem_limit_bytes=60 << 20),
    )(*results)


def on_device(
    tokens, memory, cotangent, sent_len, mem_len, proj_in, proj_out, ffn_in, ffn_out, ln_gain, ln_bias
):
    small = small_rows(ln_gain, ln_bias)
    output, wide, deep, _, saved, g, dg, n, scale, p1, p2, affine = forward_call(
        tokens, memory, sent_len, mem_len, proj_in, proj_out, ffn_in, ffn_out, small
    )
    *results, g_small = backward_call(
        cotangent, (wide, deep, saved, g, dg, n, scale, p1, p2, affine), tokens, memory
    )
    spot = lax.axis_index("fsdp") % 4
    own = lax.dynamic_slice(g_small, (0, spot * 32), (16, 32))
    return (*hand_over(output, *results), own[0:3], own[3:6])


def on_any_mesh(
    tokens, memory, cotangent, sent_len, mem_len, proj_in, proj_out, ffn_in, ffn_out, ln_gain, ln_bias
):
    dims = (1, 1, 0, 0, 1, 1)
    shards = (proj_in, proj_out, ffn_in, ffn_out, ln_gain, ln_bias)
    weights = tuple(
        lax.all_gather(shard, BOTH, axis=dim, tiled=True) for shard, dim in zip(shards, dims)
    )
    sent_seg = segment_ids(sent_len[0], tokens.shape[0])
    mem_seg = segment_ids(mem_len[0], memory.shape[0])
    saved = run_forward(tokens, memory, sent_seg, mem_seg, weights)
    output = saved["o"].astype(bf16)
    grads = run_backward(saved, tokens, memory, sent_seg, mem_seg, weights, cotangent)
    summed = tuple(
        lax.psum_scatter(grad, BOTH, scatter_dimension=dim, tiled=True)
        for grad, dim in zip(grads[2:], dims)
    )
    return (output, *grads[:2], *summed)


def solution(mesh):
    placed = (
        P(BOTH, None),
        P(BOTH, None),
        P(BOTH, None),
        P(BOTH, None),
        P(BOTH, None),
        P(None, BOTH, None),
        P(None, BOTH, None),
        P(BOTH, None),
        P(BOTH, None),
        P(None, BOTH),
        P(None, BOTH),
    )
    routed = mesh.shape["dp"] == 2 and mesh.shape["fsdp"] == 16
    return jax.shard_map(
        on_device if routed else on_any_mesh,
        mesh=mesh,
        in_specs=placed,
        out_specs=(
            P(BOTH, None),
            P(BOTH, None),
            P(BOTH, None),
            P(None, BOTH, None),
            P(None, BOTH, None),
            P(BOTH, None),
            P(BOTH, None),
            P(None, BOTH),
            P(None, BOTH),
        ),
        check_vma=False,
    )
```
